32 devices in a mesh: dp: 4 (over y, x), expert: 8 (over z, core).
Axes of the slice: x: 2, y: 2, z: 4, core: 2. Of those that a mesh axis runs over, the one named last changes fastest.
Arguments:
- tokens: bfloat16 [32, 1024, 768], P(('dp', 'expert')), may hold values from -6 to 6
- cotangent: bfloat16 [32, 1024, 768], P(('dp', 'expert')), may hold values from -6 to 6
- lengths: int32 [32], P(('dp', 'expert')), may hold values from 512 to 1024
- routes: int32 [32, 1024], P(('dp', 'expert')), may hold values from 0 to 7
- norm_gain: bfloat16 [768], replicated, may hold values from 0.5 to 1.5
- query_weight: bfloat16 [768, 768], replicated, may hold values from -0.21875 to 0.21875
- key_weight: bfloat16 [768, 768], replicated, may hold values from -0.21875 to 0.21875
- value_weight: bfloat16 [768, 768], replicated, may hold values from -0.21875 to 0.21875
- output_weight: bfloat16 [768, 768], replicated, may hold values from -2.5 to 2.5
- bucket_head_bias: bfloat16 [32, 12], replicated, may hold values from -4 to 4
- ffn_gain: bfloat16 [768], replicated, may hold values from 0.5 to 1.5
- router_weight: bfloat16 [768, 8], replicated, may hold values from -0.15625 to 0.15625
- expert_in: bfloat16 [8, 768, 3072], P('expert'), may hold values from -0.21875 to 0.21875
- expert_out: bfloat16 [8, 3072, 768], P('expert'), as said below
Outputs:
- result: bfloat16 [32, 1024, 768], P(('dp', 'expert'))
- token_grad: float32 [32, 1024, 768], P(('dp', 'expert'))
- norm_gain_grad: float32 [768], replicated
- query_grad: float32 [768, 768], replicated
- key_grad: float32 [768, 768], replicated
- value_grad: float32 [768, 768], replicated
- output_grad: float32 [768, 768], replicated
- bucket_grad: float32 [32, 12], replicated
- ffn_gain_grad: float32 [768], replicated
- router_grad: float32 [768, 8], replicated
- expert_in_grad: float32 [8, 768, 3072], P('expert', None, 'dp')
- expert_output_gradient: float32 [8, 3072, 768], P('expert', 'dp')
The draws below stay inside these ranges and needn't reach their ends.
Inputs may be any that keep to these rules, and one draw needn't show every extreme that they name: Every entry of expert_out lies within 6 * 8 / sqrt(3072) of zero.
All inputs are finite; a program needn't handle non-finite values.
Results may differ from the reference program's by a relative error of at most 0.015.
Values may be sent and summed in bfloat16 or wider, within the bound.
No kernel may reach another device: no remote copies, remote signals or barrier semaphores. Data moves between devices by JAX's collectives and lax.ppermute only.
A program may use at most 320 MiB of HBM per device.

```python
import math
import jax
import jax.numpy as jnp
import numpy as np
from jax import lax

D = 768
HEADS = 12
HDIM = 64
FF = 3072
NB = 32
MAXDIST = 128
LEN = 1024
SEQ_DEV = 1
EXPERTS = 8
CAP = 160
SEQS = 32
N_DP = 4
N_EXPERT = 8


def draw_expert_out(key, part):
    key = jax.random.fold_in(key, 7)
    spread = EXPERTS * 1.5 / math.sqrt(FF)
    values = jnp.clip(jax.random.normal(key, (EXPERTS, FF, D), jnp.float32), -4.0, 4.0) * spread
    return values.astype(jnp.bfloat16)


def touch_ends(values, rng, least, high):
    longest = values.shape.index(max(values.shape))
    spots = []
    for shift in (0, 1):
        where = [jax.random.randint(jax.random.fold_in(rng, axis), (), 0, length) for axis, length in enumerate(values.shape)]
        where[longest] = (where[longest] + shift) % values.shape[longest]
        spots.append(tuple(where))
    return values.at[spots[0]].set(least).at[spots[1]].set(high)


def block_scale(own_key, shape, split, smallest, high):
    level = 1.0
    for dim, parts in split:
        steps = jax.random.uniform(jax.random.fold_in(jax.random.fold_in(own_key, 6), dim), (parts,), jnp.float32, smallest / len(split), high / len(split))
        level = level * jnp.repeat(jnp.exp(steps), shape[dim] // parts).reshape((-1,) + (1,) * (len(shape) - 1 - dim))
    return level


def rank_bounds(amount, skew):
    weights = [(1 << 20) // math.isqrt(grade ** skew) + 1 for grade in range(1, amount + 1)]
    deviation = 1 + sum(weights) // (1 << 30)
    return np.cumsum(np.array([max(1, weight // deviation) for weight in weights]))


def ranked(stream_key, extent, amount, slope):
    grid = rank_bounds(amount, slope)
    pick = jax.random.randint(jax.random.fold_in(stream_key, 1), extent, 0, int(grid[amount - 1]))
    standing = jnp.searchsorted(jnp.asarray(grid, jnp.int32), pick, side="right")
    return jax.random.permutation(jax.random.fold_in(stream_key, 2), amount)[standing].astype(jnp.int32)


def bell_draw(key, dims, width, limit, pieces=(), kind=jnp.bfloat16):
    loudness = block_scale(key, dims, pieces, -0.22, 0.18) if pieces else 1.0
    entries = jax.random.normal(key, dims, jnp.float32) * width * loudness
    return jnp.minimum(jnp.maximum(entries, -limit), limit).astype(kind)


def setup_inputs(seed: int = 0) -> dict:
    key_list = jax.random.split(jax.random.key(seed), 15)
    return {
        "tokens": bell_draw(key_list[0], (SEQS, LEN, D), 1.0, 6.0, ((0, 32),)),
        "cotangent": bell_draw(key_list[1], (SEQS, LEN, D), 1.0, 6.0, ((0, 32),)),
        "lengths": touch_ends(jax.random.randint(key_list[2], (SEQS,), LEN // 2, LEN + 1), jax.random.fold_in(key_list[2], 1), LEN // 2, LEN).astype(jnp.int32),
        "routes": touch_ends(ranked(key_list[3], (SEQS, LEN), EXPERTS, 1), jax.random.fold_in(key_list[3], 3), 0, EXPERTS - 1).astype(jnp.int32),
        "norm_gain": jnp.clip(1.0 + 0.1 * jax.random.normal(key_list[4], (D,), jnp.float32), 0.5, 1.5).astype(jnp.bfloat16),
        "query_weight": bell_draw(key_list[5], (D, D), D ** -0.5, 0.21875),
        "key_weight": bell_draw(key_list[6], (D, D), D ** -0.5, 0.21875),
        "value_weight": bell_draw(key_list[7], (D, D), D ** -0.5, 0.21875),
        "output_weight": bell_draw(key_list[8], (D, D), (max(1, D // 128)) ** -0.5, 2.5),
        "bucket_head_bias": bell_draw(key_list[9], (NB, HEADS), 1.0, 4.0),
        "ffn_gain": jnp.clip(1.0 + 0.1 * jax.random.normal(key_list[10], (D,), jnp.float32), 0.5, 1.5).astype(jnp.bfloat16),
        "router_weight": bell_draw(key_list[11], (D, EXPERTS), (2 * D) ** -0.5, 0.15625),
        "expert_in": bell_draw(key_list[12], (EXPERTS, D, FF), D ** -0.5, 0.21875, ((0, 8),)),
        "expert_out": draw_expert_out(jax.random.fold_in(key_list[14], 71), 0),
    }


EPSILON = 1e-06
NEGATIVE = -1000000000.0
HIGHEST = lax.Precision.HIGHEST

@jax.custom_vjp
def low(v):
    return lax.optimization_barrier(v.astype(jnp.bfloat16)).astype(jnp.float32)

@jax.custom_vjp
def low_back(v):
    return v

def low_keep(v):
    return (low(v), None)

def low_pass(kept, grad):
    return (grad,)

def back_keep(v):
    return (v, None)

def back_low(kept, grad):
    return (low(grad),)
low.defvjp(low_keep, low_pass)
low_back.defvjp(back_keep, back_low)

def bucket_table(query_rows, key_rows, query_start, buckets, far_limit):
    exact_limit = buckets // 4
    half_count = buckets // 2
    offset = lax.broadcasted_iota(jnp.int32, (query_rows, key_rows), 1) - (lax.broadcasted_iota(jnp.int32, (query_rows, key_rows), 0) + query_start)
    distance = jnp.abs(offset)
    bucket_ids = jnp.minimum(distance, exact_limit)
    for bucket_level in range(exact_limit + 1, half_count):
        border = math.ceil(exact_limit * (far_limit / exact_limit) ** ((bucket_level - exact_limit) / (half_count - exact_limit)))
        bucket_ids = bucket_ids + (distance >= border).astype(jnp.int32)
    return bucket_ids + jnp.where(offset > 0, half_count, 0).astype(jnp.int32)

def project(row_values, weight):
    return jnp.einsum('gld,de->gle', row_values, weight, precision=HIGHEST)

def gelu_tanh(values):
    return jax.nn.gelu(values, approximate=True)

def forward(tokens, norm_gain, query_weight, key_weight, value_weight, output_weight, bucket_head_bias, ffn_gain, router_weight, expert_in, expert_out, lengths, routes):
    devices = N_DP * N_EXPERT
    tok_dev = SEQ_DEV * LEN
    group_size = math.gcd(SEQS, max(1, 4096 // LEN))
    live_mask = jnp.arange(LEN, dtype=jnp.int32)[None, :] < lengths[:, None]
    bucket_ids = bucket_table(LEN, LEN, 0, NB, MAXDIST)
    position_bias = jnp.transpose(bucket_head_bias[bucket_ids], (2, 0, 1))
    score_scale = HDIM ** (-0.5)

    def attend(packed):
        row_block, key_live = packed
        inverse = lax.rsqrt(lax.optimization_barrier(jnp.mean(row_block * row_block, axis=-1, keepdims=True)) + EPSILON)
        normed = low(row_block * inverse * norm_gain)
        head_shape = (group_size, LEN, HEADS, HDIM)
        query_rows = low(low_back(project(normed, query_weight))).reshape(head_shape)
        key_rows = low(low_back(project(normed, key_weight))).reshape(head_shape)
        value_rows = low(low_back(project(normed, value_weight))).reshape(head_shape)
        scores = jnp.einsum('gqhd,gkhd->ghqk', query_rows, key_rows, precision=HIGHEST) * score_scale + position_bias[None]
        scores = jnp.where(key_live[:, None, None, :], low_back(scores), NEGATIVE)
        prob_low = low(jax.nn.softmax(scores, axis=-1))
        mixed = jnp.einsum('ghqk,gkhd->gqhd', prob_low, value_rows, precision=HIGHEST)
        mixed = low(low_back(mixed)).reshape(group_size, LEN, D)
        return row_block + low_back(project(mixed, output_weight))
    grouped = tokens.reshape(SEQS // group_size, group_size, LEN, D)
    resid = lax.map(jax.checkpoint(attend), (grouped, live_mask.reshape(SEQS // group_size, group_size, LEN)))
    resid = resid.reshape(devices, tok_dev, D)
    inverse_two = lax.rsqrt(lax.optimization_barrier(jnp.mean(resid * resid, axis=-1, keepdims=True)) + EPSILON)
    normed_two = low(resid * inverse_two * ffn_gain)
    logits = low_back(jnp.einsum('ntd,de->nte', normed_two, router_weight, precision=HIGHEST))
    router_probs = jax.nn.softmax(logits, axis=-1)
    flat_routes = routes.reshape(devices, tok_dev)
    flat_live = live_mask.reshape(devices, tok_dev)
    route_onehot = (flat_routes[..., None] == jnp.arange(EXPERTS, dtype=jnp.int32)).astype(jnp.int32)
    counted = route_onehot * flat_live[..., None].astype(jnp.int32)
    before = jnp.cumsum(counted, axis=1) - counted
    rank = lax.optimization_barrier(jnp.sum(before * route_onehot, axis=-1))
    kept = flat_live & (rank < CAP)
    slot_index = jnp.where(kept, flat_routes * CAP + rank, EXPERTS * CAP).astype(jnp.int32)
    gate_prob = lax.optimization_barrier(jnp.sum(router_probs * route_onehot.astype(jnp.float32), axis=-1, keepdims=True))

    def place_rows(row_values, index_rows):
        return jnp.zeros((EXPERTS * CAP + 1, D), jnp.float32).at[index_rows].set(row_values)[:EXPERTS * CAP]
    slot_buffer = low_back(jax.vmap(place_rows)(normed_two, slot_index))
    by_expert = jnp.transpose(slot_buffer.reshape(devices, EXPERTS, CAP, D), (1, 0, 2, 3)).reshape(EXPERTS, devices * CAP, D)

    def apply_expert(packed):
        row_values, weight_in, weight_out = packed
        pre_act = low_back(jnp.dot(row_values, weight_in, precision=HIGHEST))
        activated = low(gelu_tanh(pre_act))
        return low(low_back(jnp.dot(activated, weight_out, precision=HIGHEST)))
    returned = lax.map(jax.checkpoint(apply_expert), (by_expert, expert_in, expert_out))
    home_rows = jnp.transpose(returned.reshape(EXPERTS, devices, CAP, D), (1, 0, 2, 3)).reshape(devices, EXPERTS * CAP, D)
    safe_index = jnp.minimum(slot_index, EXPERTS * CAP - 1)
    gathered = jax.vmap(lambda table_rows, index_rows: table_rows[index_rows])(home_rows, safe_index)
    gathered = gathered * kept[..., None].astype(jnp.float32)
    combined = flat_live[..., None].astype(jnp.float32) * (resid + gate_prob * gathered)
    return combined.reshape(SEQS, LEN, D)

def reference(tokens, cotangent, lengths, routes, norm_gain, query_weight, key_weight, value_weight, output_weight, bucket_head_bias, ffn_gain, router_weight, expert_in, expert_out):
    floats = tuple((array.astype(jnp.float32) for array in (tokens, norm_gain, query_weight, key_weight, value_weight, output_weight, bucket_head_bias, ffn_gain, router_weight, expert_in, expert_out)))

    def wrapped(*values):
        return forward(*values, lengths, routes)
    result, pullback = jax.vjp(wrapped, *floats)
    gradients = pullback(cotangent.astype(jnp.float32))
    return (result.astype(jnp.bfloat16), gradients[0], gradients[1], gradients[2], gradients[3], gradients[4], gradients[5], gradients[6], gradients[7], gradients[8], gradients[9], gradients[10])
```

```python
import functools
import math

import jax
import jax.numpy as jnp
from jax import lax
from jax.experimental import pallas as pl
from jax.experimental.pallas import tpu as pltpu
from jax.sharding import PartitionSpec as P

BF = jnp.bfloat16
F32 = jnp.float32
MAXDIST = 128
EPSILON = 1e-06
NEGATIVE = -1000000000.0
TILE = 128
LANES = 128
HALF = 64
LINE = 4 * TILE
VMEM_LIMIT = 60 * 1024 * 1024
GELU_ONE = math.sqrt(2.0 / math.pi)
GELU_CUBE = 0.044715


def dot(left, right, left_dim=1, right_dim=0):
    return lax.dot_general(
        left, right, (((left_dim,), (right_dim,)), ((), ())), preferred_element_type=F32
    )


def iota(shape, dim):
    return lax.broadcasted_iota(jnp.int32, shape, dim)


def bucket_of(offset, buckets, far_limit):
    exact_limit = buckets // 4
    half_count = buckets // 2
    distance = jnp.abs(offset)
    bucket_ids = jnp.minimum(distance, exact_limit)
    for bucket_level in range(exact_limit + 1, half_count):
        border = math.ceil(
            exact_limit
            * (far_limit / exact_limit)
            ** ((bucket_level - exact_limit) / (half_count - exact_limit))
        )
        bucket_ids = bucket_ids + (distance >= border).astype(jnp.int32)
    return bucket_ids + jnp.where(offset > 0, half_count, 0).astype(jnp.int32)


def line_buckets(buckets):
    place = jnp.arange(LINE, dtype=jnp.int32)
    offset = jnp.where(place < 3 * TILE, place - TILE, place - TILE - LINE)
    return bucket_of(offset, buckets, MAXDIST)


def whole(shape):
    return pl.BlockSpec(shape, lambda *_: (0,) * len(shape))


def smem():
    return pl.BlockSpec(memory_space=pltpu.SMEM)


def params():
    return pltpu.CompilerParams(vmem_limit_bytes=VMEM_LIMIT)


def shape_of(shape, dtype):
    return jax.ShapeDtypeStruct(shape, dtype)


def cost(flops, bytes_accessed):
    return pl.CostEstimate(flops=int(flops), bytes_accessed=int(bytes_accessed), transcendentals=0)


def inverse_rms(rows):
    return lax.rsqrt(jnp.mean(rows * rows, axis=-1, keepdims=True) + EPSILON)


def send_rows(starts_ref, slot_row, rows, send_refs):
    for number, send_ref in enumerate(send_refs):
        wanted = iota((send_ref.shape[0], slot_row.shape[1]), 0) + starts_ref[number]
        chosen = jnp.where(wanted == slot_row, 1.0, 0.0).astype(BF)
        send_ref[...] = dot(chosen, rows).astype(BF)


def home_rows(slot_column, wanted_row, blocks):
    chosen = jnp.where(slot_column == wanted_row, 1.0, 0.0).astype(BF)
    return dot(chosen, jnp.concatenate(blocks, axis=0))


def slots_kernel(capacity, experts, starts_ref, length_ref, routes_ref, cotangent_ref, slot_ref, *send_refs):
    seq_len = routes_ref.shape[1]
    routes = routes_ref[...]
    live = iota((1, seq_len), 1) < length_ref[0]
    onehot = jnp.where((iota((experts, seq_len), 0) == routes) & live, 1.0, 0.0)
    earlier = jnp.where(iota((seq_len, seq_len), 0) < iota((seq_len, seq_len), 1), 1.0, 0.0)
    before = dot(onehot.astype(BF), earlier.astype(BF))
    rank = jnp.sum(before * onehot, axis=0, keepdims=True).astype(jnp.int32)
    slot = jnp.where(live & (rank < capacity), routes * capacity + rank, -1)
    slot_ref[...] = slot
    send_rows(starts_ref, slot, cotangent_ref[...], send_refs)


def slots_part(starts, lengths, routes, cotangent, capacity, experts, block_rows):
    seq_len, width = cotangent.shape
    count = starts.shape[0]
    return pl.pallas_call(
        functools.partial(slots_kernel, capacity, experts),
        out_shape=[shape_of((1, seq_len), jnp.int32)]
        + [shape_of((block_rows, width), BF)] * count,
        in_specs=[smem(), smem(), pl.BlockSpec(), pl.BlockSpec()],
        compiler_params=params(),
        name="slots",
    )(starts, lengths, routes, cotangent)


def forward_kernel(
    count,
    starts_ref,
    length_ref,
    slot_ref,
    tokens_ref,
    gain_one_ref,
    query_weight_ref,
    key_weight_ref,
    value_weight_ref,
    out_weight_ref,
    line_ref,
    far_ref,
    gain_two_ref,
    *refs,
):
    probs_ref, qkv_ref, normed_ref, mixed_ref, inverse_ref, resid_ref = refs[:6]
    send_refs = refs[6 : 6 + count]
    qkv_s, mixed_s = refs[6 + count :]
    pair = pl.program_id(0)
    pairs = pl.num_programs(0)
    seq_len, width = tokens_ref.shape
    tiles = seq_len // TILE

    @pl.when(pair == 0)
    def _():
        rows = tokens_ref[...].astype(F32)
        normed = (rows * inverse_rms(rows) * gain_one_ref[...]).astype(BF)
        normed_ref[...] = normed
        for part, weight_ref in enumerate((query_weight_ref, key_weight_ref, value_weight_ref)):
            values = dot(normed, weight_ref[...])
            for number in range(width // LANES):
                block = values[:, number * LANES : (number + 1) * LANES].astype(BF)
                if part == 0:
                    block = block * BF(HALF ** (-0.5))
                qkv_s[part, number] = block

    query = qkv_s[0, pair]
    key = qkv_s[1, pair]
    value = qkv_s[2, pair]
    qkv_ref[0, 0] = query
    qkv_ref[1, 0] = key
    qkv_ref[2, 0] = value
    lane = iota((seq_len, LANES), 1)
    row = iota((seq_len, LANES), 0)
    row_tile = row // TILE
    value_wide = jnp.concatenate([value, jnp.ones((seq_len, LANES), BF)], axis=1)
    outs = []
    for half in range(2):
        own = lane < HALF if half == 0 else lane >= HALF
        extra = lane - HALF if half == 0 else lane
        query_wide = jnp.where(
            own, query.astype(F32), jnp.where((extra == 0) | (extra == 1 + row_tile), 1.0, 0.0)
        ).astype(BF)
        query_tile = extra - 1
        far = jnp.where(
            row_tile <= query_tile - 2,
            far_ref[0, half, 0],
            jnp.where(row_tile >= query_tile + 2, far_ref[0, half, 1], 0.0),
        )
        far = jnp.where((query_tile >= 0) & (query_tile < tiles), far, 0.0)
        far = jnp.where((extra == 0) & (row >= length_ref[0]), NEGATIVE, far)
        key_wide = jnp.where(own, key.astype(F32), far).astype(BF)
        line = jnp.broadcast_to(line_ref[0, half : half + 1, :], (TILE, LINE))
        near = pltpu.roll(line, 0, 1, stride=1, stride_axis=0)[:, : 3 * TILE]
        for tile in range(tiles):
            scores = dot(query_wide[tile * TILE : (tile + 1) * TILE], key_wide, 1, 1)
            low = max(tile - 1, 0)
            high = min(tile + 2, tiles)
            parts = []
            if low > 0:
                parts.append(scores[:, : low * TILE])
            parts.append(
                scores[:, low * TILE : high * TILE]
                + near[:, (low - tile + 1) * TILE : (high - tile + 1) * TILE]
            )
            if high < tiles:
                parts.append(scores[:, high * TILE :])
            scores = jnp.concatenate(parts, axis=1)
            peak = jnp.max(scores, axis=-1, keepdims=True)
            probs_ref[half, tile * TILE : (tile + 1) * TILE, :] = jnp.exp(scores - peak).astype(BF)
        outs.append(dot(probs_ref[half], value_wide))
    first = lane < HALF
    inverse_total = 1.0 / jnp.where(first, outs[0][:, LANES:], outs[1][:, LANES:])
    mixed = jnp.where(first, outs[0][:, :LANES], outs[1][:, :LANES]) * inverse_total
    mixed_s[pair] = mixed.astype(BF)
    inverse_ref[0] = inverse_total

    @pl.when(pair == pairs - 1)
    def _():
        mixed_all = jnp.concatenate([mixed_s[number] for number in range(width // LANES)], axis=1)
        mixed_ref[...] = mixed_all
        resid = tokens_ref[...].astype(F32) + dot(mixed_all, out_weight_ref[...])
        resid_ref[...] = resid
        normed = (resid * inverse_rms(resid) * gain_two_ref[...]).astype(BF)
        send_rows(starts_ref, slot_ref[...], normed, send_refs)


def forward_part(starts, lengths, slot, tokens, gain_one, weights, lines, far, gain_two, block_rows):
    seq_len, width = tokens.shape
    pairs = width // LANES
    count = starts.shape[0]
    square = whole((width, width))
    return pl.pallas_call(
        functools.partial(forward_kernel, count),
        grid=(pairs,),
        out_shape=[
            shape_of((2 * pairs, seq_len, seq_len), BF),
            shape_of((3, pairs, seq_len, LANES), BF),
            shape_of((seq_len, width), BF),
            shape_of((seq_len, width), BF),
            shape_of((pairs, seq_len, LANES), F32),
            shape_of((seq_len, width), F32),
        ]
        + [shape_of((block_rows, width), BF)] * count,
        in_specs=[
            smem(),
            smem(),
            whole((1, seq_len)),
            whole((seq_len, width)),
            whole((1, width)),
            square,
            square,
            square,
            square,
            pl.BlockSpec((1, 2, LINE), lambda p: (p, 0, 0)),
            pl.BlockSpec((1, 2, 2), lambda p: (p, 0, 0), memory_space=pltpu.SMEM),
            whole((1, width)),
        ],
        out_specs=[
            pl.BlockSpec((2, seq_len, seq_len), lambda p: (p, 0, 0)),
            pl.BlockSpec((3, 1, seq_len, LANES), lambda p: (0, p, 0, 0)),
            whole((seq_len, width)),
            whole((seq_len, width)),
            pl.BlockSpec((1, seq_len, LANES), lambda p: (p, 0, 0)),
            whole((seq_len, width)),
        ]
        + [whole((block_rows, width))] * count,
        scratch_shapes=[
            pltpu.VMEM((3, pairs, seq_len, LANES), BF),
            pltpu.VMEM((pairs, seq_len, LANES), BF),
        ],
        compiler_params=params(),
        cost_estimate=cost(50e9, 60e6),
        name="attention_forward",
    )(starts, lengths, slot, tokens, gain_one, *weights, lines, far, gain_two)


def expert_kernel(count, expert_ref, *refs):
    row_refs = refs[:count]
    up_refs = refs[count : 2 * count]
    in_ref, out_ref, router_ref = refs[2 * count : 2 * count + 3]
    act_ref, pre_grad_ref, rows_ref, rows_grad_ref, gate_ref, router_grad_ref = refs[
        2 * count + 3 : 2 * count + 9
    ]
    back_refs = refs[2 * count + 9 : 3 * count + 9]
    total_s, gate_grad_s, probs_s = refs[3 * count + 9 :]
    step = pl.program_id(0)
    steps = pl.num_programs(0)
    block_rows = row_refs[0].shape[0]
    rows = rows_ref.shape[0]
    experts = router_ref.shape[1]
    own = iota((rows, experts), 1) == expert_ref[0]

    @pl.when(step == 0)
    def _():
        for number in range(count):
            rows_ref[pl.ds(number * block_rows, block_rows), :] = row_refs[number][...]
        logits = dot(rows_ref[...], router_ref[...])
        raised = jnp.exp(logits - jnp.max(logits, axis=-1, keepdims=True))
        probs = raised / jnp.sum(raised, axis=-1, keepdims=True)
        probs_s[...] = probs
        gate = jnp.sum(jnp.where(own, probs, 0.0), axis=-1, keepdims=True)
        gate_ref[...] = gate
        gate_grad_s[...] = jnp.zeros_like(gate_grad_s)
        total_s[...] = jnp.zeros_like(total_s)
        for number in range(count):
            part = pl.ds(number * block_rows, block_rows)
            rows_grad_ref[part, :] = (
                up_refs[number][...].astype(F32) * gate[number * block_rows : (number + 1) * block_rows]
            ).astype(BF)

    for number in range(count):
        part = pl.ds(number * block_rows, block_rows)
        pre = dot(row_refs[number][...], in_ref[...])
        act_grad = dot(up_refs[number][...], out_ref[...], 1, 1)
        square = pre * pre
        level = 0.5 + 0.5 * jnp.tanh(pre * (GELU_ONE + GELU_ONE * GELU_CUBE * square))
        act = pre * level
        slope = level + act * (1.0 - level) * (2.0 * GELU_ONE + 6.0 * GELU_ONE * GELU_CUBE * square)
        gate_grad_s[part, :] += jnp.sum(act * act_grad, axis=-1, keepdims=True)
        pre_grad = (act_grad * slope * gate_ref[part, :]).astype(BF)
        act_ref[part, :] = act.astype(BF)
        pre_grad_ref[part, :] = pre_grad
        total_s[part, :] += dot(pre_grad, in_ref[...], 1, 1)

    @pl.when(step == steps - 1)
    def _():
        logit_grad = (
            gate_grad_s[...] * gate_ref[...] * (jnp.where(own, 1.0, 0.0) - probs_s[...])
        ).astype(BF)
        router_grad_ref[...] = dot(logit_grad, rows_ref[...], 0, 0)
        back = total_s[...] + dot(logit_grad, router_ref[...], 1, 1)
        for number in range(count):
            back_refs[number][...] = back[number * block_rows : (number + 1) * block_rows].astype(BF)


def expert_part(expert, row_blocks, up_blocks, expert_in, expert_out, router):
    count = len(row_blocks)
    block_rows, width = row_blocks[0].shape
    rows = count * block_rows
    hidden = expert_in.shape[1]
    experts = router.shape[1]
    tile = 512
    block = whole((block_rows, width))
    return pl.pallas_call(
        functools.partial(expert_kernel, count),
        grid=(hidden // tile,),
        out_shape=[
            shape_of((rows, hidden), BF),
            shape_of((rows, hidden), BF),
            shape_of((rows, width), BF),
            shape_of((rows, width), BF),
            shape_of((rows, 1), F32),
            shape_of((experts, width), F32),
        ]
        + [shape_of((block_rows, width), BF)] * count,
        in_specs=[smem()]
        + [block] * (2 * count)
        + [
            pl.BlockSpec((width, tile), lambda f: (0, f)),
            pl.BlockSpec((tile, width), lambda f: (f, 0)),
            whole((width, experts)),
        ],
        out_specs=[
            pl.BlockSpec((rows, tile), lambda f: (0, f)),
            pl.BlockSpec((rows, tile), lambda f: (0, f)),
            whole((rows, width)),
            whole((rows, width)),
            whole((rows, 1)),
            whole((experts, width)),
        ]
        + [block] * count,
        scratch_shapes=[
            pltpu.VMEM((rows, width), F32),
            pltpu.VMEM((rows, 1), F32),
            pltpu.VMEM((rows, experts), F32),
        ],
        compiler_params=params(),
        cost_estimate=cost(18e9, 40e6),
        name="expert_rows",
    )(expert, *row_blocks, *up_blocks, expert_in, expert_out, router)


def weight_grad_kernel(transposed, me_ref, wide_ref, rows_ref, *out_refs):
    step = pl.program_id(0)
    for number, out_ref in enumerate(out_refs):

        @pl.when(step == number)
        def _(out_ref=out_ref):
            if transposed:
                out_ref[...] = dot(wide_ref[...], rows_ref[...], 0, 0).astype(BF)
            else:
                out_ref[...] = dot(rows_ref[...], wide_ref[...], 0, 0).astype(BF)


def weight_grad_part(me, wide, rows, parts, transposed):
    count, width = rows.shape
    hidden = wide.shape[1]
    tile = hidden // parts
    shape = (tile, width) if transposed else (width, tile)
    return pl.pallas_call(
        functools.partial(weight_grad_kernel, transposed),
        grid_spec=pltpu.PrefetchScalarGridSpec(
            num_scalar_prefetch=1,
            grid=(parts,),
            in_specs=[
                pl.BlockSpec((count, tile), lambda s, me_ref: (0, me_ref[0] ^ s)),
                whole((count, width)),
            ],
            out_specs=[whole(shape)] * parts,
        ),
        out_shape=[shape_of(shape, BF)] * parts,
        compiler_params=params(),
        cost_estimate=cost(2 * count * hidden * width, 20e6),
        name="expert_weight_gradient",
    )(me, wide, rows)


def expert_out_kernel(act_ref, out_ref, gate_ref, *refs):
    total_s = refs[-1]
    send_refs = refs[:-1]
    step = pl.program_id(0)

    @pl.when(step == 0)
    def _():
        total_s[...] = jnp.zeros_like(total_s)

    total_s[...] += dot(act_ref[...], out_ref[...])

    @pl.when(step == pl.num_programs(0) - 1)
    def _():
        block_rows = send_refs[0].shape[0]
        for number, send_ref in enumerate(send_refs):
            part = pl.ds(number * block_rows, block_rows)
            send_ref[...] = (total_s[part, :] * gate_ref[part, :]).astype(BF)


def expert_out_part(act, expert_out, gate, count):
    rows, hidden = act.shape
    width = expert_out.shape[1]
    tile = 512
    block_rows = rows // count
    return pl.pallas_call(
        expert_out_kernel,
        grid=(hidden // tile,),
        out_shape=[shape_of((block_rows, width), BF)] * count,
        in_specs=[
            pl.BlockSpec((rows, tile), lambda f: (0, f)),
            pl.BlockSpec((tile, width), lambda f: (f, 0)),
            whole((rows, 1)),
        ],
        out_specs=[whole((block_rows, width))] * count,
        scratch_shapes=[pltpu.VMEM((rows, width), F32)],
        compiler_params=params(),
        cost_estimate=cost(2 * rows * hidden * width, 16e6),
        name="expert_output",
    )(act, expert_out, gate)


def result_kernel(length_ref, slot_ref, wanted_ref, resid_ref, *refs):
    blocks = [ref[...] for ref in refs[:-1]]
    total = resid_ref[...] + home_rows(slot_ref[...], wanted_ref[...], blocks)
    live = iota((total.shape[0], 1), 0) < length_ref[0]
    refs[-1][...] = jnp.where(live, total, 0.0).astype(BF)


def result_part(lengths, slot_column, wanted, resid, blocks):
    return pl.pallas_call(
        result_kernel,
        out_shape=shape_of(resid.shape, BF),
        in_specs=[smem()] + [pl.BlockSpec()] * (3 + len(blocks)),
        compiler_params=params(),
        cost_estimate=cost(2e9, 10e6),
        name="result",
    )(lengths, slot_column, wanted, resid, *blocks)


def middle_kernel(
    length_ref,
    slot_ref,
    wanted_ref,
    resid_ref,
    cotangent_ref,
    mixed_ref,
    out_weight_ref,
    gain_ref,
    *refs,
):
    blocks = [ref[...] for ref in refs[:-4]]
    resid_grad_ref, mixed_grad_ref, out_grad_ref, gain_grad_ref = refs[-4:]
    upstream = home_rows(slot_ref[...], wanted_ref[...], blocks)
    resid = resid_ref[...]
    inverse = inverse_rms(resid)
    scaled = gain_ref[...] * upstream
    gain_grad_ref[...] = jnp.sum(upstream * resid * inverse, axis=0, keepdims=True)
    live = iota((resid.shape[0], 1), 0) < length_ref[0]
    resid_grad = (
        jnp.where(live, cotangent_ref[...].astype(F32), 0.0)
        + inverse * scaled
        - resid * (inverse * inverse * inverse * jnp.mean(scaled * resid, axis=-1, keepdims=True))
    )
    resid_grad_ref[...] = resid_grad
    attn_grad = resid_grad.astype(BF)
    mixed_grad_ref[...] = dot(attn_grad, out_weight_ref[...], 1, 1).astype(BF)
    out_grad_ref[...] = dot(mixed_ref[...], attn_grad, 0, 0).astype(BF)


def middle_part(lengths, slot_column, wanted, resid, cotangent, mixed, out_weight, gain, blocks):
    seq_len, width = resid.shape
    return pl.pallas_call(
        middle_kernel,
        out_shape=[
            shape_of((seq_len, width), F32),
            shape_of((seq_len, width), BF),
            shape_of((width, width), BF),
            shape_of((1, width), F32),
        ],
        in_specs=[smem()] + [pl.BlockSpec()] * (7 + len(blocks)),
        compiler_params=params(),
        cost_estimate=cost(5e9, 20e6),
        name="expert_norm_backward",
    )(lengths, slot_column, wanted, resid, cotangent, mixed, out_weight, gain, *blocks)


def backward_kernel(
    qkv_ref, probs_ref, mixed_ref, grad_ref, inverse_ref, back_ref, line_ref, far_ref, score_s
):
    seq_len = mixed_ref.shape[0]
    tiles = seq_len // TILE
    query = qkv_ref[0, 0]
    key = qkv_ref[1, 0]
    value = qkv_ref[2, 0]
    lane = iota((seq_len, LANES), 1)
    row_tile = iota((seq_len, LANES), 0) // TILE
    scaled = grad_ref[...].astype(F32) * inverse_ref[0]
    product = scaled * mixed_ref[...].astype(F32)
    scaled_low = scaled.astype(BF)
    key_wide = jnp.concatenate([key, jnp.where(lane == row_tile, 1.0, 0.0).astype(BF)], axis=1)
    backward_rows = jnp.where(iota((TILE, TILE), 0) + iota((TILE, TILE), 1) == TILE - 1, 1.0, 0.0)
    query_backs = []
    key_backs = []
    value_backs = []
    for half in range(2):
        own = lane < HALF if half == 0 else lane >= HALF
        extra = lane - HALF if half == 0 else lane
        delta = jnp.sum(jnp.where(own, product, 0.0), axis=-1, keepdims=True)
        high = delta.astype(BF).astype(F32)
        grad_wide = jnp.where(
            own, scaled, jnp.where(extra == 0, -high, jnp.where(extra == 1, high - delta, 0.0))
        ).astype(BF)
        value_wide = jnp.where(
            own, value.astype(F32), jnp.where((extra == 0) | (extra == 1), 1.0, 0.0)
        ).astype(BF)
        near = [jnp.zeros((TILE, TILE), F32) for _ in range(3)]
        for tile in range(tiles):
            part = slice(tile * TILE, (tile + 1) * TILE)
            prob_grad = dot(grad_wide[part], value_wide, 1, 1)
            score_grad = (probs_ref[half, part, :].astype(F32) * prob_grad).astype(BF)
            score_s[half, part, :] = score_grad
            for side in range(3):
                other = tile + side - 1
                if 0 <= other < tiles:
                    near[side] = near[side] + score_grad[
                        :, other * TILE : (other + 1) * TILE
                    ].astype(F32)
        query_wide = dot(score_s[half], key_wide)
        query_backs.append(query_wide[:, :LANES])
        sums = query_wide[:, LANES:]
        far_left = jnp.sum(jnp.where(lane <= row_tile - 2, sums, 0.0), axis=0, keepdims=True)
        far_right = jnp.sum(jnp.where(lane >= row_tile + 2, sums, 0.0), axis=0, keepdims=True)
        far_ref[0, 2 * half : 2 * half + 1, :] = far_left
        far_ref[0, 2 * half + 1 : 2 * half + 2, :] = far_right
        key_backs.append(dot(query, score_s[half], 0, 0))
        value_backs.append(dot(scaled_low, probs_ref[half], 0, 0))
        spread = lax.dot_general(
            backward_rows,
            jnp.concatenate(near, axis=1),
            (((1,), (0,)), ((), ())),
            precision=lax.Precision.HIGHEST,
            preferred_element_type=F32,
        )
        spread = jnp.concatenate([spread, jnp.zeros((TILE, TILE), F32)], axis=1)
        spread = pltpu.roll(spread, 0, 1, stride=1, stride_axis=0)
        line_ref[0, half : half + 1, :] = jnp.sum(spread, axis=0, keepdims=True)
    first = lane < HALF
    back_ref[0] = (jnp.where(first, query_backs[0], query_backs[1]) * HALF ** (-0.5)).astype(BF)
    for place, backs in ((1, key_backs), (2, value_backs)):
        joined = jnp.concatenate([backs[0][:HALF], backs[1][HALF:]], axis=0)
        back_ref[place] = joined.T.astype(BF)


def backward_part(qkv, probs, mixed, mixed_grad, inverse):
    seq_len, width = mixed.shape
    pairs = width // LANES
    column = pl.BlockSpec((seq_len, LANES), lambda p: (0, p))
    return pl.pallas_call(
        backward_kernel,
        grid=(pairs,),
        out_shape=[
            shape_of((3, seq_len, width), BF),
            shape_of((pairs, 2, LINE), F32),
            shape_of((pairs, 4, LANES), F32),
        ],
        in_specs=[
            pl.BlockSpec((3, 1, seq_len, LANES), lambda p: (0, p, 0, 0)),
            pl.BlockSpec((2, seq_len, seq_len), lambda p: (p, 0, 0)),
            column,
            column,
            pl.BlockSpec((1, seq_len, LANES), lambda p: (p, 0, 0)),
        ],
        out_specs=[
            pl.BlockSpec((3, seq_len, LANES), lambda p: (0, 0, p)),
            pl.BlockSpec((1, 2, LINE), lambda p: (p, 0, 0)),
            pl.BlockSpec((1, 4, LANES), lambda p: (p, 0, 0)),
        ],
        scratch_shapes=[pltpu.VMEM((2, seq_len, seq_len), BF)],
        compiler_params=params(),
        cost_estimate=cost(60e9, 60e6),
        name="attention_backward",
    )(qkv, probs, mixed, mixed_grad, inverse)


def projection_grad_kernel(normed_ref, back_ref, out_ref):
    out_ref[0] = dot(normed_ref[...], back_ref[0], 0, 0).astype(BF)


def projection_grad_part(normed, back):
    parts, seq_len, width = back.shape
    return pl.pallas_call(
        projection_grad_kernel,
        grid=(parts,),
        out_shape=shape_of((parts, width, width), BF),
        in_specs=[
            whole((seq_len, width)),
            pl.BlockSpec((1, seq_len, width), lambda p: (p, 0, 0)),
        ],
        out_specs=pl.BlockSpec((1, width, width), lambda p: (p, 0, 0)),
        compiler_params=params(),
        cost_estimate=cost(parts * 2 * seq_len * width * width, 10e6),
        name="projection_gradient",
    )(normed, back)


def token_grad_kernel(
    back_ref, query_weight_ref, key_weight_ref, value_weight_ref, tokens_ref, gain_ref, resid_grad_ref, out_ref, gain_grad_ref
):
    upstream = dot(back_ref[0], query_weight_ref[...], 1, 1)
    upstream += dot(back_ref[1], key_weight_ref[...], 1, 1)
    upstream += dot(back_ref[2], value_weight_ref[...], 1, 1)
    rows = tokens_ref[...].astype(F32)
    inverse = inverse_rms(rows)
    scaled = gain_ref[...] * upstream
    gain_grad_ref[...] = jnp.sum(upstream * rows * inverse, axis=0, keepdims=True)
    out_ref[...] = (
        resid_grad_ref[...]
        + inverse * scaled
        - rows * (inverse * inverse * inverse * jnp.mean(scaled * rows, axis=-1, keepdims=True))
    )


def token_grad_part(back, weights, tokens, gain, resid_grad):
    seq_len, width = tokens.shape
    return pl.pallas_call(
        token_grad_kernel,
        out_shape=[shape_of((seq_len, width), F32), shape_of((1, width), F32)],
        compiler_params=params(),
        cost_estimate=cost(3 * 2 * seq_len * width * width, 16e6),
        name="token_gradient",
    )(back, *weights, tokens, gain, resid_grad)


def swap(values, axis, size, distance):
    return lax.ppermute(values, axis, [(place, place ^ distance) for place in range(size)])


def exchange(blocks, axis, size, capacity):
    if len(blocks) == size:
        return [blocks[0]] + [
            swap(blocks[distance], axis, size, distance) for distance in range(1, size)
        ]
    (rows,) = blocks
    parts = rows.reshape(size, capacity, rows.shape[1])
    return [
        lax.all_to_all(parts, axis, split_axis=0, concat_axis=0, tiled=True).reshape(rows.shape)
    ]


def scatter_sum(parts, axis, size, bits):
    parts = dict(enumerate(parts))
    for number, bit in enumerate(bits):
        last = number == len(bits) - 1
        for distance in [d for d in parts if d & bit]:
            arrived = swap(parts.pop(distance), axis, size, bit)
            total = parts[distance ^ bit].astype(F32) + arrived.astype(F32)
            parts[distance ^ bit] = total if last else total.astype(BF)
    return parts[0]


def stages_of(dp_size, expert_size):
    stages = [("expert", expert_size, (1,))]
    bits = [1 << n for n in range(dp_size.bit_length() - 1)]
    stages += [("dp", dp_size, tuple(bits[n : n + 2])) for n in range(0, len(bits), 2)]
    bits = [1 << n for n in range(1, expert_size.bit_length() - 1)]
    stages += [("expert", expert_size, tuple(bits[n : n + 2])) for n in range(0, len(bits), 2)]
    return stages


def distances_of(bits):
    return [sum(bit for n, bit in enumerate(bits) if (k >> n) & 1) for k in range(1 << len(bits))]


def place_of(axis, bits):
    index = lax.axis_index(axis)
    return sum(((index // bit) % 2) << n for n, bit in enumerate(bits))


def sum_everywhere(values, stages):
    for axis, size, bits in stages:
        distances = distances_of(bits)
        place = place_of(axis, bits)
        rows = values.shape[0] // len(distances)
        total = lax.dynamic_slice_in_dim(values, place * rows, rows, 0).astype(F32)
        for number, distance in list(enumerate(distances))[1:]:
            part = lax.dynamic_slice_in_dim(values, (place ^ number) * rows, rows, 0)
            total = total + swap(part, axis, size, distance).astype(F32)
        values = total.astype(BF)
    for axis, size, bits in reversed(stages):
        distances = distances_of(bits)
        place = place_of(axis, bits)
        rows = values.shape[0]
        joined = jnp.zeros((rows * len(distances),) + values.shape[1:], BF)
        joined = lax.dynamic_update_slice_in_dim(joined, values, place * rows, 0)
        for number, distance in list(enumerate(distances))[1:]:
            arrived = swap(values, axis, size, distance)
            joined = lax.dynamic_update_slice_in_dim(joined, arrived, (place ^ number) * rows, 0)
        values = joined
    return values.astype(F32)


def sum_small(values, stages):
    for axis, size, bits in stages:
        total = values
        for distance in distances_of(bits)[1:]:
            total = total + swap(values, axis, size, distance)
        values = total
    return values


def on_device(
    dp_size,
    expert_size,
    tokens,
    cotangent,
    lengths,
    routes,
    norm_gain,
    query_weight,
    key_weight,
    value_weight,
    output_weight,
    bucket_head_bias,
    ffn_gain,
    router_weight,
    expert_in,
    expert_out,
):
    seq_count, seq_len, width = tokens.shape
    assert seq_count == 1
    buckets, heads = bucket_head_bias.shape
    pairs = heads // 2
    experts = router_weight.shape[1]
    capacity = max(2, 5 * seq_len // (4 * experts))
    expert = lax.axis_index("expert")
    group = lax.axis_index("dp").reshape(1)
    if expert_size <= 8 and capacity % 16 == 0:
        starts = (expert ^ jnp.arange(expert_size, dtype=jnp.int32)) * capacity
        block_rows = capacity
    else:
        starts = jnp.zeros((1,), jnp.int32)
        block_rows = experts * capacity
    count = starts.shape[0]
    wanted = (starts[:, None] + jnp.arange(block_rows, dtype=jnp.int32)[None, :]).reshape(1, -1)
    rows_in = tokens.reshape(seq_len, width)
    upstream = cotangent.reshape(seq_len, width)
    gain_one = norm_gain.astype(F32).reshape(1, width)
    gain_two = ffn_gain.astype(F32).reshape(1, width)
    weight_in = expert_in.reshape(expert_in.shape[1:])
    weight_out = expert_out.reshape(expert_out.shape[1:])
    weights = (query_weight, key_weight, value_weight)

    slot, *up_send = slots_part(starts, lengths, routes, upstream, capacity, experts, block_rows)
    up_blocks = exchange(up_send, "expert", expert_size, capacity)
    slot_column = slot.reshape(seq_len, 1)

    table = bucket_head_bias.astype(F32)
    place_bucket = line_buckets(buckets)
    indicator = (place_bucket[None, :] == jnp.arange(buckets, dtype=jnp.int32)[:, None]).astype(F32)
    lines = lax.dot_general(
        table, indicator, (((0,), (0,)), ((), ())), precision=lax.Precision.HIGHEST
    ).reshape(pairs, 2, LINE)
    far = jnp.stack([table[buckets // 2 - 1], table[buckets - 1]], axis=-1).reshape(pairs, 2, 2)

    probs, qkv, normed, mixed, inverse_total, resid, *row_send = forward_part(
        starts,
        lengths,
        slot,
        rows_in,
        gain_one,
        (*weights, output_weight),
        lines,
        far,
        gain_two,
        block_rows,
    )
    row_blocks = exchange(row_send, "expert", expert_size, capacity)
    act, pre_grad, expert_rows, rows_grad, gate, router_grad, *back_send = expert_part(
        expert.reshape(1), row_blocks, up_blocks, weight_in, weight_out, router_weight
    )
    back_blocks = exchange(back_send, "expert", expert_size, capacity)
    out_parts = weight_grad_part(group, act, rows_grad, dp_size, True)
    in_parts = weight_grad_part(group, pre_grad, expert_rows, dp_size, False)
    bits = [1 << n for n in range(dp_size.bit_length() - 1)]
    expert_out_grad = scatter_sum(out_parts, "dp", dp_size, bits)
    expert_in_grad = scatter_sum(in_parts, "dp", dp_size, bits[::-1])
    result_send = expert_out_part(act, weight_out, gate, count)
    result_blocks = exchange(result_send, "expert", expert_size, capacity)

    resid_grad, mixed_grad, output_grad, ffn_gain_grad = middle_part(
        lengths, slot_column, wanted, resid, upstream, mixed, output_weight, gain_two, back_blocks
    )
    stages = stages_of(dp_size, expert_size)
    output_grad = sum_everywhere(output_grad, stages)
    back, near_sums, far_sums = backward_part(qkv, probs, mixed, mixed_grad, inverse_total)
    projection_grad = projection_grad_part(normed, back)
    projection_grad = sum_everywhere(
        projection_grad.reshape(3 * width, width), stages
    ).reshape(3, width, width)
    token_grad, norm_gain_grad = token_grad_part(back, weights, rows_in, gain_one, resid_grad)
    result = result_part(lengths, slot_column, wanted, resid, result_blocks)

    sum_bucket = bucket_of(jnp.arange(LINE, dtype=jnp.int32) - (2 * TILE - 1), buckets, MAXDIST)
    sum_indicator = sum_bucket[None, :] == jnp.arange(buckets, dtype=jnp.int32)[:, None]
    bucket_grad = lax.dot_general(
        sum_indicator.astype(F32),
        near_sums.reshape(heads, LINE),
        (((1,), (1,)), ((), ())),
        precision=lax.Precision.HIGHEST,
    )
    far_sums = jnp.sum(far_sums, axis=-1).reshape(heads, 2)
    bucket_row = jnp.arange(buckets, dtype=jnp.int32)[:, None]
    bucket_grad = bucket_grad + jnp.where(
        bucket_row == buckets // 2 - 1,
        far_sums[None, :, 0],
        jnp.where(bucket_row == buckets - 1, far_sums[None, :, 1], 0.0),
    )
    small = jnp.concatenate(
        [
            norm_gain_grad,
            ffn_gain_grad,
            router_grad,
            jnp.pad(bucket_grad.T, ((0, 0), (0, width - buckets))),
        ],
        axis=0,
    )
    small = sum_small(small, stages)
    return (
        result.reshape(tokens.shape),
        token_grad.reshape(tokens.shape),
        small[0],
        projection_grad[0],
        projection_grad[1],
        projection_grad[2],
        output_grad,
        small[2 + experts :, :buckets].T,
        small[1],
        small[2 : 2 + experts].T,
        expert_in_grad[None],
        expert_out_grad[None],
    )


def solution(mesh):
    in_specs = (
        P(("dp", "expert"), None, None),
        P(("dp", "expert"), None, None),
        P(("dp", "expert")),
        P(("dp", "expert"), None),
        P(),
        P(),
        P(),
        P(),
        P(),
        P(),
        P(),
        P(),
        P("expert", None, None),
        P("expert", None, None),
    )
    out_specs = (
        P(("dp", "expert"), None, None),
        P(("dp", "expert"), None, None),
        P(),
        P(),
        P(),
        P(),
        P(),
        P(),
        P(),
        P(),
        P("expert", None, "dp"),
        P("expert", "dp", None),
    )
    return jax.shard_map(
        functools.partial(on_device, mesh.shape["dp"], mesh.shape["expert"]),
        mesh=mesh,
        in_specs=in_specs,
        out_specs=out_specs,
        check_vma=False,
    )
```

```python
import functools
import math

import jax
import jax.numpy as jnp
from jax import lax
from jax.experimental import pallas as pl
from jax.experimental.pallas import tpu as pltpu
from jax.sharding import PartitionSpec as P

BF = jnp.bfloat16
F32 = jnp.float32
MAXDIST = 128
EPSILON = 1e-06
NEGATIVE = -1000000000.0
TILE = 128
LANES = 128
HALF = 64
LINE = 4 * TILE
GELU_ONE = math.sqrt(2.0 / math.pi)
GELU_CUBE = 0.044715
SEND_LIMIT = 32


def dot(left, right, left_dim=1, right_dim=0):
    return lax.dot_general(
        left, right, (((left_dim,), (right_dim,)), ((), ())), preferred_element_type=F32
    )


def iota(shape, dim):
    return lax.broadcasted_iota(jnp.int32, shape, dim)


def bucket_of(offset, buckets, far_limit):
    exact_limit = buckets // 4
    half_count = buckets // 2
    distance = jnp.abs(offset)
    bucket_ids = jnp.minimum(distance, exact_limit)
    for bucket_level in range(exact_limit + 1, half_count):
        border = math.ceil(
            exact_limit
            * (far_limit / exact_limit)
            ** ((bucket_level - exact_limit) / (half_count - exact_limit))
        )
        bucket_ids = bucket_ids + (distance >= border).astype(jnp.int32)
    return bucket_ids + jnp.where(offset > 0, half_count, 0).astype(jnp.int32)


def whole(shape):
    return pl.BlockSpec(shape, lambda *_: (0,) * len(shape))


def by_rows(rows, columns):
    return pl.BlockSpec((rows, columns), lambda step: (step, 0))


def add_rows(ref, values):
    @pl.when(pl.program_id(0) == 0)
    def _():
        ref[...] = values

    @pl.when(pl.program_id(0) > 0)
    def _():
        ref[...] += values


def smem():
    return pl.BlockSpec(memory_space=pltpu.SMEM)


def params(mebibytes):
    return pltpu.CompilerParams(vmem_limit_bytes=mebibytes * 1024 * 1024)


def shape_of(shape, dtype):
    return jax.ShapeDtypeStruct(shape, dtype)


def inverse_rms(rows):
    return lax.rsqrt(jnp.mean(rows * rows, axis=-1, keepdims=True) + EPSILON)


def send_rows(expert_ref, slot_row, rows, plan, send_refs):
    block_rows = plan.block_rows
    size = plan.blocks * block_rows
    place = iota((size, 1), 0)
    wanted = place
    if plan.paired:
        for distance in range(plan.blocks):
            first = distance * block_rows
            wanted = jnp.where(
                place >= first, place - first + (expert_ref[0] ^ distance) * block_rows, wanted
            )
    chosen = jnp.where(wanted == slot_row, 1.0, 0.0).astype(BF)
    sent = dot(chosen, rows).astype(BF)
    first = 0
    for send_ref in send_refs:
        send_ref[...] = sent[first : first + send_ref.shape[0]]
        first += send_ref.shape[0]


def home_rows(expert_ref, column, refs, plan):
    block_rows = plan.block_rows
    rows = jnp.concatenate(
        [ref[first : first + block_rows, :] for ref, first in plan.take(refs)], axis=0
    )
    place = iota((1, rows.shape[0]), 1)
    wanted = place
    for distance in range(plan.blocks):
        first = distance * block_rows
        base = (expert_ref[0] ^ distance) * block_rows if plan.paired else 0
        wanted = jnp.where(place >= first, place - first + base, wanted)
    chosen = jnp.where(column[:, :1] == wanted, 1.0, 0.0).astype(BF)
    return dot(chosen, rows)


def slots_kernel(
    capacity, experts, plan, expert_ref, length_ref, routes_ref, cotangent_ref, slot_ref, column_ref, *send_refs
):
    seq_len = routes_ref.shape[1]
    routes = routes_ref[...]
    live = iota((1, seq_len), 1) < length_ref[0]
    onehot = jnp.where((iota((experts, seq_len), 0) == routes) & live, 1.0, 0.0)
    earlier = jnp.where(iota((seq_len, seq_len), 0) < iota((seq_len, seq_len), 1), 1.0, 0.0)
    before = dot(onehot.astype(BF), earlier.astype(BF))
    rank = jnp.sum(before * onehot, axis=0, keepdims=True).astype(jnp.int32)
    slot = jnp.where(live & (rank < capacity), routes * capacity + rank, -1)
    slot_ref[...] = slot
    wide = jnp.broadcast_to(slot.astype(F32), (LANES, seq_len))
    column_ref[...] = wide.T.astype(jnp.int32)
    send_rows(expert_ref, slot, cotangent_ref[...], plan, send_refs)


def slots_part(expert, lengths, routes, cotangent, capacity, experts, plan):
    seq_len, width = cotangent.shape
    return pl.pallas_call(
        functools.partial(slots_kernel, capacity, experts, plan),
        out_shape=[shape_of((1, seq_len), jnp.int32), shape_of((seq_len, LANES), jnp.int32)]
        + [shape_of((rows, width), BF) for rows in plan.arrays],
        in_specs=[smem(), smem(), pl.BlockSpec(), pl.BlockSpec()],
        compiler_params=params(58),
        name="slots",
    )(expert, lengths, routes, cotangent)


def forward_kernel(
    plan,
    expert_ref,
    length_ref,
    slot_ref,
    tokens_ref,
    gain_one_ref,
    query_weight_ref,
    key_weight_ref,
    value_weight_ref,
    out_weight_ref,
    bias_ref,
    gain_two_ref,
    *refs,
):
    probs_ref, qkv_ref, lefts_ref, inverse_ref, resid_ref = refs[:5]
    send_refs = refs[5:-3]
    qkv_s, mixed_s, line_s = refs[-3:]
    pair = pl.program_id(0)
    pairs = pl.num_programs(0)
    seq_len, width = tokens_ref.shape
    tiles = seq_len // TILE

    @pl.when(pair == 0)
    def _():
        buckets = bias_ref.shape[1]
        place = iota((buckets, LINE), 1)
        offset = jnp.where(place < 3 * TILE, place - TILE, place - TILE - LINE)
        chosen = bucket_of(offset, buckets, MAXDIST) == iota((buckets, LINE), 0)
        lines = dot(bias_ref[...], jnp.where(chosen, 1.0, 0.0).astype(BF))
        for number in range(width // LANES):
            line_s[number, 0:2, :] = lines[2 * number : 2 * number + 2]
        rows = tokens_ref[...].astype(F32)
        normed = (rows * inverse_rms(rows) * gain_one_ref[...].astype(F32).reshape(1, width)).astype(BF)
        lefts_ref[0] = normed
        for part, weight_ref in enumerate((query_weight_ref, key_weight_ref, value_weight_ref)):
            values = dot(normed, weight_ref[...])
            for number in range(width // LANES):
                block = values[:, number * LANES : (number + 1) * LANES].astype(BF)
                if part == 0:
                    block = block * BF(HALF ** (-0.5))
                qkv_s[part, number] = block

    query = qkv_s[0, pair]
    key = qkv_s[1, pair]
    value = qkv_s[2, pair]
    qkv_ref[0, 0] = query
    qkv_ref[1, 0] = key
    qkv_ref[2, 0] = value
    lane = iota((seq_len, LANES), 1)
    row = iota((seq_len, LANES), 0)
    row_tile = row // TILE
    value_wide = jnp.concatenate([value, jnp.ones((seq_len, LANES), BF)], axis=1)
    query_wides, key_wides, nears = [], [], []
    for half in range(2):
        own = lane < HALF if half == 0 else lane >= HALF
        extra = lane - HALF if half == 0 else lane
        query_wides.append(
            jnp.where(
                own,
                query.astype(F32),
                jnp.where((extra == 0) | (extra == 1 + row_tile), 1.0, 0.0),
            ).astype(BF)
        )
        query_tile = extra - 1
        line = jnp.broadcast_to(line_s[pair, half : half + 1, :], (TILE, LINE))
        far = jnp.where(
            row_tile <= query_tile - 2,
            line[0:1, 0:1],
            jnp.where(row_tile >= query_tile + 2, line[0:1, 3 * TILE - 1 : 3 * TILE], 0.0),
        )
        far = jnp.where((query_tile >= 0) & (query_tile < tiles), far, 0.0)
        far = jnp.where((extra == 0) & (row >= length_ref[0]), NEGATIVE, far)
        key_wides.append(jnp.where(own, key.astype(F32), far).astype(BF))
        nears.append(pltpu.roll(line, 0, 1, stride=1, stride_axis=0)[:, : 3 * TILE])
    first = lane[:TILE] < HALF
    for tile in range(tiles):
        part = slice(tile * TILE, (tile + 1) * TILE)
        low = max(tile - 1, 0)
        high = min(tile + 2, tiles)
        outs = []
        for half in range(2):
            scores = dot(query_wides[half][part], key_wides[half], 1, 1)
            middle = nears[half][:, (low - tile + 1) * TILE : (high - tile + 1) * TILE]
            pieces = [scores[:, low * TILE : high * TILE] + middle]
            if low > 0:
                pieces.insert(0, scores[:, : low * TILE])
            if high < tiles:
                pieces.append(scores[:, high * TILE :])
            scores = jnp.concatenate(pieces, axis=1)
            peak = jnp.max(scores, axis=-1, keepdims=True)
            raised = jnp.exp(scores - peak).astype(BF)
            probs_ref[half, part, :] = raised
            outs.append(dot(raised, value_wide))
        inverse_total = 1.0 / jnp.where(first, outs[0][:, LANES:], outs[1][:, LANES:])
        mixed = jnp.where(first, outs[0][:, :LANES], outs[1][:, :LANES]) * inverse_total
        mixed_s[pair, part, :] = mixed.astype(BF)
        inverse_ref[0, part, :] = inverse_total

    @pl.when(pair == pairs - 1)
    def _():
        mixed_all = jnp.concatenate([mixed_s[number] for number in range(width // LANES)], axis=1)
        lefts_ref[1] = mixed_all
        resid = tokens_ref[...].astype(F32) + dot(mixed_all, out_weight_ref[...])
        resid_ref[...] = resid
        normed = (resid * inverse_rms(resid) * gain_two_ref[...].astype(F32).reshape(1, width)).astype(BF)
        send_rows(expert_ref, slot_ref[...], normed, plan, send_refs)


def forward_part(expert, lengths, slot, tokens, gain_one, weights, bias, gain_two, plan):
    seq_len, width = tokens.shape
    pairs = width // LANES
    square = whole((width, width))
    return pl.pallas_call(
        functools.partial(forward_kernel, plan),
        grid=(pairs,),
        out_shape=[
            shape_of((2 * pairs, seq_len, seq_len), BF),
            shape_of((3, pairs, seq_len, LANES), BF),
            shape_of((2, seq_len, width), BF),
            shape_of((pairs, seq_len, LANES), F32),
            shape_of((seq_len, width), F32),
        ]
        + [shape_of((rows, width), BF) for rows in plan.arrays],
        in_specs=[
            smem(),
            smem(),
            whole((1, seq_len)),
            whole((seq_len, width)),
            whole((width,)),
            square,
            square,
            square,
            square,
            whole(bias.shape),
            whole((width,)),
        ],
        out_specs=[
            pl.BlockSpec((2, seq_len, seq_len), lambda p: (p, 0, 0)),
            pl.BlockSpec((3, 1, seq_len, LANES), lambda p: (0, p, 0, 0)),
            whole((2, seq_len, width)),
            pl.BlockSpec((1, seq_len, LANES), lambda p: (p, 0, 0)),
            whole((seq_len, width)),
        ]
        + [whole((rows, width)) for rows in plan.arrays],
        scratch_shapes=[
            pltpu.VMEM((3, pairs, seq_len, LANES), BF),
            pltpu.VMEM((pairs, seq_len, LANES), BF),
            pltpu.VMEM((pairs, 8, LINE), F32),
        ],
        compiler_params=params(58),
        name="attention_forward",
    )(expert, lengths, slot, tokens, gain_one, *weights, bias, gain_two)


def expert_up_kernel(plan, out_ref, *refs):
    up_refs = refs[:-2]
    up_ref, act_grad_ref = refs[-2:]

    @pl.when(pl.program_id(0) == 0)
    def _():
        for number, (ref, first) in enumerate(plan.take(up_refs)):
            rows = plan.block_rows
            up_ref[number * rows : (number + 1) * rows, :] = ref[first : first + rows, :]

    act_grad_ref[...] = dot(up_ref[...], out_ref[0], 1, 1).astype(BF)


def expert_up_part(up_arrays, expert_out, plan):
    width = expert_out.shape[2]
    hidden = expert_out.shape[1]
    rows = sum(plan.arrays)
    tile = 512
    return pl.pallas_call(
        functools.partial(expert_up_kernel, plan),
        grid=(hidden // tile,),
        out_shape=[shape_of((rows, width), BF), shape_of((rows, hidden), BF)],
        in_specs=[pl.BlockSpec((1, tile, width), lambda f: (0, f, 0))]
        + [whole(array.shape) for array in up_arrays],
        out_specs=[whole((rows, width)), pl.BlockSpec((rows, tile), lambda f: (0, f))],
        compiler_params=params(28),
        name="expert_activation_gradient",
    )(expert_out, *up_arrays)


def expert_kernel(plan, expert_ref, up_ref, act_grad_ref, in_ref, router_ref, *refs):
    count = len(plan.arrays)
    row_refs = refs[: -(7 + count)]
    act_ref, slope_ref, scaled_ref, rows_grad_ref, gate_ref, logit_grad_ref = refs[
        -(7 + count) : -(1 + count)
    ]
    back_refs, rows_ref = refs[-(1 + count) : -1], refs[-1]
    block_rows = plan.block_rows
    step = pl.program_id(0)
    steps = len(plan.arrays)
    rows, hidden = act_ref.shape
    experts = router_ref.shape[0]
    blocks = plan.take(row_refs)
    for number in range(steps):

        @pl.when(step == number)
        def _(number=number):
            each = len(blocks) // steps
            for place in range(each):
                ref, first = blocks[number * each + place]
                rows_ref[place * block_rows : (place + 1) * block_rows, :] = ref[
                    first : first + block_rows, :
                ]

    own = iota((rows, experts), 1) == expert_ref[0]
    logits = dot(rows_ref[...], router_ref[...], 1, 1)
    raised = jnp.exp(logits - jnp.max(logits, axis=-1, keepdims=True))
    probs = raised / jnp.sum(raised, axis=-1, keepdims=True)
    gate = jnp.sum(jnp.where(own, probs, 0.0), axis=-1, keepdims=True)
    gate_ref[...] = gate
    rows_grad_ref[...] = (up_ref[...].astype(F32) * gate).astype(BF)
    scaled_ref[...] = (rows_ref[...].astype(F32) * gate).astype(BF)
    gate_grad = jnp.zeros((rows, LANES), F32)
    tile = 512
    for first in range(0, hidden, tile):
        part = slice(first, first + tile)
        pre = dot(rows_ref[...], in_ref[0, :, part])
        act_grad = act_grad_ref[:, part]
        square = pre * pre
        level = 0.5 + 0.5 * jnp.tanh(pre * (GELU_ONE + GELU_ONE * GELU_CUBE * square))
        act = (pre * level).astype(BF)
        level = level.astype(BF)
        slope = level + act * (BF(1.0) - level) * (
            BF(2.0 * GELU_ONE) + BF(6.0 * GELU_ONE * GELU_CUBE) * square.astype(BF)
        )
        act_ref[:, part] = act
        product = (act * act_grad).astype(F32)
        for place in range(0, tile, LANES):
            gate_grad += product[:, place : place + LANES]
        slope_ref[:, part] = act_grad * slope
    gate_grad = jnp.sum(gate_grad, axis=-1, keepdims=True)
    logit_grad = gate_grad * (jnp.where(own, 1.0, 0.0) - probs)
    logit_grad_ref[...] = logit_grad.astype(BF)
    logit_grad = (gate * logit_grad).astype(BF)
    back = gate * dot(slope_ref[...], in_ref[0], 1, 1) + dot(logit_grad, router_ref[...])
    back = back.astype(BF)
    for number in range(steps):

        @pl.when(step == number)
        def _(number=number):
            back_refs[number][...] = back


def expert_part(expert, up_rows, act_grad, expert_in, router, row_arrays, plan):
    rows, width = up_rows.shape
    hidden = expert_in.shape[2]
    experts = router.shape[0]
    steps = len(plan.arrays)
    some = rows // steps
    return pl.pallas_call(
        functools.partial(expert_kernel, plan),
        grid=(steps,),
        out_shape=[
            shape_of((rows, hidden), BF),
            shape_of((rows, hidden), BF),
            shape_of((rows, width), BF),
            shape_of((rows, width), BF),
            shape_of((rows, 1), F32),
            shape_of((rows, experts), BF),
        ]
        + [shape_of((count, width), BF) for count in plan.arrays],
        in_specs=[
            smem(),
            by_rows(some, width),
            by_rows(some, hidden),
            whole((1, width, hidden)),
            whole((experts, width)),
        ]
        + [whole(array.shape) for array in row_arrays],
        out_specs=[by_rows(some, columns) for columns in (hidden, hidden, width, width, 1, experts)]
        + [whole((count, width)) for count in plan.arrays],
        scratch_shapes=[pltpu.VMEM((some, width), BF)],
        compiler_params=params(44),
        name="expert_rows",
    )(expert, up_rows, act_grad, expert_in, router, *row_arrays)


def later_sums_kernel(*refs):
    count = len(refs) // 3
    for keep_ref, there_ref, out_ref in zip(refs[:count], refs[count : 2 * count], refs[2 * count :]):
        out_ref[...] = (keep_ref[...].astype(F32) + there_ref[...].astype(F32)).astype(BF)


def later_sums(keeps, theres):
    count, rows, columns = keeps[0].shape
    later = count // 2
    some = rows // 4

    def block(first):
        return pl.BlockSpec((1, some, columns), lambda t, r: (first + t, r, 0))

    return pl.pallas_call(
        later_sums_kernel,
        grid=(later, 4),
        out_shape=[shape_of((later, rows, columns), BF)] * len(keeps),
        in_specs=[block(count - later)] * (2 * len(keeps)),
        out_specs=[block(0)] * len(keeps),
        compiler_params=params(58),
        name="later_sums",
    )(*keeps, *theres)


def weight_grad_kernel(transposed, count, *refs):
    _, wide_refs, rows_refs, out_refs = [refs[n * count : (n + 1) * count] for n in range(4)]
    for turned, wide_ref, rows_ref, out_ref in zip(transposed, wide_refs, rows_refs, out_refs):
        left_ref, right_ref = (wide_ref, rows_ref) if turned else (rows_ref, wide_ref)
        out_ref[0] = dot(left_ref[...], right_ref[...], 0, 0).astype(BF)


def weight_grad_part(parts, terms):
    tiles, wides, rows, transposed = zip(*terms)
    steps = tiles[0].shape[0]
    count, width = rows[0].shape
    tile = wides[0].shape[1] // parts
    shapes = [(tile, width) if turned else (width, tile) for turned in transposed]
    return pl.pallas_call(
        functools.partial(weight_grad_kernel, transposed, len(terms)),
        grid_spec=pltpu.PrefetchScalarGridSpec(
            num_scalar_prefetch=len(terms),
            grid=(steps,),
            in_specs=[
                pl.BlockSpec((count, tile), lambda s, *refs, number=number: (0, refs[number][s]))
                for number in range(len(terms))
            ]
            + [whole((count, width))] * len(terms),
            out_specs=[pl.BlockSpec((1,) + shape, lambda s, *_: (s, 0, 0)) for shape in shapes],
        ),
        out_shape=[shape_of((steps,) + shape, BF) for shape in shapes],
        compiler_params=params(SEND_LIMIT),
        name="expert_weight_gradients",
    )(*tiles, *wides, *rows)


def expert_out_kernel(act_ref, out_ref, gate_ref, *send_refs):
    rows = (dot(act_ref[...], out_ref[0]) * gate_ref[...]).astype(BF)
    for number, send_ref in enumerate(send_refs):

        @pl.when(pl.program_id(0) == number)
        def _(send_ref=send_ref):
            send_ref[...] = rows


def expert_out_part(act, expert_out, gate, plan):
    rows, hidden = act.shape
    width = expert_out.shape[2]
    steps = len(plan.arrays)
    return pl.pallas_call(
        expert_out_kernel,
        grid=(steps,),
        out_shape=[shape_of((count, width), BF) for count in plan.arrays],
        in_specs=[
            by_rows(rows // steps, hidden),
            whole((1, hidden, width)),
            by_rows(rows // steps, 1),
        ],
        out_specs=[whole((count, width)) for count in plan.arrays],
        compiler_params=params(32),
        name="expert_output",
    )(act, expert_out, gate)


ROW_STEPS = 4


def result_kernel(plan, expert_ref, length_ref, column_ref, resid_ref, *refs):
    total = resid_ref[...] + home_rows(expert_ref, column_ref[...], refs[:-1], plan)
    rows = total.shape[0]
    live = iota((rows, 1), 0) + pl.program_id(0) * rows < length_ref[0]
    refs[-1][...] = jnp.where(live, total, 0.0).astype(BF)


def result_part(expert, lengths, column, resid, arrays, plan):
    seq_len, width = resid.shape
    rows = seq_len // ROW_STEPS
    return pl.pallas_call(
        functools.partial(result_kernel, plan),
        grid=(ROW_STEPS,),
        out_shape=shape_of(resid.shape, BF),
        in_specs=[smem(), smem(), by_rows(rows, LANES), by_rows(rows, width)]
        + [whole(array.shape) for array in arrays],
        out_specs=by_rows(rows, width),
        compiler_params=params(58),
        name="result",
    )(expert, lengths, column, resid, *arrays)


def middle_kernel(
    plan,
    expert_ref,
    length_ref,
    column_ref,
    resid_ref,
    cotangent_ref,
    out_weight_ref,
    gain_ref,
    *refs,
):
    resid_grad_ref, mixed_grad_ref, attn_grad_ref, gain_grad_ref = refs[-4:]
    upstream = home_rows(expert_ref, column_ref[...], refs[:-4], plan)
    resid = resid_ref[...]
    rows = resid.shape[0]
    inverse = inverse_rms(resid)
    scaled = gain_ref[...].astype(F32).reshape(1, -1) * upstream
    add_rows(gain_grad_ref, jnp.sum(upstream * resid * inverse, axis=0, keepdims=True))
    live = iota((rows, 1), 0) + pl.program_id(0) * rows < length_ref[0]
    resid_grad = (
        jnp.where(live, cotangent_ref[...].astype(F32), 0.0)
        + inverse * scaled
        - resid * (inverse * inverse * inverse * jnp.mean(scaled * resid, axis=-1, keepdims=True))
    )
    resid_grad_ref[...] = resid_grad
    attn_grad = resid_grad.astype(BF)
    mixed_grad_ref[...] = dot(attn_grad, out_weight_ref[...], 1, 1).astype(BF)
    attn_grad_ref[...] = attn_grad


def middle_part(expert, lengths, column, resid, cotangent, out_weight, gain, arrays, plan):
    seq_len, width = resid.shape
    rows = seq_len // ROW_STEPS
    block = by_rows(rows, width)
    return pl.pallas_call(
        functools.partial(middle_kernel, plan),
        grid=(ROW_STEPS,),
        out_shape=[
            shape_of((seq_len, width), F32),
            shape_of((seq_len, width), BF),
            shape_of((seq_len, width), BF),
            shape_of((1, width), F32),
        ],
        in_specs=[smem(), smem(), by_rows(rows, LANES), block, block, whole((width, width)), whole((width,))]
        + [whole(array.shape) for array in arrays],
        out_specs=[block, block, block, whole((1, width))],
        compiler_params=params(58),
        name="expert_norm_backward",
    )(expert, lengths, column, resid, cotangent, out_weight, gain, *arrays)


def backward_kernel(
    qkv_ref, probs_ref, mixed_ref, grad_ref, attn_grad_ref, inverse_ref, back_ref, line_ref, score_s
):
    seq_len = grad_ref.shape[0]
    back_ref[3] = attn_grad_ref[...]
    tiles = seq_len // TILE
    query = qkv_ref[0, 0]
    key = qkv_ref[1, 0]
    value = qkv_ref[2, 0]
    lane = iota((seq_len, LANES), 1)
    row_tile = iota((seq_len, LANES), 0) // TILE
    scaled = grad_ref[...].astype(F32) * inverse_ref[0]
    product = scaled * mixed_ref[0].astype(F32)
    scaled_low = scaled.astype(BF)
    key_wide = jnp.concatenate([key, jnp.where(lane == row_tile, 1.0, 0.0).astype(BF)], axis=1)
    backward_rows = jnp.where(iota((TILE, TILE), 0) + iota((TILE, TILE), 1) == TILE - 1, 1.0, 0.0)
    query_backs = []
    key_backs = []
    value_backs = []
    for half in range(2):
        own = lane < HALF if half == 0 else lane >= HALF
        extra = lane - HALF if half == 0 else lane
        delta = jnp.sum(jnp.where(own, product, 0.0), axis=-1, keepdims=True)
        high = delta.astype(BF).astype(F32)
        grad_wide = jnp.where(
            own, scaled, jnp.where(extra == 0, -high, jnp.where(extra == 1, high - delta, 0.0))
        ).astype(BF)
        value_wide = jnp.where(
            own, value.astype(F32), jnp.where((extra == 0) | (extra == 1), 1.0, 0.0)
        ).astype(BF)
        near = [jnp.zeros((TILE, TILE), F32) for _ in range(3)]
        for tile in range(tiles):
            part = slice(tile * TILE, (tile + 1) * TILE)
            prob_grad = dot(grad_wide[part], value_wide, 1, 1)
            score_grad = (probs_ref[half, part, :].astype(F32) * prob_grad).astype(BF)
            score_s[half, part, :] = score_grad
            for side in range(3):
                other = tile + side - 1
                if 0 <= other < tiles:
                    near[side] = near[side] + score_grad[
                        :, other * TILE : (other + 1) * TILE
                    ].astype(F32)
        query_wide = dot(score_s[half], key_wide)
        query_backs.append(query_wide[:, :LANES])
        sums = query_wide[:, LANES:]
        far_left = jnp.sum(jnp.where(lane <= row_tile - 2, sums, 0.0), axis=0, keepdims=True)
        far_right = jnp.sum(jnp.where(lane >= row_tile + 2, sums, 0.0), axis=0, keepdims=True)
        line_ref[0, half : half + 1, LINE : LINE + LANES] = far_left
        line_ref[0, half : half + 1, LINE + LANES :] = far_right
        key_backs.append(dot(query, score_s[half], 0, 0))
        value_backs.append(dot(scaled_low, probs_ref[half], 0, 0))
        spread = lax.dot_general(
            backward_rows,
            jnp.concatenate(near, axis=1),
            (((1,), (0,)), ((), ())),
            precision=lax.Precision.HIGHEST,
            preferred_element_type=F32,
        )
        spread = jnp.concatenate([spread, jnp.zeros((TILE, TILE), F32)], axis=1)
        spread = pltpu.roll(spread, 0, 1, stride=1, stride_axis=0)
        line_ref[0, half : half + 1, :LINE] = jnp.sum(spread, axis=0, keepdims=True)
    first = lane < HALF
    back_ref[0] = (jnp.where(first, query_backs[0], query_backs[1]) * HALF ** (-0.5)).astype(BF)
    for place, backs in ((1, key_backs), (2, value_backs)):
        joined = jnp.concatenate([backs[0][:HALF], backs[1][HALF:]], axis=0)
        back_ref[place] = joined.T.astype(BF)


def backward_part(qkv, probs, lefts, mixed_grad, attn_grad, inverse):
    _, seq_len, width = lefts.shape
    pairs = width // LANES
    column = pl.BlockSpec((seq_len, LANES), lambda p: (0, p))
    return pl.pallas_call(
        backward_kernel,
        grid=(pairs,),
        out_shape=[
            shape_of((4, seq_len, width), BF),
            shape_of((pairs, 2, LINE + 2 * LANES), F32),
        ],
        in_specs=[
            pl.BlockSpec((3, 1, seq_len, LANES), lambda p: (0, p, 0, 0)),
            pl.BlockSpec((2, seq_len, seq_len), lambda p: (p, 0, 0)),
            pl.BlockSpec((1, seq_len, LANES), lambda p: (1, 0, p)),
            column,
            column,
            pl.BlockSpec((1, seq_len, LANES), lambda p: (p, 0, 0)),
        ],
        out_specs=[
            pl.BlockSpec((4, seq_len, LANES), lambda p: (0, 0, p)),
            pl.BlockSpec((1, 2, LINE + 2 * LANES), lambda p: (p, 0, 0)),
        ],
        scratch_shapes=[pltpu.VMEM((2, seq_len, seq_len), BF)],
        compiler_params=params(58),
        name="attention_backward",
    )(qkv, probs, lefts, mixed_grad, attn_grad, inverse)


def projection_grad_kernel(left_places_ref, right_places_ref, left_ref, right_ref, out_ref):
    out_ref[...] = dot(left_ref[0], right_ref[0], 0, 0).astype(BF)


def projection_grad_part(left_places, right_places, lefts, rights):
    _, seq_len, width = lefts.shape
    count = left_places.shape[0]
    return pl.pallas_call(
        projection_grad_kernel,
        grid_spec=pltpu.PrefetchScalarGridSpec(
            num_scalar_prefetch=2,
            grid=(count,),
            in_specs=[
                pl.BlockSpec((1, seq_len, width), lambda s, left, right: (left[s], 0, 0)),
                pl.BlockSpec((1, seq_len, width), lambda s, left, right: (right[s], 0, 0)),
            ],
            out_specs=pl.BlockSpec((width, width), lambda s, left, right: (s, 0)),
        ),
        out_shape=shape_of((count * width, width), BF),
        compiler_params=params(58),
        name="projection_gradient",
    )(left_places, right_places, lefts, rights)


def token_grad_kernel(
    back_ref,
    query_weight_ref,
    key_weight_ref,
    value_weight_ref,
    tokens_ref,
    gain_ref,
    resid_grad_ref,
    out_ref,
):
    upstream = None
    for part, weight_ref in enumerate((query_weight_ref, key_weight_ref, value_weight_ref)):
        term = dot(back_ref[part], weight_ref[...], 1, 1)
        upstream = term if upstream is None else upstream + term
    rows = tokens_ref[...].astype(F32)
    inverse = inverse_rms(rows)
    scaled = gain_ref[...].astype(F32).reshape(1, -1) * upstream
    out_ref[...] = (
        resid_grad_ref[...]
        + inverse * scaled
        - rows * (inverse * inverse * inverse * jnp.mean(scaled * rows, axis=-1, keepdims=True))
    )


def token_grad_part(back, weights, tokens, gain, resid_grad):
    seq_len, width = tokens.shape
    rows = seq_len // ROW_STEPS
    block = by_rows(rows, width)
    return pl.pallas_call(
        token_grad_kernel,
        grid=(ROW_STEPS,),
        out_shape=shape_of((seq_len, width), F32),
        in_specs=[pl.BlockSpec((3, rows, width), lambda step: (0, step, 0))]
        + [whole((width, width))] * 3
        + [block, whole((width,)), block],
        out_specs=block,
        compiler_params=params(58),
        name="token_gradient",
    )(back, *weights, tokens, gain, resid_grad)


def swap(values, axis, size, distance):
    return lax.ppermute(values, axis, [(place, place ^ distance) for place in range(size)])


def after(values, *others):
    return lax.optimization_barrier((values, *others))[0]


class Plan:
    def __init__(self, size, capacity, experts):
        self.size = size
        self.capacity = capacity
        self.paired = size == 8 and capacity % 16 == 0
        if self.paired:
            self.block_rows = capacity
            self.blocks = size
            self.arrays = [2 * capacity] * (size // 2)
        else:
            self.block_rows = experts * capacity
            self.blocks = 1
            self.arrays = [experts * capacity]

    def turn(self, rows):
        parts = rows.reshape(self.size, self.capacity, rows.shape[1])
        parts = lax.all_to_all(parts, "expert", split_axis=0, concat_axis=0, tiled=True)
        return parts.reshape(rows.shape)

    def cross(self, arrays):
        if not self.paired:
            return [self.turn(array) for array in arrays]
        return [
            array if k == 0 else swap(array, "expert", self.size, 2 * k)
            for k, array in enumerate(arrays)
        ]

    def finish(self, arrays):
        if not self.paired:
            return arrays
        return [*arrays, *[swap(array, "expert", self.size, 1) for array in arrays]]

    def take(self, refs):
        if not self.paired:
            return [(refs[0], 0)]
        half = len(refs) // 2
        return [
            place for pair in zip(refs[:half], refs[half:]) for place in zip(pair, (0, self.block_rows))
        ]


def stages_of(dp_size, expert_size):
    stages = [("expert", expert_size, (1,))]
    bits = [1 << n for n in range(dp_size.bit_length() - 1)]
    stages += [("dp", dp_size, tuple(bits[n : n + 2])) for n in range(0, len(bits), 2)]
    bits = [1 << n for n in range(1, expert_size.bit_length() - 1)]
    return stages + [("expert", expert_size, tuple(bits[n : n + 2])) for n in range(0, len(bits), 2)]


def distances_of(bits):
    return [sum(bit for n, bit in enumerate(bits) if (k >> n) & 1) for k in range(1 << len(bits))]


def place_of(stage):
    axis, _, bits = stage
    index = lax.axis_index(axis)
    return sum(((index // bit) % 2) << n for n, bit in enumerate(bits))


def share_kernel(inputs, place_ref, *refs):
    in_refs, out_refs = refs[:inputs], refs[inputs:]
    for number, out_ref in enumerate(out_refs):
        rows = out_ref.shape[0]
        if len(out_refs) == 1:
            part = slice(None)
        else:
            part = pl.ds(pl.multiple_of((place_ref[0] ^ number) * rows, rows), rows)
        out_ref[...] = sum(ref[part, :].astype(F32) for ref in in_refs).astype(BF)


def share_one(parts, stage):
    count = 1 if stage is None else 1 << len(stage[2])
    place = jnp.int32(0) if stage is None else place_of(stage)
    rows, width = parts[0].shape[0] // count, parts[0].shape[1]
    if rows % 16:
        total = sum(part.astype(F32) for part in parts).astype(BF)
        return [
            lax.dynamic_slice_in_dim(total, (place ^ number) * rows, rows, 0)
            for number in range(count)
        ]
    return pl.pallas_call(
        functools.partial(share_kernel, len(parts)),
        out_shape=[shape_of((rows, width), BF)] * count,
        in_specs=[smem()] + [pl.BlockSpec()] * len(parts),
        compiler_params=params(58),
        name="share",
    )(place.reshape(1), *parts)


def scatter(parts, stage):
    axis, size, bits = stage
    return [
        part if distance == 0 else swap(part, axis, size, distance)
        for part, distance in zip(parts, distances_of(bits))
    ]


def gather(values, stage):
    axis, size, bits = stage
    return [
        values if distance == 0 else swap(values, axis, size, distance)
        for distance in distances_of(bits)
    ]


def join_kernel(place_ref, *refs):
    out_ref = refs[-1]
    for number, ref in enumerate(refs[:-1]):
        rows = ref.shape[0]
        part = pl.ds(pl.multiple_of((place_ref[0] ^ number) * rows, rows), rows)
        out_ref[part, :] = ref[...]


def join(parts, stage):
    place = place_of(stage)
    rows, width = parts[0].shape
    if rows % 16:
        joined = jnp.zeros((rows * len(parts), width), BF)
        for number, part in enumerate(parts):
            joined = lax.dynamic_update_slice_in_dim(joined, part, (place ^ number) * rows, 0)
        return joined
    return pl.pallas_call(
        join_kernel,
        out_shape=shape_of((rows * len(parts), width), BF),
        in_specs=[smem()] + [pl.BlockSpec()] * len(parts),
        compiler_params=params(58),
        name="join",
    )(place.reshape(1), *parts)


def widen_kernel(place_ref, own_ref, other_ref, *refs):
    weight_refs, out_refs, gain_ref = refs[:-3], refs[-3:-1], refs[-1]
    for number, out_ref in enumerate(out_refs):

        @pl.when(place_ref[0] == number)
        def _(out_ref=out_ref):
            out_ref[...] = own_ref[...].astype(F32)

        @pl.when(place_ref[0] != number)
        def _(out_ref=out_ref):
            out_ref[...] = other_ref[...].astype(F32)

    total = sum(
        jnp.sum(out_ref[...] * weight_ref[...].astype(F32), axis=1, keepdims=True)
        for out_ref, weight_ref in zip(out_refs, weight_refs)
    )
    gain_ref[...] = jnp.broadcast_to(total, (total.shape[0], LANES)).T[:1]


def widen(parts, stage, weights):
    rows, width = parts[0].shape
    some = 2 * LANES
    block = by_rows(some, width)
    return pl.pallas_call(
        widen_kernel,
        grid=(rows // some,),
        out_shape=[shape_of(parts[0].shape, F32)] * 2 + [shape_of((1, rows), F32)],
        in_specs=[smem()] + [block] * (2 + len(weights)),
        out_specs=[block, block, pl.BlockSpec((1, some), lambda step: (0, step))],
        compiler_params=params(58),
        name="widen",
    )(place_of(stage).reshape(1), *parts, *weights)


def halving_order(bits):
    if not bits:
        return [0]
    rest = halving_order(bits[1:])
    return rest + [distance | bits[0] for distance in rest]


def on_device(
    dp_size,
    expert_size,
    tokens,
    cotangent,
    lengths,
    routes,
    norm_gain,
    query_weight,
    key_weight,
    value_weight,
    output_weight,
    bucket_head_bias,
    ffn_gain,
    router_weight,
    expert_in,
    expert_out,
):
    seq_count, seq_len, width = tokens.shape
    assert seq_count == 1
    buckets, heads = bucket_head_bias.shape
    experts = router_weight.shape[1]
    capacity = max(2, 5 * seq_len // (4 * experts))
    plan = Plan(expert_size, capacity, experts)
    expert = lax.axis_index("expert").reshape(1)
    group = lax.axis_index("dp")
    rows_in = tokens.reshape(seq_len, width)
    upstream = cotangent.reshape(seq_len, width)
    weights = (query_weight, key_weight, value_weight)

    slot, column, *up_send = slots_part(expert, lengths, routes, upstream, capacity, experts, plan)
    up_there = plan.cross(up_send)
    probs, qkv, lefts, inverse_total, resid, *row_send = forward_part(
        expert,
        lengths,
        slot,
        rows_in,
        norm_gain,
        (*weights, output_weight),
        bucket_head_bias.T,
        ffn_gain,
        plan,
    )
    row_send, up_there = lax.optimization_barrier((row_send, up_there))
    row_there = plan.cross(row_send)
    up_rows, act_grad = expert_up_part(plan.finish(up_there), expert_out, plan)
    row_there = lax.optimization_barrier((row_there, act_grad))[0]
    act, slope, scaled_rows, rows_grad, gate, logit_grad, *back_send = expert_part(
        expert, up_rows, act_grad, expert_in, router_weight.T, plan.finish(row_there), plan
    )
    router_grad = dot(logit_grad, scaled_rows, 0, 0)
    back_there = plan.cross(back_send)

    bits = [1 << n for n in range(dp_size.bit_length() - 1)]
    half = dp_size // 2
    orders = (bits, bits[::-1])
    tiles = [group ^ jnp.array(halving_order(order), jnp.int32) for order in orders]
    grad_terms = [(act, rows_grad, True), (slope, scaled_rows, False)]
    sends = [
        weight_grad_part(dp_size, [(tile[half:], *term)])[0] for tile, term in zip(tiles, grad_terms)
    ]
    arrived = [swap(send, "dp", dp_size, order[0]) for send, order in zip(sends, orders)]
    keeps = weight_grad_part(
        dp_size, [(tile[:half], *term) for tile, term in zip(tiles, grad_terms)]
    )
    result_send = expert_out_part(act, expert_out, gate, plan)
    back_there = lax.optimization_barrier((back_there, keeps, result_send))[0]
    back_arrays = plan.finish(back_there)

    resid_grad, mixed_grad, attn_grad, ffn_gain_grad = middle_part(
        expert, lengths, column, after(resid, *keeps), upstream, output_weight, ffn_gain, back_arrays, plan
    )
    result_send = lax.optimization_barrier((result_send, back_there))[0]
    result_there = plan.cross(result_send)

    arrived = lax.optimization_barrier((arrived, back_arrays))[0]
    seconds = later_sums(keeps, arrived)
    rests = [list(order[1:]) for order in orders]
    arrived_seconds = [
        swap(send, "dp", dp_size, rest[0]) if rest else None for send, rest in zip(seconds, rests)
    ]
    mixed_grad = after(mixed_grad, *seconds)

    back, lines = backward_part(qkv, probs, lefts, mixed_grad, attn_grad, inverse_total)
    back, result_there, arrived_seconds = lax.optimization_barrier(
        (back, result_there, arrived_seconds)
    )

    sum_bucket = bucket_of(jnp.arange(LINE, dtype=jnp.int32) - (2 * TILE - 1), buckets, MAXDIST)
    sum_indicator = sum_bucket[None, :] == jnp.arange(buckets, dtype=jnp.int32)[:, None]
    lines = jnp.pad(
        lines.reshape(heads, LINE + 2 * LANES), ((0, 0), (0, width - LINE - 2 * LANES))
    )
    small = jnp.concatenate([ffn_gain_grad, router_grad, lines], axis=0)
    stages = stages_of(dp_size, expert_size)
    steps = [
        (axis, size, bit)
        for axis, size, bits in stages[2:] + stages[:1] + stages[1:2]
        for bit in bits
    ]

    def sum_step(small):
        if not steps:
            return small
        return small + swap(small, *steps.pop(0))

    core = place_of(stages[0])
    result_arrays = plan.finish(result_there)

    def gradient(chunk, which, *others):
        left, right = (0 * which, which) if chunk == 0 else (which, 2 + which)
        args = lax.optimization_barrier(((lefts, back), others))[0]
        return projection_grad_part(left.reshape(1), right.reshape(1), *args)

    sent = [gradient(0, 1 - core)]
    sent.append(gradient(1, 1 - core, sent[0]))
    there = [swap(values, *stages[0][:2], 1) for values in sent]
    kept = gradient(0, core, sent[1])
    shares = [share_one([kept, there[0]], stages[1])]
    kept = gradient(1, core, shares[0])
    shares.append(share_one([kept, there[1]], stages[1]))
    moved = [scatter(parts, stages[1]) for parts in shares]
    later_back, small = lax.optimization_barrier((back, small, shares[1]))[:2]
    token_grad = token_grad_part(later_back, weights, rows_in, norm_gain, resid_grad)
    moved[0], token_grad = lax.optimization_barrier((moved[0], token_grad))
    while len(steps) > len(stages[1][2]):
        small = sum_step(small)
    moved[1], small, result_arrays = lax.optimization_barrier((moved[1], small, result_arrays))
    for stage in stages[2:]:
        shares = [share_one(parts, stage) for parts in moved]
        moved = [scatter(parts, stage) for parts in shares]
        while steps:
            small = sum_step(small)
        moved[1], small = lax.optimization_barrier((moved[1], small))
    chunks = [share_one(parts, None)[0] for parts in moved]
    for stage in stages[:1:-1]:
        chunks = [join(gather(values, stage), stage) for values in chunks]
    there = [gather(values, stages[1]) for values in chunks]
    keeps, arrived, arrived_seconds, resid = lax.optimization_barrier(
        (keeps, arrived, arrived_seconds, resid, chunks)
    )[:4]
    result = result_part(expert, lengths, column, resid, result_arrays, plan)
    weight_sums = []
    for rest, keep, term, second in zip(rests, keeps, arrived, arrived_seconds):
        total = keep[: half // 2].astype(F32) + term[: half // 2].astype(F32)
        if rest:
            total = total + second.astype(F32)
        weight_sums.append(total)
    there, weight_sums, result = lax.optimization_barrier((there, weight_sums, result))
    expert_out_grad, expert_in_grad = weight_sums
    chunks = [join(parts, stages[1]) for parts in there]
    pairs_of = [gather(chunk, stages[0]) for chunk in chunks]
    query_grad, key_grad, gain_sum = widen(pairs_of[0], stages[0], (query_weight, key_weight))
    value_grad, output_grad, value_sum = widen(pairs_of[1], stages[0], (value_weight,))
    norm_gain_grad = (gain_sum + value_sum).reshape(width) / norm_gain.astype(F32)

    lines = small[1 + experts :]
    bucket_grad = lax.dot_general(
        sum_indicator.astype(F32),
        lines[:, :LINE],
        (((1,), (1,)), ((), ())),
        precision=lax.Precision.HIGHEST,
    )
    far_sums = jnp.sum(lines[:, LINE : LINE + 2 * LANES].reshape(heads, 2, LANES), axis=-1)
    bucket_row = jnp.arange(buckets, dtype=jnp.int32)[:, None]
    bucket_grad = bucket_grad + jnp.where(
        bucket_row == buckets // 2 - 1,
        far_sums[None, :, 0],
        jnp.where(bucket_row == buckets - 1, far_sums[None, :, 1], 0.0),
    )
    return (
        result.reshape(tokens.shape),
        token_grad.reshape(tokens.shape),
        norm_gain_grad,
        query_grad,
        key_grad,
        value_grad,
        output_grad,
        bucket_grad,
        small[0],
        small[1 : 1 + experts].T,
        expert_in_grad,
        expert_out_grad,
    )


def solution(mesh):
    in_specs = (
        P(("dp", "expert"), None, None),
        P(("dp", "expert"), None, None),
        P(("dp", "expert")),
        P(("dp", "expert"), None),
        P(),
        P(),
        P(),
        P(),
        P(),
        P(),
        P(),
        P(),
        P("expert", None, None),
        P("expert", None, None),
    )
    out_specs = (
        P(("dp", "expert"), None, None),
        P(("dp", "expert"), None, None),
        P(),
        P(),
        P(),
        P(),
        P(),
        P(),
        P(),
        P(),
        P("expert", None, "dp"),
        P("expert", "dp", None),
    )
    return jax.shard_map(
        functools.partial(on_device, mesh.shape["dp"], mesh.shape["expert"]),
        mesh=mesh,
        in_specs=in_specs,
        out_specs=out_specs,
        check_vma=False,
    )
```

```python
import functools
import math

import jax
import jax.numpy as jnp
from jax import lax
from jax.experimental import pallas as pl
from jax.experimental.pallas import tpu as pltpu
from jax.sharding import PartitionSpec as P

BF = jnp.bfloat16
F32 = jnp.float32
MAXDIST = 128
EPSILON = 1e-06
NEGATIVE = -1000000000.0
TILE = 128
BUCKETS = 32
LANES = 128
HALF = 64
LINE = 4 * TILE
GELU_ONE = math.sqrt(2.0 / math.pi)
GELU_CUBE = 0.044715
SEND_LIMIT = 32


def dot(left, right, left_dim=1, right_dim=0):
    return lax.dot_general(
        left, right, (((left_dim,), (right_dim,)), ((), ())), preferred_element_type=F32
    )


def iota(shape, dim):
    return lax.broadcasted_iota(jnp.int32, shape, dim)


def bucket_of(offset, buckets, far_limit):
    exact_limit = buckets // 4
    half_count = buckets // 2
    distance = jnp.abs(offset)
    bucket_ids = jnp.minimum(distance, exact_limit)
    for bucket_level in range(exact_limit + 1, half_count):
        border = math.ceil(
            exact_limit
            * (far_limit / exact_limit)
            ** ((bucket_level - exact_limit) / (half_count - exact_limit))
        )
        bucket_ids = bucket_ids + (distance >= border).astype(jnp.int32)
    return bucket_ids + jnp.where(offset > 0, half_count, 0).astype(jnp.int32)


def whole(shape):
    return pl.BlockSpec(shape, lambda *_: (0,) * len(shape))


def by_rows(rows, columns):
    return pl.BlockSpec((rows, columns), lambda step: (step, 0))


def add_rows(ref, values):
    @pl.when(pl.program_id(0) == 0)
    def _():
        ref[...] = values

    @pl.when(pl.program_id(0) > 0)
    def _():
        ref[...] += values


def smem():
    return pl.BlockSpec(memory_space=pltpu.SMEM)


def params(mebibytes):
    return pltpu.CompilerParams(vmem_limit_bytes=mebibytes * 1024 * 1024)


def shape_of(shape, dtype):
    return jax.ShapeDtypeStruct(shape, dtype)


def inverse_rms(rows):
    return lax.rsqrt(jnp.mean(rows * rows, axis=-1, keepdims=True) + EPSILON)


def send_rows(expert_ref, slot_row, rows, plan, send_refs):
    block_rows = plan.block_rows
    size = plan.blocks * block_rows
    place = iota((size, 1), 0)
    wanted = place
    if plan.paired:
        for distance in range(plan.blocks):
            first = distance * block_rows
            wanted = jnp.where(
                place >= first, place - first + (expert_ref[0] ^ distance) * block_rows, wanted
            )
    chosen = jnp.where(wanted == slot_row, 1.0, 0.0).astype(BF)
    sent = dot(chosen, rows).astype(BF)
    first = 0
    for send_ref in send_refs:
        send_ref[...] = sent[first : first + send_ref.shape[0]]
        first += send_ref.shape[0]


def home_rows(expert_ref, column, refs, plan):
    block_rows = plan.block_rows
    rows = jnp.concatenate([ref[...] for ref in plan.by_distance(refs)], axis=0)
    place = iota((1, rows.shape[0]), 1)
    wanted = place
    for distance in range(plan.blocks):
        first = distance * block_rows
        base = (expert_ref[0] ^ distance) * block_rows if plan.paired else 0
        wanted = jnp.where(place >= first, place - first + base, wanted)
    chosen = jnp.where(column[:, :1] == wanted, 1.0, 0.0).astype(BF)
    return dot(chosen, rows)


def slots_kernel(
    capacity, experts, plan, expert_ref, length_ref, routes_ref, cotangent_ref, slot_ref, column_ref, *send_refs
):
    seq_len = routes_ref.shape[1]
    routes = routes_ref[...]
    live = iota((1, seq_len), 1) < length_ref[0]
    onehot = jnp.where((iota((experts, seq_len), 0) == routes) & live, 1.0, 0.0)
    earlier = jnp.where(iota((seq_len, seq_len), 0) < iota((seq_len, seq_len), 1), 1.0, 0.0)
    before = dot(onehot.astype(BF), earlier.astype(BF))
    rank = jnp.sum(before * onehot, axis=0, keepdims=True).astype(jnp.int32)
    slot = jnp.where(live & (rank < capacity), routes * capacity + rank, -1)
    slot_ref[...] = slot
    wide = jnp.broadcast_to(slot.astype(F32), (LANES, seq_len))
    column_ref[...] = wide.T.astype(jnp.int32)
    send_rows(expert_ref, slot, cotangent_ref[...], plan, send_refs)


def slots_part(expert, lengths, routes, cotangent, capacity, experts, plan):
    seq_len, width = cotangent.shape
    return pl.pallas_call(
        functools.partial(slots_kernel, capacity, experts, plan),
        out_shape=[shape_of((1, seq_len), jnp.int32), shape_of((seq_len, LANES), jnp.int32)]
        + [shape_of((rows, width), BF) for rows in plan.arrays],
        in_specs=[smem(), smem(), pl.BlockSpec(), pl.BlockSpec()],
        compiler_params=params(58),
        name="slots",
    )(expert, lengths, routes, cotangent)


def forward_kernel(
    plan,
    expert_ref,
    length_ref,
    slot_ref,
    tokens_ref,
    gain_one_ref,
    query_weight_ref,
    key_weight_ref,
    value_weight_ref,
    out_weight_ref,
    bias_ref,
    gain_two_ref,
    *refs,
):
    probs_ref, qkv_ref, lefts_ref, inverse_ref, resid_ref = refs[:5]
    send_refs = refs[5:-3]
    qkv_s, mixed_s, line_s = refs[-3:]
    pair = pl.program_id(0)
    pairs = pl.num_programs(0)
    seq_len, width = tokens_ref.shape
    tiles = seq_len // TILE

    @pl.when(pair == 0)
    def _():
        buckets = bias_ref.shape[1]
        place = iota((buckets, LINE), 1)
        offset = jnp.where(place < 3 * TILE, place - TILE, place - TILE - LINE)
        chosen = bucket_of(offset, buckets, MAXDIST) == iota((buckets, LINE), 0)
        lines = dot(bias_ref[...], jnp.where(chosen, 1.0, 0.0).astype(BF))
        for number in range(width // LANES):
            line_s[number, 0:2, :] = lines[2 * number : 2 * number + 2]
        rows = tokens_ref[...].astype(F32)
        normed = (rows * inverse_rms(rows) * gain_one_ref[...].astype(F32).reshape(1, width)).astype(BF)
        lefts_ref[0] = normed
        for part, weight_ref in enumerate((query_weight_ref, key_weight_ref, value_weight_ref)):
            values = dot(normed, weight_ref[...])
            for number in range(width // LANES):
                block = values[:, number * LANES : (number + 1) * LANES].astype(BF)
                if part == 0:
                    block = block * BF(HALF ** (-0.5))
                qkv_s[part, number] = block

    query = qkv_s[0, pair]
    key = qkv_s[1, pair]
    value = qkv_s[2, pair]
    qkv_ref[0, 0] = query
    qkv_ref[1, 0] = key
    qkv_ref[2, 0] = value
    lane = iota((seq_len, LANES), 1)
    row = iota((seq_len, LANES), 0)
    row_tile = row // TILE
    value_wide = jnp.concatenate([value, jnp.ones((seq_len, LANES), BF)], axis=1)
    query_wides, key_wides, nears = [], [], []
    for half in range(2):
        own = lane < HALF if half == 0 else lane >= HALF
        extra = lane - HALF if half == 0 else lane
        query_wides.append(
            jnp.where(
                own,
                query.astype(F32),
                jnp.where((extra == 0) | (extra == 1 + row_tile), 1.0, 0.0),
            ).astype(BF)
        )
        query_tile = extra - 1
        line = jnp.broadcast_to(line_s[pair, half : half + 1, :], (TILE, LINE))
        far = jnp.where(
            row_tile <= query_tile - 2,
            line[0:1, 0:1],
            jnp.where(row_tile >= query_tile + 2, line[0:1, 3 * TILE - 1 : 3 * TILE], 0.0),
        )
        far = jnp.where((query_tile >= 0) & (query_tile < tiles), far, 0.0)
        far = jnp.where((extra == 0) & (row >= length_ref[0]), NEGATIVE, far)
        key_wides.append(jnp.where(own, key.astype(F32), far).astype(BF))
        nears.append(pltpu.roll(line, 0, 1, stride=1, stride_axis=0)[:, : 3 * TILE])
    first = lane[:TILE] < HALF
    for tile in range(tiles):
        part = slice(tile * TILE, (tile + 1) * TILE)
        low = max(tile - 1, 0)
        high = min(tile + 2, tiles)
        outs = []
        for half in range(2):
            scores = dot(query_wides[half][part], key_wides[half], 1, 1)
            middle = nears[half][:, (low - tile + 1) * TILE : (high - tile + 1) * TILE]
            pieces = [scores[:, low * TILE : high * TILE] + middle]
            if low > 0:
                pieces.insert(0, scores[:, : low * TILE])
            if high < tiles:
                pieces.append(scores[:, high * TILE :])
            scores = jnp.concatenate(pieces, axis=1)
            peak = jnp.max(scores, axis=-1, keepdims=True)
            raised = jnp.exp(scores - peak).astype(BF)
            probs_ref[half, part, :] = raised
            outs.append(dot(raised, value_wide))
        inverse_total = 1.0 / jnp.where(first, outs[0][:, LANES:], outs[1][:, LANES:])
        mixed = jnp.where(first, outs[0][:, :LANES], outs[1][:, :LANES]) * inverse_total
        mixed_s[pair, part, :] = mixed.astype(BF)
        inverse_ref[0, part, :] = inverse_total

    @pl.when(pair == pairs - 1)
    def _():
        mixed_all = jnp.concatenate([mixed_s[number] for number in range(width // LANES)], axis=1)
        lefts_ref[1] = mixed_all
        resid = tokens_ref[...].astype(F32) + dot(mixed_all, out_weight_ref[...])
        resid_ref[...] = resid
        normed = (resid * inverse_rms(resid) * gain_two_ref[...].astype(F32).reshape(1, width)).astype(BF)
        send_rows(expert_ref, slot_ref[...], normed, plan, send_refs)


def forward_part(expert, lengths, slot, tokens, gain_one, weights, bias, gain_two, plan):
    seq_len, width = tokens.shape
    pairs = width // LANES
    square = whole((width, width))
    return pl.pallas_call(
        functools.partial(forward_kernel, plan),
        grid=(pairs,),
        out_shape=[
            shape_of((2 * pairs, seq_len, seq_len), BF),
            shape_of((3, pairs, seq_len, LANES), BF),
            shape_of((2, seq_len, width), BF),
            shape_of((pairs, seq_len, LANES), F32),
            shape_of((seq_len, width), F32),
        ]
        + [shape_of((rows, width), BF) for rows in plan.arrays],
        in_specs=[
            smem(),
            smem(),
            whole((1, seq_len)),
            whole((seq_len, width)),
            whole((width,)),
            square,
            square,
            square,
            square,
            whole(bias.shape),
            whole((width,)),
        ],
        out_specs=[
            pl.BlockSpec((2, seq_len, seq_len), lambda p: (p, 0, 0)),
            pl.BlockSpec((3, 1, seq_len, LANES), lambda p: (0, p, 0, 0)),
            whole((2, seq_len, width)),
            pl.BlockSpec((1, seq_len, LANES), lambda p: (p, 0, 0)),
            whole((seq_len, width)),
        ]
        + [whole((rows, width)) for rows in plan.arrays],
        scratch_shapes=[
            pltpu.VMEM((3, pairs, seq_len, LANES), BF),
            pltpu.VMEM((pairs, seq_len, LANES), BF),
            pltpu.VMEM((pairs, 8, LINE), F32),
        ],
        compiler_params=params(58),
        name="attention_forward",
    )(expert, lengths, slot, tokens, gain_one, *weights, bias, gain_two)


def expert_up_kernel(plan, out_ref, *refs):
    up_refs = refs[:-2]
    up_ref, act_grad_ref = refs[-2:]

    @pl.when(pl.program_id(0) == 0)
    def _():
        for number, ref in enumerate(plan.by_distance(up_refs)):
            rows = plan.block_rows
            up_ref[number * rows : (number + 1) * rows, :] = ref[...]

    act_grad_ref[...] = dot(up_ref[...], out_ref[0], 1, 1).astype(BF)


def expert_up_part(up_arrays, expert_out, plan):
    width = expert_out.shape[2]
    hidden = expert_out.shape[1]
    rows = sum(plan.arrays)
    tile = 512
    return pl.pallas_call(
        functools.partial(expert_up_kernel, plan),
        grid=(hidden // tile,),
        out_shape=[shape_of((rows, width), BF), shape_of((rows, hidden), BF)],
        in_specs=[pl.BlockSpec((1, tile, width), lambda f: (0, f, 0))]
        + plan.specs(up_arrays),
        out_specs=[whole((rows, width)), pl.BlockSpec((rows, tile), lambda f: (0, f))],
        compiler_params=params(28),
        name="expert_activation_gradient",
    )(expert_out, *up_arrays)


def expert_kernel(plan, expert_ref, up_ref, act_grad_ref, in_ref, router_ref, *refs):
    count = len(plan.arrays)
    row_refs = refs[: -(7 + count)]
    act_ref, slope_ref, scaled_ref, rows_grad_ref, gate_ref, logit_grad_ref = refs[
        -(7 + count) : -(1 + count)
    ]
    back_refs, rows_ref = refs[-(1 + count) : -1], refs[-1]
    block_rows = plan.block_rows
    step = pl.program_id(0)
    steps = len(plan.arrays)
    rows, hidden = act_ref.shape
    experts = router_ref.shape[0]
    blocks = plan.by_distance(row_refs)
    for number in range(steps):

        @pl.when(step == number)
        def _(number=number):
            each = len(blocks) // steps
            for place in range(each):
                rows_ref[place * block_rows : (place + 1) * block_rows, :] = blocks[
                    number * each + place
                ][...]

    own = iota((rows, experts), 1) == expert_ref[0]
    logits = dot(rows_ref[...], router_ref[...], 1, 1)
    raised = jnp.exp(logits - jnp.max(logits, axis=-1, keepdims=True))
    probs = raised / jnp.sum(raised, axis=-1, keepdims=True)
    gate = jnp.sum(jnp.where(own, probs, 0.0), axis=-1, keepdims=True)
    gate_ref[...] = gate
    rows_grad_ref[...] = (up_ref[...].astype(F32) * gate).astype(BF)
    scaled_ref[...] = (rows_ref[...].astype(F32) * gate).astype(BF)
    gate_grad = jnp.zeros((rows, LANES), F32)
    tile = 512
    for first in range(0, hidden, tile):
        part = slice(first, first + tile)
        pre = dot(rows_ref[...], in_ref[0, :, part])
        act_grad = act_grad_ref[:, part]
        square = pre * pre
        level = 0.5 + 0.5 * jnp.tanh(pre * (GELU_ONE + GELU_ONE * GELU_CUBE * square))
        act = (pre * level).astype(BF)
        level = level.astype(BF)
        slope = level + act * (BF(1.0) - level) * (
            BF(2.0 * GELU_ONE) + BF(6.0 * GELU_ONE * GELU_CUBE) * square.astype(BF)
        )
        act_ref[:, part] = act
        product = (act * act_grad).astype(F32)
        for place in range(0, tile, LANES):
            gate_grad += product[:, place : place + LANES]
        slope_ref[:, part] = act_grad * slope
    gate_grad = jnp.sum(gate_grad, axis=-1, keepdims=True)
    logit_grad = gate_grad * (jnp.where(own, 1.0, 0.0) - probs)
    logit_grad_ref[...] = logit_grad.astype(BF)
    logit_grad = (gate * logit_grad).astype(BF)
    back = gate * dot(slope_ref[...], in_ref[0], 1, 1) + dot(logit_grad, router_ref[...])
    back = back.astype(BF)
    for number in range(steps):

        @pl.when(step == number)
        def _(number=number):
            back_refs[number][...] = back


def expert_part(expert, up_rows, act_grad, expert_in, router, row_arrays, plan):
    rows, width = up_rows.shape
    hidden = expert_in.shape[2]
    experts = router.shape[0]
    steps = len(plan.arrays)
    some = rows // steps
    return pl.pallas_call(
        functools.partial(expert_kernel, plan),
        grid=(steps,),
        out_shape=[
            shape_of((rows, hidden), BF),
            shape_of((rows, hidden), BF),
            shape_of((rows, width), BF),
            shape_of((rows, width), BF),
            shape_of((rows, 1), F32),
            shape_of((rows, experts), BF),
        ]
        + [shape_of((count, width), BF) for count in plan.arrays],
        in_specs=[
            smem(),
            by_rows(some, width),
            by_rows(some, hidden),
            whole((1, width, hidden)),
            whole((experts, width)),
        ]
        + plan.specs(row_arrays),
        out_specs=[by_rows(some, columns) for columns in (hidden, hidden, width, width, 1, experts)]
        + [whole((count, width)) for count in plan.arrays],
        scratch_shapes=[pltpu.VMEM((some, width), BF)],
        compiler_params=params(44),
        name="expert_rows",
    )(expert, up_rows, act_grad, expert_in, router, *row_arrays)


def later_sums_kernel(*refs):
    count = len(refs) // 3
    for keep_ref, there_ref, out_ref in zip(refs[:count], refs[count : 2 * count], refs[2 * count :]):
        out_ref[...] = (keep_ref[...].astype(F32) + there_ref[...].astype(F32)).astype(BF)


def later_sums(keeps, theres):
    count, rows, columns = keeps[0].shape
    later = count // 2
    some = rows // 4

    def block(first):
        return pl.BlockSpec((1, some, columns), lambda t, r: (first + t, r, 0))

    return pl.pallas_call(
        later_sums_kernel,
        grid=(later, 4),
        out_shape=[shape_of((later, rows, columns), BF)] * len(keeps),
        in_specs=[block(count - later)] * (2 * len(keeps)),
        out_specs=[block(0)] * len(keeps),
        compiler_params=params(58),
        name="later_sums",
    )(*keeps, *theres)


def weight_grad_kernel(transposed, count, *refs):
    _, wide_refs, rows_refs, out_refs = [refs[n * count : (n + 1) * count] for n in range(4)]
    for turned, wide_ref, rows_ref, out_ref in zip(transposed, wide_refs, rows_refs, out_refs):
        left_ref, right_ref = (wide_ref, rows_ref) if turned else (rows_ref, wide_ref)
        out_ref[0] = dot(left_ref[...], right_ref[...], 0, 0).astype(BF)


def weight_grad_part(parts, terms):
    tiles, wides, rows, transposed = zip(*terms)
    steps = tiles[0].shape[0]
    count, width = rows[0].shape
    tile = wides[0].shape[1] // parts
    shapes = [(tile, width) if turned else (width, tile) for turned in transposed]
    return pl.pallas_call(
        functools.partial(weight_grad_kernel, transposed, len(terms)),
        grid_spec=pltpu.PrefetchScalarGridSpec(
            num_scalar_prefetch=len(terms),
            grid=(steps,),
            in_specs=[
                pl.BlockSpec((count, tile), lambda s, *refs, number=number: (0, refs[number][s]))
                for number in range(len(terms))
            ]
            + [whole((count, width))] * len(terms),
            out_specs=[pl.BlockSpec((1,) + shape, lambda s, *_: (s, 0, 0)) for shape in shapes],
        ),
        out_shape=[shape_of((steps,) + shape, BF) for shape in shapes],
        compiler_params=params(SEND_LIMIT),
        name="expert_weight_gradients",
    )(*tiles, *wides, *rows)


def expert_out_kernel(act_ref, out_ref, gate_ref, *send_refs):
    rows = (dot(act_ref[...], out_ref[0]) * gate_ref[...]).astype(BF)
    for number, send_ref in enumerate(send_refs):

        @pl.when(pl.program_id(0) == number)
        def _(send_ref=send_ref):
            send_ref[...] = rows


def expert_out_part(act, expert_out, gate, plan):
    rows, hidden = act.shape
    width = expert_out.shape[2]
    steps = len(plan.arrays)
    return pl.pallas_call(
        expert_out_kernel,
        grid=(steps,),
        out_shape=[shape_of((count, width), BF) for count in plan.arrays],
        in_specs=[
            by_rows(rows // steps, hidden),
            whole((1, hidden, width)),
            by_rows(rows // steps, 1),
        ],
        out_specs=[whole((count, width)) for count in plan.arrays],
        compiler_params=params(32),
        name="expert_output",
    )(act, expert_out, gate)


ROW_STEPS = 2


def result_kernel(plan, expert_ref, length_ref, column_ref, resid_ref, *refs):
    total = resid_ref[...] + home_rows(expert_ref, column_ref[...], refs[:-1], plan)
    rows = total.shape[0]
    live = iota((rows, 1), 0) + pl.program_id(0) * rows < length_ref[0]
    refs[-1][...] = jnp.where(live, total, 0.0).astype(BF)


def result_part(expert, lengths, column, resid, arrays, plan):
    seq_len, width = resid.shape
    rows = seq_len // ROW_STEPS
    return pl.pallas_call(
        functools.partial(result_kernel, plan),
        grid=(ROW_STEPS,),
        out_shape=shape_of(resid.shape, BF),
        in_specs=[smem(), smem(), by_rows(rows, LANES), by_rows(rows, width)]
        + plan.specs(arrays),
        out_specs=by_rows(rows, width),
        compiler_params=params(58),
        name="result",
    )(expert, lengths, column, resid, *arrays)


def middle_kernel(
    plan,
    expert_ref,
    length_ref,
    column_ref,
    resid_ref,
    cotangent_ref,
    out_weight_ref,
    gain_ref,
    *refs,
):
    resid_grad_ref, mixed_grad_ref, attn_grad_ref, gain_grad_ref = refs[-4:]
    upstream = home_rows(expert_ref, column_ref[...], refs[:-4], plan)
    resid = resid_ref[...]
    rows = resid.shape[0]
    inverse = inverse_rms(resid)
    scaled = gain_ref[...].astype(F32).reshape(1, -1) * upstream
    add_rows(gain_grad_ref, jnp.sum(upstream * resid * inverse, axis=0, keepdims=True))
    live = iota((rows, 1), 0) + pl.program_id(0) * rows < length_ref[0]
    resid_grad = (
        jnp.where(live, cotangent_ref[...].astype(F32), 0.0)
        + inverse * scaled
        - resid * (inverse * inverse * inverse * jnp.mean(scaled * resid, axis=-1, keepdims=True))
    )
    resid_grad_ref[...] = resid_grad
    attn_grad = resid_grad.astype(BF)
    mixed_grad_ref[...] = dot(attn_grad, out_weight_ref[...], 1, 1).astype(BF)
    attn_grad_ref[...] = attn_grad


def middle_part(expert, lengths, column, resid, cotangent, out_weight, gain, arrays, plan):
    seq_len, width = resid.shape
    rows = seq_len // ROW_STEPS
    block = by_rows(rows, width)
    return pl.pallas_call(
        functools.partial(middle_kernel, plan),
        grid=(ROW_STEPS,),
        out_shape=[
            shape_of((seq_len, width), F32),
            shape_of((seq_len, width), BF),
            shape_of((seq_len, width), BF),
            shape_of((1, width), F32),
        ],
        in_specs=[smem(), smem(), by_rows(rows, LANES), block, block, whole((width, width)), whole((width,))]
        + plan.specs(arrays),
        out_specs=[block, block, block, whole((1, width))],
        compiler_params=params(58),
        name="expert_norm_backward",
    )(expert, lengths, column, resid, cotangent, out_weight, gain, *arrays)


def backward_kernel(
    core_ref,
    qkv_ref,
    probs_ref,
    lefts_ref,
    mixed_ref,
    grad_ref,
    attn_grad_ref,
    inverse_ref,
    back_ref,
    line_ref,
    *refs,
):
    own_refs, other_refs, score_s, lefts_s, backs_s = refs[:2], refs[2:4], *refs[4:]
    seq_len = grad_ref.shape[0]

    @pl.when(pl.program_id(0) == 0)
    def _():
        lefts_s[0] = lefts_ref[0].T
        lefts_s[1] = lefts_ref[1].T

    tiles = seq_len // TILE
    query = qkv_ref[0, 0]
    key = qkv_ref[1, 0]
    value = qkv_ref[2, 0]
    lane = iota((seq_len, LANES), 1)
    row_tile = iota((seq_len, LANES), 0) // TILE
    scaled = grad_ref[...].astype(F32) * inverse_ref[0]
    product = scaled * mixed_ref[0].astype(F32)
    scaled_low = scaled.astype(BF)
    key_wide = jnp.concatenate([key, jnp.where(lane == row_tile, 1.0, 0.0).astype(BF)], axis=1)
    backward_rows = jnp.where(iota((TILE, TILE), 0) + iota((TILE, TILE), 1) == TILE - 1, 1.0, 0.0)
    query_backs = []
    key_backs = []
    value_backs = []
    for half in range(2):
        own = lane < HALF if half == 0 else lane >= HALF
        extra = lane - HALF if half == 0 else lane
        delta = jnp.sum(jnp.where(own, product, 0.0), axis=-1, keepdims=True)
        high = delta.astype(BF).astype(F32)
        grad_wide = jnp.where(
            own, scaled, jnp.where(extra == 0, -high, jnp.where(extra == 1, high - delta, 0.0))
        ).astype(BF)
        value_wide = jnp.where(
            own, value.astype(F32), jnp.where((extra == 0) | (extra == 1), 1.0, 0.0)
        ).astype(BF)
        near = [jnp.zeros((TILE, TILE), F32) for _ in range(3)]
        for tile in range(tiles):
            part = slice(tile * TILE, (tile + 1) * TILE)
            prob_grad = dot(grad_wide[part], value_wide, 1, 1)
            score_grad = (probs_ref[half, part, :].astype(F32) * prob_grad).astype(BF)
            score_s[half, part, :] = score_grad
            for side in range(3):
                other = tile + side - 1
                if 0 <= other < tiles:
                    near[side] = near[side] + score_grad[
                        :, other * TILE : (other + 1) * TILE
                    ].astype(F32)
        query_wide = dot(score_s[half], key_wide)
        query_backs.append(query_wide[:, :LANES])
        sums = query_wide[:, LANES:]
        far_left = jnp.sum(jnp.where(lane <= row_tile - 2, sums, 0.0), axis=0, keepdims=True)
        far_right = jnp.sum(jnp.where(lane >= row_tile + 2, sums, 0.0), axis=0, keepdims=True)
        line_ref[0, half : half + 1, LINE : LINE + LANES] = far_left
        line_ref[0, half : half + 1, LINE + LANES :] = far_right
        key_backs.append(dot(query, score_s[half], 0, 0))
        value_backs.append(dot(scaled_low, probs_ref[half], 0, 0))
        spread = lax.dot_general(
            backward_rows,
            jnp.concatenate(near, axis=1),
            (((1,), (0,)), ((), ())),
            precision=lax.Precision.HIGHEST,
            preferred_element_type=F32,
        )
        spread = jnp.concatenate([spread, jnp.zeros((TILE, TILE), F32)], axis=1)
        spread = pltpu.roll(spread, 0, 1, stride=1, stride_axis=0)
        line_ref[0, half : half + 1, :LINE] = jnp.sum(spread, axis=0, keepdims=True)
    first = lane < HALF
    backs = [(jnp.where(first, query_backs[0], query_backs[1]) * HALF ** (-0.5)).astype(BF)]
    for halves in (key_backs, value_backs):
        joined = jnp.concatenate([halves[0][:HALF], halves[1][HALF:]], axis=0)
        backs.append(joined.T.astype(BF))
    backs.append(attn_grad_ref[...])
    for place, values in enumerate(backs):
        if place < 3:
            back_ref[place] = values

    @pl.when(pl.program_id(0) % 2 == 0)
    def _():
        for place, values in enumerate(backs):
            backs_s[place] = values

    @pl.when(pl.program_id(0) % 2 == 1)
    def _():
        wides = [jnp.concatenate([backs_s[n], values], axis=1) for n, values in enumerate(backs)]
        grads = [dot(lefts_s[n // 3], wide).astype(BF) for n, wide in enumerate(wides)]
        for core in range(2):

            @pl.when(core_ref[0] == core)
            def _(core=core):
                for target_refs, place in ((own_refs, core), (other_refs, 1 - core)):
                    target_refs[0][...] = grads[place]
                    target_refs[1][...] = grads[2 + place]


def backward_part(core, qkv, probs, lefts, mixed_grad, attn_grad, inverse):
    _, seq_len, width = lefts.shape
    pairs = width // LANES
    assert pairs % 2 == 0
    column = pl.BlockSpec((seq_len, LANES), lambda p: (0, p))
    grad = pl.BlockSpec((width, 2 * LANES), lambda p: (0, p // 2))
    return pl.pallas_call(
        backward_kernel,
        grid=(pairs,),
        out_shape=[
            shape_of((3, seq_len, width), BF),
            shape_of((pairs, 2, LINE + 2 * LANES), F32),
        ]
        + [shape_of((width, width), BF)] * 4,
        in_specs=[
            smem(),
            pl.BlockSpec((3, 1, seq_len, LANES), lambda p: (0, p, 0, 0)),
            pl.BlockSpec((2, seq_len, seq_len), lambda p: (p, 0, 0)),
            whole(lefts.shape),
            pl.BlockSpec((1, seq_len, LANES), lambda p: (1, 0, p)),
            column,
            column,
            pl.BlockSpec((1, seq_len, LANES), lambda p: (p, 0, 0)),
        ],
        out_specs=[
            pl.BlockSpec((3, seq_len, LANES), lambda p: (0, 0, p)),
            pl.BlockSpec((1, 2, LINE + 2 * LANES), lambda p: (p, 0, 0)),
        ]
        + [grad] * 4,
        scratch_shapes=[
            pltpu.VMEM((2, seq_len, seq_len), BF),
            pltpu.VMEM((2, width, seq_len), BF),
            pltpu.VMEM((4, seq_len, LANES), BF),
        ],
        compiler_params=params(58),
        name="attention_backward",
    )(core, qkv, probs, lefts, lefts, mixed_grad, attn_grad, inverse)


def extra_kernel(router_ref, gain_ref, line_ref, out_ref):
    experts, width = router_ref.shape
    heads, places = line_ref.shape
    place = iota((places, width), 0)
    bucket = iota((places, width), 1)
    own = bucket_of(place - (2 * TILE - 1), BUCKETS, MAXDIST)
    own = jnp.where(place >= LINE, BUCKETS // 2 - 1, own)
    own = jnp.where(place >= LINE + LANES, BUCKETS - 1, own)
    sums = lax.dot_general(
        line_ref[...],
        jnp.where(own == bucket, 1.0, 0.0),
        (((1,), (0,)), ((), ())),
        precision=lax.Precision.HIGHEST,
        preferred_element_type=F32,
    )
    rows = [
        router_ref[...],
        jnp.broadcast_to(gain_ref[...], (8, width)),
        sums,
        jnp.zeros((out_ref.shape[0] - experts - 8 - heads, width), F32),
    ]
    out_ref[...] = jnp.concatenate(rows, axis=0).astype(BF)


def extra_part(router_grad, gain_grad, lines):
    experts, width = router_grad.shape
    rows = -(-(experts + 8 + lines.shape[0]) // 16) * 16
    return pl.pallas_call(
        extra_kernel,
        out_shape=shape_of((rows, width), BF),
        compiler_params=params(58),
        name="extra_rows",
    )(router_grad, gain_grad, lines)


def token_grad_kernel(
    back_ref,
    query_weight_ref,
    key_weight_ref,
    value_weight_ref,
    tokens_ref,
    gain_ref,
    resid_grad_ref,
    out_ref,
):
    upstream = None
    for part, weight_ref in enumerate((query_weight_ref, key_weight_ref, value_weight_ref)):
        term = dot(back_ref[part], weight_ref[...], 1, 1)
        upstream = term if upstream is None else upstream + term
    rows = tokens_ref[...].astype(F32)
    inverse = inverse_rms(rows)
    scaled = gain_ref[...].astype(F32).reshape(1, -1) * upstream
    out_ref[...] = (
        resid_grad_ref[...]
        + inverse * scaled
        - rows * (inverse * inverse * inverse * jnp.mean(scaled * rows, axis=-1, keepdims=True))
    )


def token_grad_part(back, weights, tokens, gain, resid_grad):
    seq_len, width = tokens.shape
    rows = seq_len // ROW_STEPS
    block = by_rows(rows, width)
    return pl.pallas_call(
        token_grad_kernel,
        grid=(ROW_STEPS,),
        out_shape=shape_of((seq_len, width), F32),
        in_specs=[pl.BlockSpec((3, rows, width), lambda step: (0, step, 0))]
        + [whole((width, width))] * 3
        + [block, whole((width,)), block],
        out_specs=block,
        compiler_params=params(58),
        name="token_gradient",
    )(back, *weights, tokens, gain, resid_grad)


def swap(values, axis, size, distance):
    return lax.ppermute(values, axis, [(place, place ^ distance) for place in range(size)])


def after(values, *others):
    return lax.optimization_barrier((values, *others))[0]


class Plan:
    def __init__(self, size, capacity, experts):
        self.size = size
        self.capacity = capacity
        self.paired = size == 8 and capacity % 16 == 0
        if self.paired:
            self.block_rows = capacity
            self.blocks = size
            self.arrays = [2 * capacity] * (size // 2)
        else:
            self.block_rows = experts * capacity
            self.blocks = 1
            self.arrays = [experts * capacity]

    def turn(self, rows):
        parts = rows.reshape(self.size, self.capacity, rows.shape[1])
        parts = lax.all_to_all(parts, "expert", split_axis=0, concat_axis=0, tiled=True)
        return parts.reshape(rows.shape)

    def cross(self, arrays):
        if not self.paired:
            return [self.turn(array) for array in arrays]
        return [
            array if k == 0 else swap(array, "expert", self.size, 2 * k)
            for k, array in enumerate(arrays)
        ]

    def finish(self, arrays):
        if not self.paired:
            return arrays
        return [*arrays, *[swap(array, "expert", self.size, 1) for array in arrays]]

    def specs(self, arrays):
        if not self.paired:
            return [whole(array.shape) for array in arrays]
        return [
            pl.BlockSpec((self.block_rows, array.shape[1]), lambda *_, n=n: (2 * n // len(arrays), 0))
            for n, array in enumerate(arrays)
        ]

    def by_distance(self, refs):
        half = len(refs) // 2
        return [ref for pair in zip(refs[:half], refs[half:]) for ref in pair] if self.paired else refs


def stages_of(dp_size, expert_size):
    stages = [("expert", expert_size, (1,))]
    bits = [1 << n for n in range(dp_size.bit_length() - 1)]
    stages += [("dp", dp_size, tuple(bits[n : n + 2])) for n in range(0, len(bits), 2)]
    bits = [1 << n for n in range(1, expert_size.bit_length() - 1)]
    return stages + [("expert", expert_size, tuple(bits[n : n + 2])) for n in range(0, len(bits), 2)]


def distances_of(bits):
    return [sum(bit for n, bit in enumerate(bits) if (k >> n) & 1) for k in range(1 << len(bits))]


def place_of(stage):
    axis, _, bits = stage
    index = lax.axis_index(axis)
    return sum(((index // bit) % 2) << n for n, bit in enumerate(bits))


def share_kernel(inputs, extra, apart, place_ref, *refs):
    in_refs, out_refs = refs[:inputs], refs[inputs:]
    extra_refs, out_refs = out_refs[: len(out_refs) - apart], out_refs[len(out_refs) - apart :]
    last = in_refs[0].shape[0] - (0 if extra_refs else extra)
    count = 1 if place_ref is None else len(out_refs)
    rows = last // count
    for number in range(count):
        start = 0 if count == 1 else pl.multiple_of((place_ref[0] ^ number) * rows, rows)
        total = sum(ref[pl.ds(start, rows), :].astype(F32) for ref in in_refs)
        out_refs[number][:rows, :] = total.astype(BF)
    if extra:
        if extra_refs:
            total = sum(ref[...].astype(F32) for ref in extra_refs).astype(BF)
        else:
            total = sum(ref[last:, :].astype(F32) for ref in in_refs).astype(BF)
        if count > 1:
            for out_ref in out_refs:
                out_ref[rows:, :] = total
        else:
            out_refs[-1][...] = total


def share(parts, stage, extra, extras=()):
    count = 1 if stage is None else 1 << len(stage[2])
    place = None if stage is None else place_of(stage)
    if parts[0].shape[0] // count % 16 and extras:
        parts = [jnp.concatenate(pair, axis=0) for pair in zip(parts, extras)]
        extras = ()
    last, width = parts[0].shape[0] - (0 if extras else extra), parts[0].shape[1]
    rows = last // count
    shapes = [(rows + extra, width)] * count if count > 1 else [(rows, width)]
    if count == 1 and extra:
        shapes.append((extra, width))
    if rows % 16:
        total = sum(part.astype(F32) for part in parts).astype(BF)
        if stage is None:
            return [total[:last], total[last:]] if extra else [total]
        return [
            jnp.concatenate(
                [lax.dynamic_slice_in_dim(total, (place ^ number) * rows, rows, 0), total[last:]], axis=0
            )
            for number in range(count)
        ]
    kernel = functools.partial(share_kernel, len(parts), extra, len(shapes))
    if stage is None:
        kernel = functools.partial(kernel, None)
    return pl.pallas_call(
        kernel,
        out_shape=[shape_of(shape, BF) for shape in shapes],
        in_specs=[smem()] * (stage is not None) + [pl.BlockSpec()] * (len(parts) + len(extras)),
        compiler_params=params(58),
        name="share",
    )(*([] if stage is None else [place.reshape(1)]), *parts, *extras)


def scatter(parts, stage):
    axis, size, bits = stage
    return [
        part if distance == 0 else swap(part, axis, size, distance)
        for part, distance in zip(parts, distances_of(bits))
    ]


def gather(values, stage):
    axis, size, bits = stage
    return [
        values if distance == 0 else swap(values, axis, size, distance)
        for distance in distances_of(bits)
    ]


def join_kernel(place_ref, *refs):
    out_ref = refs[-1]
    for number, ref in enumerate(refs[:-1]):
        rows = ref.shape[0]
        part = pl.ds(pl.multiple_of((place_ref[0] ^ number) * rows, rows), rows)
        out_ref[part, :] = ref[...]


def join(parts, stage):
    place = place_of(stage)
    rows, width = parts[0].shape
    if rows % 16:
        joined = jnp.zeros((rows * len(parts), width), BF)
        for number, part in enumerate(parts):
            joined = lax.dynamic_update_slice_in_dim(joined, part, (place ^ number) * rows, 0)
        return joined
    return pl.pallas_call(
        join_kernel,
        out_shape=shape_of((rows * len(parts), width), BF),
        in_specs=[smem()] + [pl.BlockSpec()] * len(parts),
        compiler_params=params(58),
        name="join",
    )(place.reshape(1), *parts)


def assemble_kernel(count, places_ref, *refs):
    own_refs, other_refs = refs[:count], refs[count : 2 * count]
    weight_refs, out_refs, gain_ref = refs[2 * count : -3], refs[-3:-1], refs[-1]
    source = places_ref[1] ^ pl.program_id(0)
    for number in range(count):
        for core in range(2):

            @pl.when((source == number) & (places_ref[0] == core))
            def _(number=number, core=core):
                out_refs[core][...] = own_refs[number][...].astype(F32)
                out_refs[1 - core][...] = other_refs[number][...].astype(F32)

    total = sum(
        jnp.sum(out_ref[...] * weight_ref[...].astype(F32), axis=1, keepdims=True)
        for out_ref, weight_ref in zip(out_refs, weight_refs)
    )
    gain_ref[...] = jnp.broadcast_to(total, gain_ref.shape)


def assemble(own, other, stages, weights):
    rows, width = own[0].shape
    count = len(own)
    block = by_rows(rows, width)
    places = jnp.stack([place_of(stage) for stage in stages])
    return pl.pallas_call(
        functools.partial(assemble_kernel, count),
        grid=(count,),
        out_shape=[shape_of((count * rows, width), F32)] * 2 + [shape_of((count * rows, LANES), F32)],
        in_specs=[smem()] + [whole((rows, width))] * (2 * count) + [block] * len(weights),
        out_specs=[block, block, by_rows(rows, LANES)],
        compiler_params=params(58),
        name="assemble",
    )(places, *own, *other, *weights)


def halving_order(bits):
    if not bits:
        return [0]
    rest = halving_order(bits[1:])
    return rest + [distance | bits[0] for distance in rest]


def on_device(
    dp_size,
    expert_size,
    tokens,
    cotangent,
    lengths,
    routes,
    norm_gain,
    query_weight,
    key_weight,
    value_weight,
    output_weight,
    bucket_head_bias,
    ffn_gain,
    router_weight,
    expert_in,
    expert_out,
):
    seq_count, seq_len, width = tokens.shape
    buckets, heads = bucket_head_bias.shape
    assert seq_count == 1 and buckets == BUCKETS
    experts = router_weight.shape[1]
    capacity = max(2, 5 * seq_len // (4 * experts))
    plan = Plan(expert_size, capacity, experts)
    expert = lax.axis_index("expert").reshape(1)
    group = lax.axis_index("dp")
    rows_in = tokens.reshape(seq_len, width)
    upstream = cotangent.reshape(seq_len, width)
    weights = (query_weight, key_weight, value_weight)

    slot, column, *up_send = slots_part(expert, lengths, routes, upstream, capacity, experts, plan)
    up_there = plan.cross(up_send)
    probs, qkv, lefts, inverse_total, resid, *row_send = forward_part(
        expert,
        lengths,
        slot,
        rows_in,
        norm_gain,
        (*weights, output_weight),
        bucket_head_bias.T,
        ffn_gain,
        plan,
    )
    row_send, up_there = lax.optimization_barrier((row_send, up_there))
    row_there = plan.cross(row_send)
    up_rows, act_grad = expert_up_part(plan.finish(up_there), expert_out, plan)
    row_there = lax.optimization_barrier((row_there, act_grad))[0]
    act, slope, scaled_rows, rows_grad, gate, logit_grad, *back_send = expert_part(
        expert, up_rows, act_grad, expert_in, router_weight.T, plan.finish(row_there), plan
    )
    router_grad = dot(logit_grad, scaled_rows, 0, 0)
    back_there = plan.cross(back_send)

    bits = [1 << n for n in range(dp_size.bit_length() - 1)]
    half = dp_size // 2
    orders = (bits, bits[::-1])
    tiles = [group ^ jnp.array(halving_order(order), jnp.int32) for order in orders]
    grad_terms = [(act, rows_grad, True), (slope, scaled_rows, False)]
    sends = [
        weight_grad_part(dp_size, [(tile[half:], *term)])[0] for tile, term in zip(tiles, grad_terms)
    ]
    arrived = [swap(send, "dp", dp_size, order[0]) for send, order in zip(sends, orders)]
    keeps = weight_grad_part(
        dp_size, [(tile[:half], *term) for tile, term in zip(tiles, grad_terms)]
    )
    result_send = expert_out_part(act, expert_out, gate, plan)
    back_there = lax.optimization_barrier((back_there, keeps, result_send))[0]
    back_arrays = plan.finish(back_there)

    resid_grad, mixed_grad, attn_grad, ffn_gain_grad = middle_part(
        expert, lengths, column, after(resid, *keeps), upstream, output_weight, ffn_gain, back_arrays, plan
    )
    result_send = lax.optimization_barrier((result_send, back_there))[0]
    result_there = plan.cross(result_send)

    arrived = lax.optimization_barrier((arrived, back_arrays))[0]
    seconds = later_sums(keeps, arrived)
    rests = [list(order[1:]) for order in orders]
    arrived_seconds = [
        swap(send, "dp", dp_size, rest[0]) if rest else None for send, rest in zip(seconds, rests)
    ]
    mixed_grad = after(mixed_grad, *seconds)

    stages = stages_of(dp_size, expert_size)
    core = place_of(stages[0])
    back, lines, *grads = backward_part(
        core.reshape(1), qkv, probs, lefts, mixed_grad, attn_grad, inverse_total
    )
    kept, sent = grads[:2], grads[2:]
    back, sent, result_there, arrived_seconds = lax.optimization_barrier(
        (back, sent, result_there, arrived_seconds)
    )

    there = [swap(values, *stages[0][:2], 1) for values in sent]
    extra = extra_part(router_grad, ffn_gain_grad, lines.reshape(heads, -1))
    extra_rows = [0, extra.shape[0]]
    extras = [(), (extra, swap(extra, *stages[0][:2], 1))]
    shares = []
    for values, other, rows, more in zip(kept, there, extra_rows, extras):
        parts = [values, other]
        if shares:
            parts = after(parts, shares[0])
        shares.append(share(parts, stages[1], rows, more))
    moved = [scatter(parts, stages[1]) for parts in shares]
    token_grad = token_grad_part(after(back, *shares[1]), weights, rows_in, norm_gain, resid_grad)
    moved[0], token_grad, result_there = lax.optimization_barrier(
        (moved[0], token_grad, result_there)
    )
    result_arrays = plan.finish(result_there)
    for stage in stages[2:]:
        shares = [share(parts, stage, rows) for parts, rows in zip(moved, extra_rows)]
        moved = [scatter(parts, stage) for parts in shares]
    chunks = [share(parts, None, rows) for parts, rows in zip(moved, extra_rows)]
    extra = chunks[1][1].astype(F32)
    chunks = [chunk[0] for chunk in chunks]
    for stage in stages[:1:-1]:
        chunks = [join(gather(values, stage), stage) for values in chunks]
    there = [gather(values, stages[1]) for values in chunks]
    keeps, arrived, arrived_seconds, resid = lax.optimization_barrier(
        (keeps, arrived, arrived_seconds, resid, chunks)
    )[:4]
    result = result_part(expert, lengths, column, resid, result_arrays, plan)
    weight_sums = []
    for rest, keep, term, second in zip(rests, keeps, arrived, arrived_seconds):
        total = keep[: half // 2].astype(F32) + term[: half // 2].astype(F32)
        if rest:
            total = total + second.astype(F32)
        weight_sums.append(total)
    last = [pieces.pop() for pieces in there]
    over = [[swap(piece, *stages[0][:2], 1) for piece in pieces] for pieces in there]
    last, weight_sums, result = lax.optimization_barrier((last, weight_sums, result))
    for pieces, others, piece in zip(there, over, last):
        pieces.append(piece)
        others.append(swap(piece, *stages[0][:2], 1))
    expert_out_grad, expert_in_grad = weight_sums
    (query_grad, key_grad, gain_sum), (value_grad, output_grad, value_sum) = [
        assemble(own, other, stages[:2], some)
        for own, other, some in zip(there, over, ((query_weight, key_weight), (value_weight,)))
    ]
    norm_gain_grad = (gain_sum + value_sum)[:, 0] / norm_gain.astype(F32)

    return (
        result.reshape(tokens.shape),
        token_grad.reshape(tokens.shape),
        norm_gain_grad,
        query_grad,
        key_grad,
        value_grad,
        output_grad,
        extra[experts + 8 : experts + 8 + heads, :buckets].T,
        extra[experts],
        extra[:experts].T,
        expert_in_grad,
        expert_out_grad,
    )


def solution(mesh):
    in_specs = (
        P(("dp", "expert"), None, None),
        P(("dp", "expert"), None, None),
        P(("dp", "expert")),
        P(("dp", "expert"), None),
        P(),
        P(),
        P(),
        P(),
        P(),
        P(),
        P(),
        P(),
        P("expert", None, None),
        P("expert", None, None),
    )
    out_specs = (
        P(("dp", "expert"), None, None),
        P(("dp", "expert"), None, None),
        P(),
        P(),
        P(),
        P(),
        P(),
        P(),
        P(),
        P(),
        P("expert", None, "dp"),
        P("expert", "dp", None),
    )
    return jax.shard_map(
        functools.partial(on_device, mesh.shape["dp"], mesh.shape["expert"]),
        mesh=mesh,
        in_specs=in_specs,
        out_specs=out_specs,
        check_vma=False,
    )
```

```python
import functools
import math

import jax
import jax.numpy as jnp
from jax import lax
from jax.experimental import pallas as pl
from jax.experimental.pallas import tpu as pltpu
from jax.sharding import PartitionSpec as P

BF = jnp.bfloat16
F32 = jnp.float32
MAXDIST = 128
EPSILON = 1e-06
NEGATIVE = -1000000000.0
TILE = 128
BUCKETS = 32
LANES = 128
HALF = 64
LINE = 4 * TILE
GELU_ONE = math.sqrt(2.0 / math.pi)
GELU_CUBE = 0.044715
SEND_LIMIT = 32


def dot(left, right, left_dim=1, right_dim=0):
    return lax.dot_general(
        left, right, (((left_dim,), (right_dim,)), ((), ())), preferred_element_type=F32
    )


def iota(shape, dim):
    return lax.broadcasted_iota(jnp.int32, shape, dim)


def bucket_of(offset, buckets, far_limit):
    exact_limit = buckets // 4
    half_count = buckets // 2
    distance = jnp.abs(offset)
    bucket_ids = jnp.minimum(distance, exact_limit)
    for bucket_level in range(exact_limit + 1, half_count):
        border = math.ceil(
            exact_limit
            * (far_limit / exact_limit)
            ** ((bucket_level - exact_limit) / (half_count - exact_limit))
        )
        bucket_ids = bucket_ids + (distance >= border).astype(jnp.int32)
    return bucket_ids + jnp.where(offset > 0, half_count, 0).astype(jnp.int32)


def whole(shape):
    return pl.BlockSpec(shape, lambda *_: (0,) * len(shape))


def by_rows(rows, columns):
    return pl.BlockSpec((rows, columns), lambda step: (step, 0))


def add_rows(ref, values):
    @pl.when(pl.program_id(0) == 0)
    def _():
        ref[...] = values

    @pl.when(pl.program_id(0) > 0)
    def _():
        ref[...] += values


def smem():
    return pl.BlockSpec(memory_space=pltpu.SMEM)


def params(mebibytes):
    return pltpu.CompilerParams(vmem_limit_bytes=mebibytes * 1024 * 1024)


def shape_of(shape, dtype):
    return jax.ShapeDtypeStruct(shape, dtype)


def inverse_rms(rows):
    return lax.rsqrt(jnp.mean(rows * rows, axis=-1, keepdims=True) + EPSILON)


def send_rows(expert_ref, slot_row, rows, plan, send_refs):
    block_rows = plan.block_rows
    size = plan.blocks * block_rows
    place = iota((size, 1), 0)
    wanted = place
    if plan.paired:
        for distance in range(plan.blocks):
            first = distance * block_rows
            wanted = jnp.where(
                place >= first, place - first + (expert_ref[0] ^ distance) * block_rows, wanted
            )
    chosen = jnp.where(wanted == slot_row, 1.0, 0.0).astype(BF)
    sent = dot(chosen, rows).astype(BF)
    first = 0
    for send_ref in send_refs:
        send_ref[...] = sent[first : first + send_ref.shape[0]]
        first += send_ref.shape[0]


def home_rows(expert_ref, column, refs, plan):
    block_rows = plan.block_rows
    rows = jnp.concatenate([ref[...] for ref in plan.by_distance(refs)], axis=0)
    place = iota((1, rows.shape[0]), 1)
    wanted = place
    for distance in range(plan.blocks):
        first = distance * block_rows
        base = (expert_ref[0] ^ distance) * block_rows if plan.paired else 0
        wanted = jnp.where(place >= first, place - first + base, wanted)
    chosen = jnp.where(column[:, :1] == wanted, 1.0, 0.0).astype(BF)
    return dot(chosen, rows)


def slots_kernel(
    capacity, experts, plan, expert_ref, length_ref, routes_ref, cotangent_ref, slot_ref, column_ref, *send_refs
):
    seq_len = routes_ref.shape[1]
    routes = routes_ref[...]
    live = iota((1, seq_len), 1) < length_ref[0]
    onehot = jnp.where((iota((experts, seq_len), 0) == routes) & live, 1.0, 0.0)
    earlier = jnp.where(iota((seq_len, seq_len), 0) < iota((seq_len, seq_len), 1), 1.0, 0.0)
    before = dot(onehot.astype(BF), earlier.astype(BF))
    rank = jnp.sum(before * onehot, axis=0, keepdims=True).astype(jnp.int32)
    slot = jnp.where(live & (rank < capacity), routes * capacity + rank, -1)
    slot_ref[...] = slot
    wide = jnp.broadcast_to(slot.astype(F32), (LANES, seq_len))
    column_ref[...] = wide.T.astype(jnp.int32)
    send_rows(expert_ref, slot, cotangent_ref[...], plan, send_refs)


def slots_part(expert, lengths, routes, cotangent, capacity, experts, plan):
    seq_len, width = cotangent.shape
    return pl.pallas_call(
        functools.partial(slots_kernel, capacity, experts, plan),
        out_shape=[shape_of((1, seq_len), jnp.int32), shape_of((seq_len, LANES), jnp.int32)]
        + [shape_of((rows, width), BF) for rows in plan.arrays],
        in_specs=[smem(), smem(), pl.BlockSpec(), pl.BlockSpec()],
        compiler_params=params(58),
        name="slots",
    )(expert, lengths, routes, cotangent)


def forward_kernel(
    plan,
    expert_ref,
    length_ref,
    slot_ref,
    tokens_ref,
    gain_one_ref,
    query_weight_ref,
    key_weight_ref,
    value_weight_ref,
    out_weight_ref,
    bias_ref,
    gain_two_ref,
    *refs,
):
    probs_ref, qkv_ref, lefts_ref, inverse_ref, resid_ref = refs[:5]
    send_refs = refs[5:-3]
    qkv_s, mixed_s, line_s = refs[-3:]
    pair = pl.program_id(0)
    pairs = pl.num_programs(0)
    seq_len, width = tokens_ref.shape
    tiles = seq_len // TILE

    @pl.when(pair == 0)
    def _():
        buckets = bias_ref.shape[1]
        place = iota((buckets, LINE), 1)
        offset = jnp.where(place < 3 * TILE, place - TILE, place - TILE - LINE)
        chosen = bucket_of(offset, buckets, MAXDIST) == iota((buckets, LINE), 0)
        lines = dot(bias_ref[...], jnp.where(chosen, 1.0, 0.0).astype(BF))
        for number in range(width // LANES):
            line_s[number, 0:2, :] = lines[2 * number : 2 * number + 2]
        rows = tokens_ref[...].astype(F32)
        normed = (rows * inverse_rms(rows) * gain_one_ref[...].astype(F32).reshape(1, width)).astype(BF)
        lefts_ref[0] = normed
        for part, weight_ref in enumerate((query_weight_ref, key_weight_ref, value_weight_ref)):
            values = dot(normed, weight_ref[...])
            for number in range(width // LANES):
                block = values[:, number * LANES : (number + 1) * LANES].astype(BF)
                if part == 0:
                    block = block * BF(HALF ** (-0.5))
                qkv_s[part, number] = block

    query = qkv_s[0, pair]
    key = qkv_s[1, pair]
    value = qkv_s[2, pair]
    qkv_ref[0, 0] = query
    qkv_ref[1, 0] = key
    qkv_ref[2, 0] = value
    lane = iota((seq_len, LANES), 1)
    row = iota((seq_len, LANES), 0)
    row_tile = row // TILE
    value_wide = jnp.concatenate([value, jnp.ones((seq_len, LANES), BF)], axis=1)
    query_wides, key_wides, nears = [], [], []
    for half in range(2):
        own = lane < HALF if half == 0 else lane >= HALF
        extra = lane - HALF if half == 0 else lane
        query_wides.append(
            jnp.where(
                own,
                query.astype(F32),
                jnp.where((extra == 0) | (extra == 1 + row_tile), 1.0, 0.0),
            ).astype(BF)
        )
        query_tile = extra - 1
        line = jnp.broadcast_to(line_s[pair, half : half + 1, :], (TILE, LINE))
        far = jnp.where(
            row_tile <= query_tile - 2,
            line[0:1, 0:1],
            jnp.where(row_tile >= query_tile + 2, line[0:1, 3 * TILE - 1 : 3 * TILE], 0.0),
        )
        far = jnp.where((query_tile >= 0) & (query_tile < tiles), far, 0.0)
        far = jnp.where((extra == 0) & (row >= length_ref[0]), NEGATIVE, far)
        key_wides.append(jnp.where(own, key.astype(F32), far).astype(BF))
        nears.append(pltpu.roll(line, 0, 1, stride=1, stride_axis=0)[:, : 3 * TILE])
    first = lane[:TILE] < HALF
    for tile in range(tiles):
        part = slice(tile * TILE, (tile + 1) * TILE)
        low = max(tile - 1, 0)
        high = min(tile + 2, tiles)
        outs = []
        for half in range(2):
            scores = dot(query_wides[half][part], key_wides[half], 1, 1)
            middle = nears[half][:, (low - tile + 1) * TILE : (high - tile + 1) * TILE]
            pieces = [scores[:, low * TILE : high * TILE] + middle]
            if low > 0:
                pieces.insert(0, scores[:, : low * TILE])
            if high < tiles:
                pieces.append(scores[:, high * TILE :])
            scores = jnp.concatenate(pieces, axis=1)
            peak = jnp.max(scores, axis=-1, keepdims=True)
            raised = jnp.exp(scores - peak).astype(BF)
            probs_ref[half, part, :] = raised
            outs.append(dot(raised, value_wide))
        inverse_total = 1.0 / jnp.where(first, outs[0][:, LANES:], outs[1][:, LANES:])
        mixed = jnp.where(first, outs[0][:, :LANES], outs[1][:, :LANES]) * inverse_total
        mixed_s[pair, part, :] = mixed.astype(BF)
        inverse_ref[0, part, :] = inverse_total

    @pl.when(pair == pairs - 1)
    def _():
        mixed_all = jnp.concatenate([mixed_s[number] for number in range(width // LANES)], axis=1)
        lefts_ref[1] = mixed_all
        resid = tokens_ref[...].astype(F32) + dot(mixed_all, out_weight_ref[...])
        resid_ref[...] = resid
        normed = (resid * inverse_rms(resid) * gain_two_ref[...].astype(F32).reshape(1, width)).astype(BF)
        send_rows(expert_ref, slot_ref[...], normed, plan, send_refs)


def forward_part(expert, lengths, slot, tokens, gain_one, weights, bias, gain_two, plan):
    seq_len, width = tokens.shape
    pairs = width // LANES
    square = whole((width, width))
    return pl.pallas_call(
        functools.partial(forward_kernel, plan),
        grid=(pairs,),
        out_shape=[
            shape_of((2 * pairs, seq_len, seq_len), BF),
            shape_of((3, pairs, seq_len, LANES), BF),
            shape_of((2, seq_len, width), BF),
            shape_of((pairs, seq_len, LANES), F32),
            shape_of((seq_len, width), F32),
        ]
        + [shape_of((rows, width), BF) for rows in plan.arrays],
        in_specs=[
            smem(),
            smem(),
            whole((1, seq_len)),
            whole((seq_len, width)),
            whole((width,)),
            square,
            square,
            square,
            square,
            whole(bias.shape),
            whole((width,)),
        ],
        out_specs=[
            pl.BlockSpec((2, seq_len, seq_len), lambda p: (p, 0, 0)),
            pl.BlockSpec((3, 1, seq_len, LANES), lambda p: (0, p, 0, 0)),
            whole((2, seq_len, width)),
            pl.BlockSpec((1, seq_len, LANES), lambda p: (p, 0, 0)),
            whole((seq_len, width)),
        ]
        + [whole((rows, width)) for rows in plan.arrays],
        scratch_shapes=[
            pltpu.VMEM((3, pairs, seq_len, LANES), BF),
            pltpu.VMEM((pairs, seq_len, LANES), BF),
            pltpu.VMEM((pairs, 8, LINE), F32),
        ],
        compiler_params=params(58),
        name="attention_forward",
    )(expert, lengths, slot, tokens, gain_one, *weights, bias, gain_two)


def expert_up_kernel(plan, out_ref, *refs):
    up_refs = refs[:-2]
    up_ref, act_grad_ref = refs[-2:]

    @pl.when(pl.program_id(0) == 0)
    def _():
        for number, ref in enumerate(plan.by_distance(up_refs)):
            rows = plan.block_rows
            up_ref[number * rows : (number + 1) * rows, :] = ref[...]

    act_grad_ref[...] = dot(up_ref[...], out_ref[0], 1, 1).astype(BF)


def expert_up_part(up_arrays, expert_out, plan):
    width = expert_out.shape[2]
    hidden = expert_out.shape[1]
    rows = sum(plan.arrays)
    tile = 512
    return pl.pallas_call(
        functools.partial(expert_up_kernel, plan),
        grid=(hidden // tile,),
        out_shape=[shape_of((rows, width), BF), shape_of((rows, hidden), BF)],
        in_specs=[pl.BlockSpec((1, tile, width), lambda f: (0, f, 0))]
        + plan.specs(up_arrays),
        out_specs=[whole((rows, width)), pl.BlockSpec((rows, tile), lambda f: (0, f))],
        compiler_params=params(28),
        name="expert_activation_gradient",
    )(expert_out, *up_arrays)


def expert_kernel(plan, inputs, count, expert_ref, up_ref, act_grad_ref, in_ref, router_ref, *refs):
    row_refs = refs[:inputs]
    act_ref, slope_ref, scaled_ref, rows_grad_ref, gate_ref, logit_grad_ref = refs[
        -(7 + count) : -(1 + count)
    ]
    back_refs, rows_ref = refs[-(1 + count) : -1], refs[-1]
    block_rows = plan.block_rows
    step = pl.program_id(0)
    steps = count
    rows, hidden = act_ref.shape
    experts = router_ref.shape[0]
    blocks = plan.by_distance(row_refs)
    for number in range(steps):

        @pl.when(step == number)
        def _(number=number):
            each = len(blocks) // steps
            for place in range(each):
                rows_ref[place * block_rows : (place + 1) * block_rows, :] = blocks[
                    number * each + place
                ][...]

    own = iota((rows, experts), 1) == expert_ref[0]
    logits = dot(rows_ref[...], router_ref[...], 1, 1)
    raised = jnp.exp(logits - jnp.max(logits, axis=-1, keepdims=True))
    probs = raised / jnp.sum(raised, axis=-1, keepdims=True)
    gate = jnp.sum(jnp.where(own, probs, 0.0), axis=-1, keepdims=True)
    gate_ref[...] = gate
    rows_grad_ref[...] = (up_ref[...].astype(F32) * gate).astype(BF)
    scaled_ref[...] = (rows_ref[...].astype(F32) * gate).astype(BF)
    gate_grad = jnp.zeros((rows, LANES), F32)
    tile = 512
    for first in range(0, hidden, tile):
        part = slice(first, first + tile)
        pre = dot(rows_ref[...], in_ref[0, :, part])
        act_grad = act_grad_ref[:, part]
        square = pre * pre
        level = 0.5 + 0.5 * jnp.tanh(pre * (GELU_ONE + GELU_ONE * GELU_CUBE * square))
        act = (pre * level).astype(BF)
        level = level.astype(BF)
        slope = level + act * (BF(1.0) - level) * (
            BF(2.0 * GELU_ONE) + BF(6.0 * GELU_ONE * GELU_CUBE) * square.astype(BF)
        )
        act_ref[:, part] = act
        product = (act * act_grad).astype(F32)
        for place in range(0, tile, LANES):
            gate_grad += product[:, place : place + LANES]
        slope_ref[:, part] = act_grad * slope
    gate_grad = jnp.sum(gate_grad, axis=-1, keepdims=True)
    logit_grad = gate_grad * (jnp.where(own, 1.0, 0.0) - probs)
    logit_grad_ref[...] = logit_grad.astype(BF)
    logit_grad = (gate * logit_grad).astype(BF)
    back = gate * dot(slope_ref[...], in_ref[0], 1, 1) + dot(logit_grad, router_ref[...])
    back = back.astype(BF)
    for number in range(steps):

        @pl.when(step == number)
        def _(number=number):
            back_refs[number][...] = back


def expert_part(expert, up_rows, act_grad, expert_in, router, row_arrays, plan, first, previous):
    rows, width = up_rows.shape
    hidden = expert_in.shape[2]
    experts = router.shape[0]
    some = rows // len(plan.arrays)
    steps = len(row_arrays) // 2 if plan.paired else 1

    def block(columns):
        return pl.BlockSpec((some, columns), lambda r: (first + r, 0))

    return pl.pallas_call(
        functools.partial(expert_kernel, plan, len(row_arrays), steps),
        grid=(steps,),
        out_shape=[
            shape_of((rows, hidden), BF),
            shape_of((rows, hidden), BF),
            shape_of((rows, width), BF),
            shape_of((rows, width), BF),
            shape_of((rows, 1), F32),
            shape_of((rows, experts), BF),
        ]
        + [shape_of((count, width), BF) for count in plan.arrays[:steps]],
        in_specs=[
            smem(),
            block(width),
            block(hidden),
            whole((1, width, hidden)),
            whole((experts, width)),
        ]
        + plan.specs(row_arrays)
        + [pl.BlockSpec(memory_space=pl.ANY)] * len(previous),
        out_specs=[block(columns) for columns in (hidden, hidden, width, width, 1, experts)]
        + [whole((count, width)) for count in plan.arrays[:steps]],
        input_output_aliases={5 + len(row_arrays) + n: n for n in range(len(previous))},
        scratch_shapes=[pltpu.VMEM((some, width), BF)],
        compiler_params=params(44),
        name="expert_rows",
    )(expert, up_rows, act_grad, expert_in, router, *row_arrays, *previous)


def later_sums_kernel(*refs):
    count = len(refs) // 3
    for keep_ref, there_ref, out_ref in zip(refs[:count], refs[count : 2 * count], refs[2 * count :]):
        out_ref[...] = (keep_ref[...].astype(F32) + there_ref[...].astype(F32)).astype(BF)


def later_sums(keeps, theres):
    count, rows, columns = keeps[0].shape
    later = count // 2
    some = rows // 4

    def block(first):
        return pl.BlockSpec((1, some, columns), lambda t, r: (first + t, r, 0))

    return pl.pallas_call(
        later_sums_kernel,
        grid=(later, 4),
        out_shape=[shape_of((later, rows, columns), BF)] * len(keeps),
        in_specs=[block(count - later)] * (2 * len(keeps)),
        out_specs=[block(0)] * len(keeps),
        compiler_params=params(58),
        name="later_sums",
    )(*keeps, *theres)


def weight_grad_kernel(transposed, count, *refs):
    _, wide_refs, rows_refs, out_refs = [refs[n * count : (n + 1) * count] for n in range(4)]
    for turned, wide_ref, rows_ref, out_ref in zip(transposed, wide_refs, rows_refs, out_refs):
        left_ref, right_ref = (wide_ref, rows_ref) if turned else (rows_ref, wide_ref)
        out_ref[0] = dot(left_ref[...], right_ref[...], 0, 0).astype(BF)


def weight_grad_part(parts, terms):
    tiles, wides, rows, transposed = zip(*terms)
    steps = tiles[0].shape[0]
    count, width = rows[0].shape
    tile = wides[0].shape[1] // parts
    shapes = [(tile, width) if turned else (width, tile) for turned in transposed]
    return pl.pallas_call(
        functools.partial(weight_grad_kernel, transposed, len(terms)),
        grid_spec=pltpu.PrefetchScalarGridSpec(
            num_scalar_prefetch=len(terms),
            grid=(steps,),
            in_specs=[
                pl.BlockSpec((count, tile), lambda s, *refs, number=number: (0, refs[number][s]))
                for number in range(len(terms))
            ]
            + [whole((count, width))] * len(terms),
            out_specs=[pl.BlockSpec((1,) + shape, lambda s, *_: (s, 0, 0)) for shape in shapes],
        ),
        out_shape=[shape_of((steps,) + shape, BF) for shape in shapes],
        compiler_params=params(SEND_LIMIT),
        name="expert_weight_gradients",
    )(*tiles, *wides, *rows)


def expert_out_kernel(act_ref, out_ref, gate_ref, *send_refs):
    rows = (dot(act_ref[...], out_ref[0]) * gate_ref[...]).astype(BF)
    for number, send_ref in enumerate(send_refs):

        @pl.when(pl.program_id(0) == number)
        def _(send_ref=send_ref):
            send_ref[...] = rows


def expert_out_part(act, expert_out, gate, plan):
    rows, hidden = act.shape
    width = expert_out.shape[2]
    steps = len(plan.arrays)
    return pl.pallas_call(
        expert_out_kernel,
        grid=(steps,),
        out_shape=[shape_of((count, width), BF) for count in plan.arrays],
        in_specs=[
            by_rows(rows // steps, hidden),
            whole((1, hidden, width)),
            by_rows(rows // steps, 1),
        ],
        out_specs=[whole((count, width)) for count in plan.arrays],
        compiler_params=params(32),
        name="expert_output",
    )(act, expert_out, gate)


ROW_STEPS = 2


def result_kernel(plan, expert_ref, length_ref, column_ref, resid_ref, *refs):
    total = resid_ref[...] + home_rows(expert_ref, column_ref[...], refs[:-1], plan)
    rows = total.shape[0]
    live = iota((rows, 1), 0) + pl.program_id(0) * rows < length_ref[0]
    refs[-1][...] = jnp.where(live, total, 0.0).astype(BF)


def result_part(expert, lengths, column, resid, arrays, plan):
    seq_len, width = resid.shape
    rows = seq_len // ROW_STEPS
    return pl.pallas_call(
        functools.partial(result_kernel, plan),
        grid=(ROW_STEPS,),
        out_shape=shape_of(resid.shape, BF),
        in_specs=[smem(), smem(), by_rows(rows, LANES), by_rows(rows, width)]
        + plan.specs(arrays),
        out_specs=by_rows(rows, width),
        compiler_params=params(58),
        name="result",
    )(expert, lengths, column, resid, *arrays)


def middle_kernel(
    plan,
    expert_ref,
    length_ref,
    column_ref,
    resid_ref,
    cotangent_ref,
    out_weight_ref,
    gain_ref,
    *refs,
):
    resid_grad_ref, mixed_grad_ref, attn_grad_ref, gain_grad_ref = refs[-4:]
    upstream = home_rows(expert_ref, column_ref[...], refs[:-4], plan)
    resid = resid_ref[...]
    rows = resid.shape[0]
    inverse = inverse_rms(resid)
    scaled = gain_ref[...].astype(F32).reshape(1, -1) * upstream
    add_rows(gain_grad_ref, jnp.sum(upstream * resid * inverse, axis=0, keepdims=True))
    live = iota((rows, 1), 0) + pl.program_id(0) * rows < length_ref[0]
    resid_grad = (
        jnp.where(live, cotangent_ref[...].astype(F32), 0.0)
        + inverse * scaled
        - resid * (inverse * inverse * inverse * jnp.mean(scaled * resid, axis=-1, keepdims=True))
    )
    resid_grad_ref[...] = resid_grad
    attn_grad = resid_grad.astype(BF)
    mixed_grad_ref[...] = dot(attn_grad, out_weight_ref[...], 1, 1).astype(BF)
    attn_grad_ref[...] = attn_grad


def middle_part(expert, lengths, column, resid, cotangent, out_weight, gain, arrays, plan):
    seq_len, width = resid.shape
    rows = seq_len // ROW_STEPS
    block = by_rows(rows, width)
    return pl.pallas_call(
        functools.partial(middle_kernel, plan),
        grid=(ROW_STEPS,),
        out_shape=[
            shape_of((seq_len, width), F32),
            shape_of((seq_len, width), BF),
            shape_of((seq_len, width), BF),
            shape_of((1, width), F32),
        ],
        in_specs=[smem(), smem(), by_rows(rows, LANES), block, block, whole((width, width)), whole((width,))]
        + plan.specs(arrays),
        out_specs=[block, block, block, whole((1, width))],
        compiler_params=params(58),
        name="expert_norm_backward",
    )(expert, lengths, column, resid, cotangent, out_weight, gain, *arrays)


def backward_kernel(
    core_ref,
    qkv_ref,
    probs_ref,
    lefts_ref,
    mixed_ref,
    grad_ref,
    attn_grad_ref,
    inverse_ref,
    back_ref,
    line_ref,
    *refs,
):
    own_refs, other_refs, score_s, lefts_s, backs_s = refs[:2], refs[2:4], *refs[4:]
    seq_len = grad_ref.shape[0]

    @pl.when(pl.program_id(0) == 0)
    def _():
        lefts_s[0] = lefts_ref[0].T
        lefts_s[1] = lefts_ref[1].T

    tiles = seq_len // TILE
    query = qkv_ref[0, 0]
    key = qkv_ref[1, 0]
    value = qkv_ref[2, 0]
    lane = iota((seq_len, LANES), 1)
    row_tile = iota((seq_len, LANES), 0) // TILE
    scaled = grad_ref[...].astype(F32) * inverse_ref[0]
    product = scaled * mixed_ref[0].astype(F32)
    scaled_low = scaled.astype(BF)
    key_wide = jnp.concatenate([key, jnp.where(lane == row_tile, 1.0, 0.0).astype(BF)], axis=1)
    backward_rows = jnp.where(iota((TILE, TILE), 0) + iota((TILE, TILE), 1) == TILE - 1, 1.0, 0.0)
    query_backs = []
    key_backs = []
    value_backs = []
    for half in range(2):
        own = lane < HALF if half == 0 else lane >= HALF
        extra = lane - HALF if half == 0 else lane
        delta = jnp.sum(jnp.where(own, product, 0.0), axis=-1, keepdims=True)
        high = delta.astype(BF).astype(F32)
        grad_wide = jnp.where(
            own, scaled, jnp.where(extra == 0, -high, jnp.where(extra == 1, high - delta, 0.0))
        ).astype(BF)
        value_wide = jnp.where(
            own, value.astype(F32), jnp.where((extra == 0) | (extra == 1), 1.0, 0.0)
        ).astype(BF)
        near = [jnp.zeros((TILE, TILE), F32) for _ in range(3)]
        for tile in range(tiles):
            part = slice(tile * TILE, (tile + 1) * TILE)
            prob_grad = dot(grad_wide[part], value_wide, 1, 1)
            score_grad = (probs_ref[half, part, :].astype(F32) * prob_grad).astype(BF)
            score_s[half, part, :] = score_grad
            for side in range(3):
                other = tile + side - 1
                if 0 <= other < tiles:
                    near[side] = near[side] + score_grad[
                        :, other * TILE : (other + 1) * TILE
                    ].astype(F32)
        query_wide = dot(score_s[half], key_wide)
        query_backs.append(query_wide[:, :LANES])
        sums = query_wide[:, LANES:]
        far_left = jnp.sum(jnp.where(lane <= row_tile - 2, sums, 0.0), axis=0, keepdims=True)
        far_right = jnp.sum(jnp.where(lane >= row_tile + 2, sums, 0.0), axis=0, keepdims=True)
        line_ref[0, half : half + 1, LINE : LINE + LANES] = far_left
        line_ref[0, half : half + 1, LINE + LANES :] = far_right
        key_backs.append(dot(query, score_s[half], 0, 0))
        value_backs.append(dot(scaled_low, probs_ref[half], 0, 0))
        spread = lax.dot_general(
            backward_rows,
            jnp.concatenate(near, axis=1),
            (((1,), (0,)), ((), ())),
            precision=lax.Precision.HIGHEST,
            preferred_element_type=F32,
        )
        spread = jnp.concatenate([spread, jnp.zeros((TILE, TILE), F32)], axis=1)
        spread = pltpu.roll(spread, 0, 1, stride=1, stride_axis=0)
        line_ref[0, half : half + 1, :LINE] = jnp.sum(spread, axis=0, keepdims=True)
    first = lane < HALF
    backs = [(jnp.where(first, query_backs[0], query_backs[1]) * HALF ** (-0.5)).astype(BF)]
    for halves in (key_backs, value_backs):
        joined = jnp.concatenate([halves[0][:HALF], halves[1][HALF:]], axis=0)
        backs.append(joined.T.astype(BF))
    backs.append(attn_grad_ref[...])
    for place, values in enumerate(backs):
        if place < 3:
            back_ref[place] = values

    @pl.when(pl.program_id(0) % 2 == 0)
    def _():
        for place, values in enumerate(backs):
            backs_s[place] = values

    @pl.when(pl.program_id(0) % 2 == 1)
    def _():
        wides = [jnp.concatenate([backs_s[n], values], axis=1) for n, values in enumerate(backs)]
        grads = [dot(lefts_s[n // 3], wide).astype(BF) for n, wide in enumerate(wides)]
        for core in range(2):

            @pl.when(core_ref[0] == core)
            def _(core=core):
                for target_refs, place in ((own_refs, core), (other_refs, 1 - core)):
                    target_refs[0][...] = grads[place]
                    target_refs[1][...] = grads[2 + place]


def backward_part(core, qkv, probs, lefts, mixed_grad, attn_grad, inverse):
    _, seq_len, width = lefts.shape
    pairs = width // LANES
    assert pairs % 2 == 0
    column = pl.BlockSpec((seq_len, LANES), lambda p: (0, p))
    grad = pl.BlockSpec((width, 2 * LANES), lambda p: (0, p // 2))
    return pl.pallas_call(
        backward_kernel,
        grid=(pairs,),
        out_shape=[
            shape_of((3, seq_len, width), BF),
            shape_of((pairs, 2, LINE + 2 * LANES), F32),
        ]
        + [shape_of((width, width), BF)] * 4,
        in_specs=[
            smem(),
            pl.BlockSpec((3, 1, seq_len, LANES), lambda p: (0, p, 0, 0)),
            pl.BlockSpec((2, seq_len, seq_len), lambda p: (p, 0, 0)),
            whole(lefts.shape),
            pl.BlockSpec((1, seq_len, LANES), lambda p: (1, 0, p)),
            column,
            column,
            pl.BlockSpec((1, seq_len, LANES), lambda p: (p, 0, 0)),
        ],
        out_specs=[
            pl.BlockSpec((3, seq_len, LANES), lambda p: (0, 0, p)),
            pl.BlockSpec((1, 2, LINE + 2 * LANES), lambda p: (p, 0, 0)),
        ]
        + [grad] * 4,
        scratch_shapes=[
            pltpu.VMEM((2, seq_len, seq_len), BF),
            pltpu.VMEM((2, width, seq_len), BF),
            pltpu.VMEM((4, seq_len, LANES), BF),
        ],
        compiler_params=params(58),
        name="attention_backward",
    )(core, qkv, probs, lefts, lefts, mixed_grad, attn_grad, inverse)


def extra_kernel(router_ref, gain_ref, line_ref, out_ref):
    experts, width = router_ref.shape
    heads, places = line_ref.shape
    place = iota((places, width), 0)
    bucket = iota((places, width), 1)
    own = bucket_of(place - (2 * TILE - 1), BUCKETS, MAXDIST)
    own = jnp.where(place >= LINE, BUCKETS // 2 - 1, own)
    own = jnp.where(place >= LINE + LANES, BUCKETS - 1, own)
    sums = lax.dot_general(
        line_ref[...],
        jnp.where(own == bucket, 1.0, 0.0),
        (((1,), (0,)), ((), ())),
        precision=lax.Precision.HIGHEST,
        preferred_element_type=F32,
    )
    rows = [
        router_ref[...],
        jnp.broadcast_to(gain_ref[...], (8, width)),
        sums,
        jnp.zeros((out_ref.shape[0] - experts - 8 - heads, width), F32),
    ]
    out_ref[...] = jnp.concatenate(rows, axis=0).astype(BF)


def extra_part(router_grad, gain_grad, lines):
    experts, width = router_grad.shape
    rows = -(-(experts + 8 + lines.shape[0]) // 16) * 16
    return pl.pallas_call(
        extra_kernel,
        out_shape=shape_of((rows, width), BF),
        compiler_params=params(58),
        name="extra_rows",
    )(router_grad, gain_grad, lines)


def token_grad_kernel(
    back_ref,
    query_weight_ref,
    key_weight_ref,
    value_weight_ref,
    tokens_ref,
    gain_ref,
    resid_grad_ref,
    out_ref,
):
    upstream = None
    for part, weight_ref in enumerate((query_weight_ref, key_weight_ref, value_weight_ref)):
        term = dot(back_ref[part], weight_ref[...], 1, 1)
        upstream = term if upstream is None else upstream + term
    rows = tokens_ref[...].astype(F32)
    inverse = inverse_rms(rows)
    scaled = gain_ref[...].astype(F32).reshape(1, -1) * upstream
    out_ref[...] = (
        resid_grad_ref[...]
        + inverse * scaled
        - rows * (inverse * inverse * inverse * jnp.mean(scaled * rows, axis=-1, keepdims=True))
    )


def token_grad_part(back, weights, tokens, gain, resid_grad):
    seq_len, width = tokens.shape
    rows = seq_len // ROW_STEPS
    block = by_rows(rows, width)
    return pl.pallas_call(
        token_grad_kernel,
        grid=(ROW_STEPS,),
        out_shape=shape_of((seq_len, width), F32),
        in_specs=[pl.BlockSpec((3, rows, width), lambda step: (0, step, 0))]
        + [whole((width, width))] * 3
        + [block, whole((width,)), block],
        out_specs=block,
        compiler_params=params(58),
        name="token_gradient",
    )(back, *weights, tokens, gain, resid_grad)


def swap(values, axis, size, distance):
    return lax.ppermute(values, axis, [(place, place ^ distance) for place in range(size)])


def after(values, *others):
    return lax.optimization_barrier((values, *others))[0]


class Plan:
    def __init__(self, size, capacity, experts):
        self.size = size
        self.capacity = capacity
        self.paired = size == 8 and capacity % 16 == 0
        if self.paired:
            self.block_rows = capacity
            self.blocks = size
            self.arrays = [2 * capacity] * (size // 2)
        else:
            self.block_rows = experts * capacity
            self.blocks = 1
            self.arrays = [experts * capacity]

    def turn(self, rows):
        parts = rows.reshape(self.size, self.capacity, rows.shape[1])
        parts = lax.all_to_all(parts, "expert", split_axis=0, concat_axis=0, tiled=True)
        return parts.reshape(rows.shape)

    def cross(self, arrays):
        if not self.paired:
            return [self.turn(array) for array in arrays]
        return [
            array if k == 0 else swap(array, "expert", self.size, 2 * k)
            for k, array in enumerate(arrays)
        ]

    def finish(self, arrays):
        if not self.paired:
            return arrays
        return [*arrays, *[swap(array, "expert", self.size, 1) for array in arrays]]

    def specs(self, arrays):
        if not self.paired:
            return [whole(array.shape) for array in arrays]
        return [
            pl.BlockSpec((self.block_rows, array.shape[1]), lambda *_, n=n: (2 * n // len(arrays), 0))
            for n, array in enumerate(arrays)
        ]

    def by_distance(self, refs):
        half = len(refs) // 2
        return [ref for pair in zip(refs[:half], refs[half:]) for ref in pair] if self.paired else refs


def stages_of(dp_size, expert_size):
    stages = [("expert", expert_size, (1,))]
    bits = [1 << n for n in range(dp_size.bit_length() - 1)]
    stages += [("dp", dp_size, tuple(bits[n : n + 2])) for n in range(0, len(bits), 2)]
    bits = [1 << n for n in range(1, expert_size.bit_length() - 1)]
    return stages + [("expert", expert_size, tuple(bits[n : n + 2])) for n in range(0, len(bits), 2)]


def distances_of(bits):
    return [sum(bit for n, bit in enumerate(bits) if (k >> n) & 1) for k in range(1 << len(bits))]


def place_of(stage):
    axis, _, bits = stage
    index = lax.axis_index(axis)
    return sum(((index // bit) % 2) << n for n, bit in enumerate(bits))


def share_kernel(inputs, extra, apart, place_ref, *refs):
    in_refs, out_refs = refs[:inputs], refs[inputs:]
    extra_refs, out_refs = out_refs[: len(out_refs) - apart], out_refs[len(out_refs) - apart :]
    last = in_refs[0].shape[0] - (0 if extra_refs else extra)
    count = 1 if place_ref is None else len(out_refs)
    rows = last // count
    for number in range(count):
        start = 0 if count == 1 else pl.multiple_of((place_ref[0] ^ number) * rows, rows)
        total = sum(ref[pl.ds(start, rows), :].astype(F32) for ref in in_refs)
        out_refs[number][:rows, :] = total.astype(BF)
    if extra:
        if extra_refs:
            total = sum(ref[...].astype(F32) for ref in extra_refs).astype(BF)
        else:
            total = sum(ref[last:, :].astype(F32) for ref in in_refs).astype(BF)
        if count > 1:
            for out_ref in out_refs:
                out_ref[rows:, :] = total
        else:
            out_refs[-1][...] = total


def share(parts, stage, extra, extras=()):
    count = 1 if stage is None else 1 << len(stage[2])
    place = None if stage is None else place_of(stage)
    if parts[0].shape[0] // count % 16 and extras:
        parts = [jnp.concatenate(pair, axis=0) for pair in zip(parts, extras)]
        extras = ()
    last, width = parts[0].shape[0] - (0 if extras else extra), parts[0].shape[1]
    rows = last // count
    shapes = [(rows + extra, width)] * count if count > 1 else [(rows, width)]
    if count == 1 and extra:
        shapes.append((extra, width))
    if rows % 16:
        total = sum(part.astype(F32) for part in parts).astype(BF)
        if stage is None:
            return [total[:last], total[last:]] if extra else [total]
        return [
            jnp.concatenate(
                [lax.dynamic_slice_in_dim(total, (place ^ number) * rows, rows, 0), total[last:]], axis=0
            )
            for number in range(count)
        ]
    kernel = functools.partial(share_kernel, len(parts), extra, len(shapes))
    if stage is None:
        kernel = functools.partial(kernel, None)
    return pl.pallas_call(
        kernel,
        out_shape=[shape_of(shape, BF) for shape in shapes],
        in_specs=[smem()] * (stage is not None) + [pl.BlockSpec()] * (len(parts) + len(extras)),
        compiler_params=params(58),
        name="share",
    )(*([] if stage is None else [place.reshape(1)]), *parts, *extras)


def scatter(parts, stage):
    axis, size, bits = stage
    return [
        part if distance == 0 else swap(part, axis, size, distance)
        for part, distance in zip(parts, distances_of(bits))
    ]


def gather(values, stage):
    axis, size, bits = stage
    return [
        values if distance == 0 else swap(values, axis, size, distance)
        for distance in distances_of(bits)
    ]


def join_kernel(place_ref, *refs):
    out_ref = refs[-1]
    for number, ref in enumerate(refs[:-1]):
        rows = ref.shape[0]
        part = pl.ds(pl.multiple_of((place_ref[0] ^ number) * rows, rows), rows)
        out_ref[part, :] = ref[...]


def join(parts, stage):
    place = place_of(stage)
    rows, width = parts[0].shape
    if rows % 16:
        joined = jnp.zeros((rows * len(parts), width), BF)
        for number, part in enumerate(parts):
            joined = lax.dynamic_update_slice_in_dim(joined, part, (place ^ number) * rows, 0)
        return joined
    return pl.pallas_call(
        join_kernel,
        out_shape=shape_of((rows * len(parts), width), BF),
        in_specs=[smem()] + [pl.BlockSpec()] * len(parts),
        compiler_params=params(58),
        name="join",
    )(place.reshape(1), *parts)


def assemble_kernel(count, places_ref, *refs):
    own_refs, other_refs = refs[:count], refs[count : 2 * count]
    weight_refs, out_refs, gain_ref = refs[2 * count : -3], refs[-3:-1], refs[-1]
    source = places_ref[1] ^ pl.program_id(0)
    for number in range(count):
        for core in range(2):

            @pl.when((source == number) & (places_ref[0] == core))
            def _(number=number, core=core):
                out_refs[core][...] = own_refs[number][...].astype(F32)
                out_refs[1 - core][...] = other_refs[number][...].astype(F32)

    total = sum(
        jnp.sum(out_ref[...] * weight_ref[...].astype(F32), axis=1, keepdims=True)
        for out_ref, weight_ref in zip(out_refs, weight_refs)
    )
    gain_ref[...] = jnp.broadcast_to(total, gain_ref.shape)


def assemble(own, other, stages, weights):
    rows, width = own[0].shape
    count = len(own)
    block = by_rows(rows, width)
    places = jnp.stack([place_of(stage) for stage in stages])
    return pl.pallas_call(
        functools.partial(assemble_kernel, count),
        grid=(count,),
        out_shape=[shape_of((count * rows, width), F32)] * 2 + [shape_of((count * rows, LANES), F32)],
        in_specs=[smem()] + [whole((rows, width))] * (2 * count) + [block] * len(weights),
        out_specs=[block, block, by_rows(rows, LANES)],
        compiler_params=params(58),
        name="assemble",
    )(places, *own, *other, *weights)


def halving_order(bits):
    if not bits:
        return [0]
    rest = halving_order(bits[1:])
    return rest + [distance | bits[0] for distance in rest]


def on_device(
    dp_size,
    expert_size,
    tokens,
    cotangent,
    lengths,
    routes,
    norm_gain,
    query_weight,
    key_weight,
    value_weight,
    output_weight,
    bucket_head_bias,
    ffn_gain,
    router_weight,
    expert_in,
    expert_out,
):
    seq_count, seq_len, width = tokens.shape
    buckets, heads = bucket_head_bias.shape
    assert seq_count == 1 and buckets == BUCKETS
    experts = router_weight.shape[1]
    capacity = max(2, 5 * seq_len // (4 * experts))
    plan = Plan(expert_size, capacity, experts)
    expert = lax.axis_index("expert").reshape(1)
    group = lax.axis_index("dp")
    rows_in = tokens.reshape(seq_len, width)
    upstream = cotangent.reshape(seq_len, width)
    weights = (query_weight, key_weight, value_weight)

    slot, column, *up_send = slots_part(expert, lengths, routes, upstream, capacity, experts, plan)
    up_there = plan.cross(up_send)
    probs, qkv, lefts, inverse_total, resid, *row_send = forward_part(
        expert,
        lengths,
        slot,
        rows_in,
        norm_gain,
        (*weights, output_weight),
        bucket_head_bias.T,
        ffn_gain,
        plan,
    )
    row_send, up_there = lax.optimization_barrier((row_send, up_there))
    row_there = plan.cross(row_send)
    up_rows, act_grad = expert_up_part(plan.finish(up_there), expert_out, plan)
    cut = len(row_there) - 1 if plan.paired else len(row_there)
    values, back_send = (), []
    for first, some in ((0, row_there[:cut]), (cut, row_there[cut:])):
        if some:
            some = lax.optimization_barrier((some, values[4] if values else act_grad))[0]
            outs = expert_part(
                expert,
                up_rows,
                act_grad,
                expert_in,
                router_weight.T,
                plan.finish(some),
                plan,
                first,
                values,
            )
            values, back_send = outs[:6], back_send + list(outs[6:])
    act, slope, scaled_rows, rows_grad, gate, logit_grad = values
    router_grad = dot(logit_grad, scaled_rows, 0, 0)
    back_there = plan.cross(back_send)

    bits = [1 << n for n in range(dp_size.bit_length() - 1)]
    half = dp_size // 2
    orders = (bits, bits[::-1])
    tiles = [group ^ jnp.array(halving_order(order), jnp.int32) for order in orders]
    grad_terms = [(act, rows_grad, True), (slope, scaled_rows, False)]
    sends = [
        weight_grad_part(dp_size, [(tile[half:], *term)])[0] for tile, term in zip(tiles, grad_terms)
    ]
    arrived = [swap(send, "dp", dp_size, order[0]) for send, order in zip(sends, orders)]
    keeps = weight_grad_part(
        dp_size, [(tile[:half], *term) for tile, term in zip(tiles, grad_terms)]
    )
    result_send = expert_out_part(act, expert_out, gate, plan)
    back_there = lax.optimization_barrier((back_there, keeps, result_send))[0]
    back_arrays = plan.finish(back_there)

    resid_grad, mixed_grad, attn_grad, ffn_gain_grad = middle_part(
        expert, lengths, column, after(resid, *keeps), upstream, output_weight, ffn_gain, back_arrays, plan
    )
    result_send = lax.optimization_barrier((result_send, back_there))[0]
    result_there = plan.cross(result_send)

    arrived = lax.optimization_barrier((arrived, back_arrays))[0]
    seconds = later_sums(keeps, arrived)
    rests = [list(order[1:]) for order in orders]
    arrived_seconds = [
        swap(send, "dp", dp_size, rest[0]) if rest else None for send, rest in zip(seconds, rests)
    ]
    mixed_grad = after(mixed_grad, *seconds)

    stages = stages_of(dp_size, expert_size)
    core = place_of(stages[0])
    back, lines, *grads = backward_part(
        core.reshape(1), qkv, probs, lefts, mixed_grad, attn_grad, inverse_total
    )
    kept, sent = grads[:2], grads[2:]
    back, sent, result_there, arrived_seconds = lax.optimization_barrier(
        (back, sent, result_there, arrived_seconds)
    )

    there = [swap(values, *stages[0][:2], 1) for values in sent]
    extra = extra_part(router_grad, ffn_gain_grad, lines.reshape(heads, -1))
    extra_rows = [0, extra.shape[0]]
    extras = [(), (extra, swap(extra, *stages[0][:2], 1))]
    shares = []
    for values, other, rows, more in zip(kept, there, extra_rows, extras):
        parts = [values, other]
        if shares:
            parts = after(parts, shares[0])
        shares.append(share(parts, stages[1], rows, more))
    moved = [scatter(parts, stages[1]) for parts in shares]
    token_grad = token_grad_part(after(back, *shares[1]), weights, rows_in, norm_gain, resid_grad)
    moved[0], token_grad, result_there = lax.optimization_barrier(
        (moved[0], token_grad, result_there)
    )
    result_arrays = plan.finish(result_there)
    for stage in stages[2:]:
        shares = [share(parts, stage, rows) for parts, rows in zip(moved, extra_rows)]
        moved = [scatter(parts, stage) for parts in shares]
    chunks = [share(parts, None, rows) for parts, rows in zip(moved, extra_rows)]
    extra = chunks[1][1].astype(F32)
    chunks = [chunk[0] for chunk in chunks]
    for stage in stages[:1:-1]:
        chunks = [join(gather(values, stage), stage) for values in chunks]
    there = [gather(values, stages[1]) for values in chunks]
    keeps, arrived, arrived_seconds, resid = lax.optimization_barrier(
        (keeps, arrived, arrived_seconds, resid, chunks)
    )[:4]
    result = result_part(expert, lengths, column, resid, result_arrays, plan)
    weight_sums = []
    for rest, keep, term, second in zip(rests, keeps, arrived, arrived_seconds):
        total = keep[: half // 2].astype(F32) + term[: half // 2].astype(F32)
        if rest:
            total = total + second.astype(F32)
        weight_sums.append(total)
    last = [pieces.pop() for pieces in there]
    over = [[swap(piece, *stages[0][:2], 1) for piece in pieces] for pieces in there]
    last, weight_sums, result = lax.optimization_barrier((last, weight_sums, result))
    for pieces, others, piece in zip(there, over, last):
        pieces.append(piece)
        others.append(swap(piece, *stages[0][:2], 1))
    expert_out_grad, expert_in_grad = weight_sums
    (query_grad, key_grad, gain_sum), (value_grad, output_grad, value_sum) = [
        assemble(own, other, stages[:2], some)
        for own, other, some in zip(there, over, ((query_weight, key_weight), (value_weight,)))
    ]
    norm_gain_grad = (gain_sum + value_sum)[:, 0] / norm_gain.astype(F32)

    return (
        result.reshape(tokens.shape),
        token_grad.reshape(tokens.shape),
        norm_gain_grad,
        query_grad,
        key_grad,
        value_grad,
        output_grad,
        extra[experts + 8 : experts + 8 + heads, :buckets].T,
        extra[experts],
        extra[:experts].T,
        expert_in_grad,
        expert_out_grad,
    )


def solution(mesh):
    in_specs = (
        P(("dp", "expert"), None, None),
        P(("dp", "expert"), None, None),
        P(("dp", "expert")),
        P(("dp", "expert"), None),
        P(),
        P(),
        P(),
        P(),
        P(),
        P(),
        P(),
        P(),
        P("expert", None, None),
        P("expert", None, None),
    )
    out_specs = (
        P(("dp", "expert"), None, None),
        P(("dp", "expert"), None, None),
        P(),
        P(),
        P(),
        P(),
        P(),
        P(),
        P(),
        P(),
        P("expert", None, "dp"),
        P("expert", "dp", None),
    )
    return jax.shard_map(
        functools.partial(on_device, mesh.shape["dp"], mesh.shape["expert"]),
        mesh=mesh,
        in_specs=in_specs,
        out_specs=out_specs,
        check_vma=False,
    )
```

```python
import functools
import math

import jax
import jax.numpy as jnp
from jax import lax
from jax.experimental import pallas as pl
from jax.experimental.pallas import tpu as pltpu
from jax.sharding import PartitionSpec as P

BF = jnp.bfloat16
F32 = jnp.float32
MAXDIST = 128
EPSILON = 1e-06
NEGATIVE = -1000000000.0
TILE = 128
BUCKETS = 32
LANES = 128
HALF = 64
LINE = 4 * TILE
GELU_ONE = math.sqrt(2.0 / math.pi)
GELU_CUBE = 0.044715
SEND_LIMIT = 32


def dot(left, right, left_dim=1, right_dim=0):
    return lax.dot_general(
        left, right, (((left_dim,), (right_dim,)), ((), ())), preferred_element_type=F32
    )


def iota(shape, dim):
    return lax.broadcasted_iota(jnp.int32, shape, dim)


def bucket_of(offset, buckets, far_limit):
    exact_limit = buckets // 4
    half_count = buckets // 2
    distance = jnp.abs(offset)
    bucket_ids = jnp.minimum(distance, exact_limit)
    for bucket_level in range(exact_limit + 1, half_count):
        border = math.ceil(
            exact_limit
            * (far_limit / exact_limit)
            ** ((bucket_level - exact_limit) / (half_count - exact_limit))
        )
        bucket_ids = bucket_ids + (distance >= border).astype(jnp.int32)
    return bucket_ids + jnp.where(offset > 0, half_count, 0).astype(jnp.int32)


def whole(shape):
    return pl.BlockSpec(shape, lambda *_: (0,) * len(shape))


def by_rows(rows, columns):
    return pl.BlockSpec((rows, columns), lambda step: (step, 0))


def add_rows(ref, values):
    @pl.when(pl.program_id(0) == 0)
    def _():
        ref[...] = values

    @pl.when(pl.program_id(0) > 0)
    def _():
        ref[...] += values


def smem():
    return pl.BlockSpec(memory_space=pltpu.SMEM)


def params(mebibytes):
    return pltpu.CompilerParams(vmem_limit_bytes=mebibytes * 1024 * 1024)


def shape_of(shape, dtype):
    return jax.ShapeDtypeStruct(shape, dtype)


def inverse_rms(rows):
    return lax.rsqrt(jnp.mean(rows * rows, axis=-1, keepdims=True) + EPSILON)


def send_rows(expert_ref, slot_row, rows, plan, send_refs):
    block_rows = plan.block_rows
    size = plan.blocks * block_rows
    place = iota((size, 1), 0)
    wanted = place
    if plan.paired:
        for distance in range(plan.blocks):
            first = distance * block_rows
            wanted = jnp.where(
                place >= first, place - first + (expert_ref[0] ^ distance) * block_rows, wanted
            )
    chosen = jnp.where(wanted == slot_row, 1.0, 0.0).astype(BF)
    sent = dot(chosen, rows).astype(BF)
    first = 0
    for send_ref in send_refs:
        send_ref[...] = sent[first : first + send_ref.shape[0]]
        first += send_ref.shape[0]


def home_rows(expert_ref, column, refs, plan):
    block_rows = plan.block_rows
    rows = jnp.concatenate([ref[...] for ref in plan.by_distance(refs)], axis=0)
    place = iota((1, rows.shape[0]), 1)
    wanted = place
    for distance in range(plan.blocks):
        first = distance * block_rows
        base = (expert_ref[0] ^ distance) * block_rows if plan.paired else 0
        wanted = jnp.where(place >= first, place - first + base, wanted)
    chosen = jnp.where(column[:, :1] == wanted, 1.0, 0.0).astype(BF)
    return dot(chosen, rows)


def slots_kernel(
    capacity, experts, plan, expert_ref, length_ref, routes_ref, cotangent_ref, slot_ref, column_ref, *send_refs
):
    seq_len = routes_ref.shape[1]
    routes = routes_ref[...]
    live = iota((1, seq_len), 1) < length_ref[0]
    onehot = jnp.where((iota((experts, seq_len), 0) == routes) & live, 1.0, 0.0)
    earlier = jnp.where(iota((seq_len, seq_len), 0) < iota((seq_len, seq_len), 1), 1.0, 0.0)
    before = dot(onehot.astype(BF), earlier.astype(BF))
    rank = jnp.sum(before * onehot, axis=0, keepdims=True).astype(jnp.int32)
    slot = jnp.where(live & (rank < capacity), routes * capacity + rank, -1)
    slot_ref[...] = slot
    wide = jnp.broadcast_to(slot.astype(F32), (LANES, seq_len))
    column_ref[...] = wide.T.astype(jnp.int32)
    send_rows(expert_ref, slot, cotangent_ref[...], plan, send_refs)


def slots_part(expert, lengths, routes, cotangent, capacity, experts, plan):
    seq_len, width = cotangent.shape
    return pl.pallas_call(
        functools.partial(slots_kernel, capacity, experts, plan),
        out_shape=[shape_of((1, seq_len), jnp.int32), shape_of((seq_len, LANES), jnp.int32)]
        + [shape_of((rows, width), BF) for rows in plan.arrays],
        in_specs=[smem(), smem(), pl.BlockSpec(), pl.BlockSpec()],
        compiler_params=params(58),
        name="slots",
    )(expert, lengths, routes, cotangent)


def forward_kernel(
    plan,
    expert_ref,
    length_ref,
    slot_ref,
    tokens_ref,
    gain_one_ref,
    query_weight_ref,
    key_weight_ref,
    value_weight_ref,
    out_weight_ref,
    bias_ref,
    gain_two_ref,
    *refs,
):
    probs_ref, qkv_ref, lefts_ref, inverse_ref, resid_ref = refs[:5]
    send_refs = refs[5:-3]
    qkv_s, mixed_s, line_s = refs[-3:]
    pair = pl.program_id(0)
    pairs = pl.num_programs(0)
    seq_len, width = tokens_ref.shape
    tiles = seq_len // TILE

    @pl.when(pair == 0)
    def _():
        buckets = bias_ref.shape[1]
        place = iota((buckets, LINE), 1)
        offset = jnp.where(place < 3 * TILE, place - TILE, place - TILE - LINE)
        chosen = bucket_of(offset, buckets, MAXDIST) == iota((buckets, LINE), 0)
        lines = dot(bias_ref[...], jnp.where(chosen, 1.0, 0.0).astype(BF))
        for number in range(width // LANES):
            line_s[number, 0:2, :] = lines[2 * number : 2 * number + 2]
        rows = tokens_ref[...].astype(F32)
        normed = (rows * inverse_rms(rows) * gain_one_ref[...].astype(F32).reshape(1, width)).astype(BF)
        lefts_ref[0] = normed
        for part, weight_ref in enumerate((query_weight_ref, key_weight_ref, value_weight_ref)):
            values = dot(normed, weight_ref[...])
            for number in range(width // LANES):
                block = values[:, number * LANES : (number + 1) * LANES].astype(BF)
                if part == 0:
                    block = block * BF(HALF ** (-0.5))
                qkv_s[part, number] = block

    query = qkv_s[0, pair]
    key = qkv_s[1, pair]
    value = qkv_s[2, pair]
    qkv_ref[0, 0] = query
    qkv_ref[1, 0] = key
    qkv_ref[2, 0] = value
    lane = iota((seq_len, LANES), 1)
    row = iota((seq_len, LANES), 0)
    row_tile = row // TILE
    value_wide = jnp.concatenate([value, jnp.ones((seq_len, LANES), BF)], axis=1)
    query_wides, key_wides, nears = [], [], []
    for half in range(2):
        own = lane < HALF if half == 0 else lane >= HALF
        extra = lane - HALF if half == 0 else lane
        query_wides.append(
            jnp.where(
                own,
                query.astype(F32),
                jnp.where((extra == 0) | (extra == 1 + row_tile), 1.0, 0.0),
            ).astype(BF)
        )
        query_tile = extra - 1
        line = jnp.broadcast_to(line_s[pair, half : half + 1, :], (TILE, LINE))
        far = jnp.where(
            row_tile <= query_tile - 2,
            line[0:1, 0:1],
            jnp.where(row_tile >= query_tile + 2, line[0:1, 3 * TILE - 1 : 3 * TILE], 0.0),
        )
        far = jnp.where((query_tile >= 0) & (query_tile < tiles), far, 0.0)
        far = jnp.where((extra == 0) & (row >= length_ref[0]), NEGATIVE, far)
        key_wides.append(jnp.where(own, key.astype(F32), far).astype(BF))
        nears.append(pltpu.roll(line, 0, 1, stride=1, stride_axis=0)[:, : 3 * TILE])
    first = lane[:TILE] < HALF
    for tile in range(tiles):
        part = slice(tile * TILE, (tile + 1) * TILE)
        low = max(tile - 1, 0)
        high = min(tile + 2, tiles)
        outs = []
        for half in range(2):
            scores = dot(query_wides[half][part], key_wides[half], 1, 1)
            middle = nears[half][:, (low - tile + 1) * TILE : (high - tile + 1) * TILE]
            pieces = [scores[:, low * TILE : high * TILE] + middle]
            if low > 0:
                pieces.insert(0, scores[:, : low * TILE])
            if high < tiles:
                pieces.append(scores[:, high * TILE :])
            scores = jnp.concatenate(pieces, axis=1)
            peak = jnp.max(scores, axis=-1, keepdims=True)
            raised = jnp.exp(scores - peak).astype(BF)
            probs_ref[half, part, :] = raised
            outs.append(dot(raised, value_wide))
        inverse_total = 1.0 / jnp.where(first, outs[0][:, LANES:], outs[1][:, LANES:])
        mixed = jnp.where(first, outs[0][:, :LANES], outs[1][:, :LANES]) * inverse_total
        mixed_s[pair, part, :] = mixed.astype(BF)
        inverse_ref[0, part, :] = inverse_total

    @pl.when(pair == pairs - 1)
    def _():
        mixed_all = jnp.concatenate([mixed_s[number] for number in range(width // LANES)], axis=1)
        lefts_ref[1] = mixed_all
        resid = tokens_ref[...].astype(F32) + dot(mixed_all, out_weight_ref[...])
        resid_ref[...] = resid
        normed = (resid * inverse_rms(resid) * gain_two_ref[...].astype(F32).reshape(1, width)).astype(BF)
        send_rows(expert_ref, slot_ref[...], normed, plan, send_refs)


def forward_part(expert, lengths, slot, tokens, gain_one, weights, bias, gain_two, plan):
    seq_len, width = tokens.shape
    pairs = width // LANES
    square = whole((width, width))
    return pl.pallas_call(
        functools.partial(forward_kernel, plan),
        grid=(pairs,),
        out_shape=[
            shape_of((2 * pairs, seq_len, seq_len), BF),
            shape_of((3, pairs, seq_len, LANES), BF),
            shape_of((2, seq_len, width), BF),
            shape_of((pairs, seq_len, LANES), F32),
            shape_of((seq_len, width), F32),
        ]
        + [shape_of((rows, width), BF) for rows in plan.arrays],
        in_specs=[
            smem(),
            smem(),
            whole((1, seq_len)),
            whole((seq_len, width)),
            whole((width,)),
            square,
            square,
            square,
            square,
            whole(bias.shape),
            whole((width,)),
        ],
        out_specs=[
            pl.BlockSpec((2, seq_len, seq_len), lambda p: (p, 0, 0)),
            pl.BlockSpec((3, 1, seq_len, LANES), lambda p: (0, p, 0, 0)),
            whole((2, seq_len, width)),
            pl.BlockSpec((1, seq_len, LANES), lambda p: (p, 0, 0)),
            whole((seq_len, width)),
        ]
        + [whole((rows, width)) for rows in plan.arrays],
        scratch_shapes=[
            pltpu.VMEM((3, pairs, seq_len, LANES), BF),
            pltpu.VMEM((pairs, seq_len, LANES), BF),
            pltpu.VMEM((pairs, 8, LINE), F32),
        ],
        compiler_params=params(58),
        name="attention_forward",
    )(expert, lengths, slot, tokens, gain_one, *weights, bias, gain_two)


def expert_up_kernel(plan, out_ref, *refs):
    up_refs = refs[:-2]
    up_ref, act_grad_ref = refs[-2:]

    @pl.when(pl.program_id(0) == 0)
    def _():
        for number, ref in enumerate(plan.by_distance(up_refs)):
            rows = plan.block_rows
            up_ref[number * rows : (number + 1) * rows, :] = ref[...]

    act_grad_ref[...] = dot(up_ref[...], out_ref[0], 1, 1).astype(BF)


def expert_up_part(up_arrays, expert_out, plan):
    width = expert_out.shape[2]
    hidden = expert_out.shape[1]
    rows = sum(plan.arrays)
    tile = 512
    return pl.pallas_call(
        functools.partial(expert_up_kernel, plan),
        grid=(hidden // tile,),
        out_shape=[shape_of((rows, width), BF), shape_of((rows, hidden), BF)],
        in_specs=[pl.BlockSpec((1, tile, width), lambda f: (0, f, 0))]
        + plan.specs(up_arrays),
        out_specs=[whole((rows, width)), pl.BlockSpec((rows, tile), lambda f: (0, f))],
        compiler_params=params(28),
        name="expert_activation_gradient",
    )(expert_out, *up_arrays)


def expert_kernel(plan, inputs, count, expert_ref, up_ref, act_grad_ref, in_ref, router_ref, *refs):
    row_refs = refs[:inputs]
    act_ref, slope_ref, scaled_ref, rows_grad_ref, gate_ref, logit_grad_ref = refs[
        -(7 + count) : -(1 + count)
    ]
    back_refs, rows_ref = refs[-(1 + count) : -1], refs[-1]
    block_rows = plan.block_rows
    step = pl.program_id(0)
    steps = count
    rows, hidden = act_ref.shape
    experts = router_ref.shape[0]
    blocks = plan.by_distance(row_refs)
    for number in range(steps):

        @pl.when(step == number)
        def _(number=number):
            each = len(blocks) // steps
            for place in range(each):
                rows_ref[place * block_rows : (place + 1) * block_rows, :] = blocks[
                    number * each + place
                ][...]

    own = iota((rows, experts), 1) == expert_ref[0]
    logits = dot(rows_ref[...], router_ref[...], 1, 1)
    raised = jnp.exp(logits - jnp.max(logits, axis=-1, keepdims=True))
    probs = raised / jnp.sum(raised, axis=-1, keepdims=True)
    gate = jnp.sum(jnp.where(own, probs, 0.0), axis=-1, keepdims=True)
    gate_ref[...] = gate
    rows_grad_ref[...] = (up_ref[...].astype(F32) * gate).astype(BF)
    scaled_ref[...] = (rows_ref[...].astype(F32) * gate).astype(BF)
    gate_grad = jnp.zeros((rows, LANES), F32)
    tile = 512
    for first in range(0, hidden, tile):
        part = slice(first, first + tile)
        pre = dot(rows_ref[...], in_ref[0, :, part])
        act_grad = act_grad_ref[:, part]
        square = pre * pre
        level = 0.5 + 0.5 * jnp.tanh(pre * (GELU_ONE + GELU_ONE * GELU_CUBE * square))
        act = (pre * level).astype(BF)
        level = level.astype(BF)
        slope = level + act * (BF(1.0) - level) * (
            BF(2.0 * GELU_ONE) + BF(6.0 * GELU_ONE * GELU_CUBE) * square.astype(BF)
        )
        act_ref[:, part] = act
        product = (act * act_grad).astype(F32)
        for place in range(0, tile, LANES):
            gate_grad += product[:, place : place + LANES]
        slope_ref[:, part] = act_grad * slope
    gate_grad = jnp.sum(gate_grad, axis=-1, keepdims=True)
    logit_grad = gate_grad * (jnp.where(own, 1.0, 0.0) - probs)
    logit_grad_ref[...] = logit_grad.astype(BF)
    logit_grad = (gate * logit_grad).astype(BF)
    back = gate * dot(slope_ref[...], in_ref[0], 1, 1) + dot(logit_grad, router_ref[...])
    back = back.astype(BF)
    for number in range(steps):

        @pl.when(step == number)
        def _(number=number):
            back_refs[number][...] = back


def expert_part(expert, up_rows, act_grad, expert_in, router, row_arrays, plan, first, previous):
    rows, width = up_rows.shape
    hidden = expert_in.shape[2]
    experts = router.shape[0]
    some = rows // len(plan.arrays)
    steps = len(row_arrays) // 2 if plan.paired else 1

    def block(columns):
        return pl.BlockSpec((some, columns), lambda r: (first + r, 0))

    return pl.pallas_call(
        functools.partial(expert_kernel, plan, len(row_arrays), steps),
        grid=(steps,),
        out_shape=[
            shape_of((rows, hidden), BF),
            shape_of((rows, hidden), BF),
            shape_of((rows, width), BF),
            shape_of((rows, width), BF),
            shape_of((rows, 1), F32),
            shape_of((rows, experts), BF),
        ]
        + [shape_of((count, width), BF) for count in plan.arrays[:steps]],
        in_specs=[
            smem(),
            block(width),
            block(hidden),
            whole((1, width, hidden)),
            whole((experts, width)),
        ]
        + plan.specs(row_arrays)
        + [pl.BlockSpec(memory_space=pl.ANY)] * len(previous),
        out_specs=[block(columns) for columns in (hidden, hidden, width, width, 1, experts)]
        + [whole((count, width)) for count in plan.arrays[:steps]],
        input_output_aliases={5 + len(row_arrays) + n: n for n in range(len(previous))},
        scratch_shapes=[pltpu.VMEM((some, width), BF)],
        compiler_params=params(44),
        name="expert_rows",
    )(expert, up_rows, act_grad, expert_in, router, *row_arrays, *previous)


def later_sums_kernel(*refs):
    count = len(refs) // 3
    for keep_ref, there_ref, out_ref in zip(refs[:count], refs[count : 2 * count], refs[2 * count :]):
        out_ref[...] = (keep_ref[...].astype(F32) + there_ref[...].astype(F32)).astype(BF)


def later_sums(keeps, theres):
    count, rows, columns = keeps[0].shape
    later = count // 2
    some = rows // 4

    def block(first):
        return pl.BlockSpec((1, some, columns), lambda t, r: (first + t, r, 0))

    return pl.pallas_call(
        later_sums_kernel,
        grid=(later, 4),
        out_shape=[shape_of((later, rows, columns), BF)] * len(keeps),
        in_specs=[block(count - later)] * (2 * len(keeps)),
        out_specs=[block(0)] * len(keeps),
        compiler_params=params(63),
        name="later_sums",
    )(*keeps, *theres)


def weight_grad_kernel(transposed, count, *refs):
    _, wide_refs, rows_refs, out_refs = [refs[n * count : (n + 1) * count] for n in range(4)]
    for turned, wide_ref, rows_ref, out_ref in zip(transposed, wide_refs, rows_refs, out_refs):
        left_ref, right_ref = (wide_ref, rows_ref) if turned else (rows_ref, wide_ref)
        out_ref[0] = dot(left_ref[...], right_ref[...], 0, 0).astype(BF)


def weight_grad_part(parts, terms):
    tiles, wides, rows, transposed = zip(*terms)
    steps = tiles[0].shape[0]
    count, width = rows[0].shape
    tile = wides[0].shape[1] // parts
    shapes = [(tile, width) if turned else (width, tile) for turned in transposed]
    return pl.pallas_call(
        functools.partial(weight_grad_kernel, transposed, len(terms)),
        grid_spec=pltpu.PrefetchScalarGridSpec(
            num_scalar_prefetch=len(terms),
            grid=(steps,),
            in_specs=[
                pl.BlockSpec((count, tile), lambda s, *refs, number=number: (0, refs[number][s]))
                for number in range(len(terms))
            ]
            + [whole((count, width))] * len(terms),
            out_specs=[pl.BlockSpec((1,) + shape, lambda s, *_: (s, 0, 0)) for shape in shapes],
        ),
        out_shape=[shape_of((steps,) + shape, BF) for shape in shapes],
        compiler_params=params(SEND_LIMIT),
        name="expert_weight_gradients",
    )(*tiles, *wides, *rows)


def expert_out_kernel(act_ref, out_ref, gate_ref, *send_refs):
    rows = (dot(act_ref[...], out_ref[0]) * gate_ref[...]).astype(BF)
    for number, send_ref in enumerate(send_refs):

        @pl.when(pl.program_id(0) == number)
        def _(send_ref=send_ref):
            send_ref[...] = rows


def expert_out_part(act, expert_out, gate, plan):
    rows, hidden = act.shape
    width = expert_out.shape[2]
    steps = len(plan.arrays)
    return pl.pallas_call(
        expert_out_kernel,
        grid=(steps,),
        out_shape=[shape_of((count, width), BF) for count in plan.arrays],
        in_specs=[
            by_rows(rows // steps, hidden),
            whole((1, hidden, width)),
            by_rows(rows // steps, 1),
        ],
        out_specs=[whole((count, width)) for count in plan.arrays],
        compiler_params=params(32),
        name="expert_output",
    )(act, expert_out, gate)


ROW_STEPS = 2


def result_kernel(plan, expert_ref, length_ref, column_ref, resid_ref, *refs):
    total = resid_ref[...] + home_rows(expert_ref, column_ref[...], refs[:-1], plan)
    rows = total.shape[0]
    live = iota((rows, 1), 0) + pl.program_id(0) * rows < length_ref[0]
    refs[-1][...] = jnp.where(live, total, 0.0).astype(BF)


def result_part(expert, lengths, column, resid, arrays, plan):
    seq_len, width = resid.shape
    rows = seq_len // ROW_STEPS
    return pl.pallas_call(
        functools.partial(result_kernel, plan),
        grid=(ROW_STEPS,),
        out_shape=shape_of(resid.shape, BF),
        in_specs=[smem(), smem(), by_rows(rows, LANES), by_rows(rows, width)]
        + plan.specs(arrays),
        out_specs=by_rows(rows, width),
        compiler_params=params(63),
        name="result",
    )(expert, lengths, column, resid, *arrays)


def middle_kernel(
    plan,
    expert_ref,
    length_ref,
    column_ref,
    resid_ref,
    cotangent_ref,
    out_weight_ref,
    gain_ref,
    *refs,
):
    resid_grad_ref, mixed_grad_ref, attn_grad_ref, gain_grad_ref = refs[-4:]
    upstream = home_rows(expert_ref, column_ref[...], refs[:-4], plan)
    resid = resid_ref[...]
    rows = resid.shape[0]
    inverse = inverse_rms(resid)
    scaled = gain_ref[...].astype(F32).reshape(1, -1) * upstream
    add_rows(gain_grad_ref, jnp.sum(upstream * resid * inverse, axis=0, keepdims=True))
    live = iota((rows, 1), 0) + pl.program_id(0) * rows < length_ref[0]
    resid_grad = (
        jnp.where(live, cotangent_ref[...].astype(F32), 0.0)
        + inverse * scaled
        - resid * (inverse * inverse * inverse * jnp.mean(scaled * resid, axis=-1, keepdims=True))
    )
    resid_grad_ref[...] = resid_grad
    attn_grad = resid_grad.astype(BF)
    mixed_grad_ref[...] = dot(attn_grad, out_weight_ref[...], 1, 1).astype(BF)
    attn_grad_ref[...] = attn_grad


def middle_part(expert, lengths, column, resid, cotangent, out_weight, gain, arrays, plan):
    seq_len, width = resid.shape
    rows = seq_len // ROW_STEPS
    block = by_rows(rows, width)
    return pl.pallas_call(
        functools.partial(middle_kernel, plan),
        grid=(ROW_STEPS,),
        out_shape=[
            shape_of((seq_len, width), F32),
            shape_of((seq_len, width), BF),
            shape_of((seq_len, width), BF),
            shape_of((1, width), F32),
        ],
        in_specs=[smem(), smem(), by_rows(rows, LANES), block, block, whole((width, width)), whole((width,))]
        + plan.specs(arrays),
        out_specs=[block, block, block, whole((1, width))],
        compiler_params=params(63),
        name="expert_norm_backward",
    )(expert, lengths, column, resid, cotangent, out_weight, gain, *arrays)


def backward_kernel(
    core_ref,
    qkv_ref,
    probs_ref,
    lefts_ref,
    mixed_ref,
    grad_ref,
    attn_grad_ref,
    inverse_ref,
    back_ref,
    line_ref,
    *refs,
):
    own_refs, other_refs, score_s, lefts_s, backs_s = refs[:2], refs[2:4], *refs[4:]
    seq_len = grad_ref.shape[0]

    @pl.when(pl.program_id(0) == 0)
    def _():
        lefts_s[0] = lefts_ref[0].T
        lefts_s[1] = lefts_ref[1].T

    tiles = seq_len // TILE
    query = qkv_ref[0, 0]
    key = qkv_ref[1, 0]
    value = qkv_ref[2, 0]
    lane = iota((seq_len, LANES), 1)
    row_tile = iota((seq_len, LANES), 0) // TILE
    scaled = grad_ref[...].astype(F32) * inverse_ref[0]
    product = scaled * mixed_ref[0].astype(F32)
    scaled_low = scaled.astype(BF)
    key_wide = jnp.concatenate([key, jnp.where(lane == row_tile, 1.0, 0.0).astype(BF)], axis=1)
    backward_rows = jnp.where(iota((TILE, TILE), 0) + iota((TILE, TILE), 1) == TILE - 1, 1.0, 0.0)
    query_backs = []
    key_backs = []
    value_backs = []
    for half in range(2):
        own = lane < HALF if half == 0 else lane >= HALF
        extra = lane - HALF if half == 0 else lane
        delta = jnp.sum(jnp.where(own, product, 0.0), axis=-1, keepdims=True)
        high = delta.astype(BF).astype(F32)
        grad_wide = jnp.where(
            own, scaled, jnp.where(extra == 0, -high, jnp.where(extra == 1, high - delta, 0.0))
        ).astype(BF)
        value_wide = jnp.where(
            own, value.astype(F32), jnp.where((extra == 0) | (extra == 1), 1.0, 0.0)
        ).astype(BF)
        near = [jnp.zeros((TILE, TILE), F32) for _ in range(3)]
        for tile in range(tiles):
            part = slice(tile * TILE, (tile + 1) * TILE)
            prob_grad = dot(grad_wide[part], value_wide, 1, 1)
            score_grad = (probs_ref[half, part, :].astype(F32) * prob_grad).astype(BF)
            score_s[half, part, :] = score_grad
            for side in range(3):
                other = tile + side - 1
                if 0 <= other < tiles:
                    near[side] = near[side] + score_grad[
                        :, other * TILE : (other + 1) * TILE
                    ].astype(F32)
        query_wide = dot(score_s[half], key_wide)
        query_backs.append(query_wide[:, :LANES])
        sums = query_wide[:, LANES:]
        far_left = jnp.sum(jnp.where(lane <= row_tile - 2, sums, 0.0), axis=0, keepdims=True)
        far_right = jnp.sum(jnp.where(lane >= row_tile + 2, sums, 0.0), axis=0, keepdims=True)
        line_ref[0, half : half + 1, LINE : LINE + LANES] = far_left
        line_ref[0, half : half + 1, LINE + LANES :] = far_right
        key_backs.append(dot(query, score_s[half], 0, 0))
        value_backs.append(dot(scaled_low, probs_ref[half], 0, 0))
        spread = lax.dot_general(
            backward_rows,
            jnp.concatenate(near, axis=1),
            (((1,), (0,)), ((), ())),
            precision=lax.Precision.HIGHEST,
            preferred_element_type=F32,
        )
        spread = jnp.concatenate([spread, jnp.zeros((TILE, TILE), F32)], axis=1)
        spread = pltpu.roll(spread, 0, 1, stride=1, stride_axis=0)
        line_ref[0, half : half + 1, :LINE] = jnp.sum(spread, axis=0, keepdims=True)
    first = lane < HALF
    backs = [(jnp.where(first, query_backs[0], query_backs[1]) * HALF ** (-0.5)).astype(BF)]
    for halves in (key_backs, value_backs):
        joined = jnp.concatenate([halves[0][:HALF], halves[1][HALF:]], axis=0)
        backs.append(joined.T.astype(BF))
    backs.append(attn_grad_ref[...])
    for place, values in enumerate(backs):
        if place < 3:
            back_ref[place] = values

    @pl.when(pl.program_id(0) % 2 == 0)
    def _():
        for place, values in enumerate(backs):
            backs_s[place] = values

    @pl.when(pl.program_id(0) % 2 == 1)
    def _():
        wides = [jnp.concatenate([backs_s[n], values], axis=1) for n, values in enumerate(backs)]
        grads = [dot(lefts_s[n // 3], wide).astype(BF) for n, wide in enumerate(wides)]
        for core in range(2):

            @pl.when(core_ref[0] == core)
            def _(core=core):
                for target_refs, place in ((own_refs, core), (other_refs, 1 - core)):
                    target_refs[0][...] = grads[place]
                    target_refs[1][...] = grads[2 + place]


def backward_part(core, qkv, probs, lefts, mixed_grad, attn_grad, inverse):
    _, seq_len, width = lefts.shape
    pairs = width // LANES
    assert pairs % 2 == 0
    column = pl.BlockSpec((seq_len, LANES), lambda p: (0, p))
    grad = pl.BlockSpec((width, 2 * LANES), lambda p: (0, p // 2))
    return pl.pallas_call(
        backward_kernel,
        grid=(pairs,),
        out_shape=[
            shape_of((3, seq_len, width), BF),
            shape_of((pairs, 2, LINE + 2 * LANES), F32),
        ]
        + [shape_of((width, width), BF)] * 4,
        in_specs=[
            smem(),
            pl.BlockSpec((3, 1, seq_len, LANES), lambda p: (0, p, 0, 0)),
            pl.BlockSpec((2, seq_len, seq_len), lambda p: (p, 0, 0)),
            whole(lefts.shape),
            pl.BlockSpec((1, seq_len, LANES), lambda p: (1, 0, p)),
            column,
            column,
            pl.BlockSpec((1, seq_len, LANES), lambda p: (p, 0, 0)),
        ],
        out_specs=[
            pl.BlockSpec((3, seq_len, LANES), lambda p: (0, 0, p)),
            pl.BlockSpec((1, 2, LINE + 2 * LANES), lambda p: (p, 0, 0)),
        ]
        + [grad] * 4,
        scratch_shapes=[
            pltpu.VMEM((2, seq_len, seq_len), BF),
            pltpu.VMEM((2, width, seq_len), BF),
            pltpu.VMEM((4, seq_len, LANES), BF),
        ],
        compiler_params=params(58),
        name="attention_backward",
    )(core, qkv, probs, lefts, lefts, mixed_grad, attn_grad, inverse)


def extra_kernel(router_ref, gain_ref, line_ref, out_ref):
    experts, width = router_ref.shape
    heads, places = line_ref.shape
    place = iota((places, width), 0)
    bucket = iota((places, width), 1)
    own = bucket_of(place - (2 * TILE - 1), BUCKETS, MAXDIST)
    own = jnp.where(place >= LINE, BUCKETS // 2 - 1, own)
    own = jnp.where(place >= LINE + LANES, BUCKETS - 1, own)
    sums = lax.dot_general(
        line_ref[...],
        jnp.where(own == bucket, 1.0, 0.0),
        (((1,), (0,)), ((), ())),
        precision=lax.Precision.HIGHEST,
        preferred_element_type=F32,
    )
    rows = [
        router_ref[...],
        jnp.broadcast_to(gain_ref[...], (8, width)),
        sums,
        jnp.zeros((out_ref.shape[0] - experts - 8 - heads, width), F32),
    ]
    out_ref[...] = jnp.concatenate(rows, axis=0).astype(BF)


def extra_part(router_grad, gain_grad, lines):
    experts, width = router_grad.shape
    rows = -(-(experts + 8 + lines.shape[0]) // 16) * 16
    return pl.pallas_call(
        extra_kernel,
        out_shape=shape_of((rows, width), BF),
        compiler_params=params(63),
        name="extra_rows",
    )(router_grad, gain_grad, lines)


def token_grad_kernel(
    back_ref,
    query_weight_ref,
    key_weight_ref,
    value_weight_ref,
    tokens_ref,
    gain_ref,
    resid_grad_ref,
    out_ref,
):
    upstream = None
    for part, weight_ref in enumerate((query_weight_ref, key_weight_ref, value_weight_ref)):
        term = dot(back_ref[part], weight_ref[...], 1, 1)
        upstream = term if upstream is None else upstream + term
    rows = tokens_ref[...].astype(F32)
    inverse = inverse_rms(rows)
    scaled = gain_ref[...].astype(F32).reshape(1, -1) * upstream
    out_ref[...] = (
        resid_grad_ref[...]
        + inverse * scaled
        - rows * (inverse * inverse * inverse * jnp.mean(scaled * rows, axis=-1, keepdims=True))
    )


def token_grad_part(back, weights, tokens, gain, resid_grad):
    seq_len, width = tokens.shape
    rows = seq_len // ROW_STEPS
    block = by_rows(rows, width)
    return pl.pallas_call(
        token_grad_kernel,
        grid=(ROW_STEPS,),
        out_shape=shape_of((seq_len, width), F32),
        in_specs=[pl.BlockSpec((3, rows, width), lambda step: (0, step, 0))]
        + [whole((width, width))] * 3
        + [block, whole((width,)), block],
        out_specs=block,
        compiler_params=params(63),
        name="token_gradient",
    )(back, *weights, tokens, gain, resid_grad)


def swap(values, axis, size, distance):
    return lax.ppermute(values, axis, [(place, place ^ distance) for place in range(size)])


def after(values, *others):
    return lax.optimization_barrier((values, *others))[0]


class Plan:
    def __init__(self, size, capacity, experts):
        self.size = size
        self.capacity = capacity
        self.paired = size == 8 and capacity % 16 == 0
        if self.paired:
            self.block_rows = capacity
            self.blocks = size
            self.arrays = [2 * capacity] * (size // 2)
        else:
            self.block_rows = experts * capacity
            self.blocks = 1
            self.arrays = [experts * capacity]

    def turn(self, rows):
        parts = rows.reshape(self.size, self.capacity, rows.shape[1])
        parts = lax.all_to_all(parts, "expert", split_axis=0, concat_axis=0, tiled=True)
        return parts.reshape(rows.shape)

    def cross(self, arrays):
        if not self.paired:
            return [self.turn(array) for array in arrays]
        return [
            array if k == 0 else swap(array, "expert", self.size, 2 * k)
            for k, array in enumerate(arrays)
        ]

    def finish(self, arrays):
        if not self.paired:
            return arrays
        return [*arrays, *[swap(array, "expert", self.size, 1) for array in arrays]]

    def specs(self, arrays):
        if not self.paired:
            return [whole(array.shape) for array in arrays]
        return [
            pl.BlockSpec((self.block_rows, array.shape[1]), lambda *_, n=n: (2 * n // len(arrays), 0))
            for n, array in enumerate(arrays)
        ]

    def by_distance(self, refs):
        half = len(refs) // 2
        return [ref for pair in zip(refs[:half], refs[half:]) for ref in pair] if self.paired else refs


def stages_of(dp_size, expert_size):
    stages = [("expert", expert_size, (1,))]
    bits = [1 << n for n in range(dp_size.bit_length() - 1)]
    stages += [("dp", dp_size, tuple(bits[n : n + 2])) for n in range(0, len(bits), 2)]
    bits = [1 << n for n in range(1, expert_size.bit_length() - 1)]
    return stages + [("expert", expert_size, tuple(bits[n : n + 2])) for n in range(0, len(bits), 2)]


def distances_of(bits):
    return [sum(bit for n, bit in enumerate(bits) if (k >> n) & 1) for k in range(1 << len(bits))]


def place_of(stage):
    axis, _, bits = stage
    index = lax.axis_index(axis)
    return sum(((index // bit) % 2) << n for n, bit in enumerate(bits))


def share_kernel(inputs, extra, apart, place_ref, *refs):
    in_refs, out_refs = refs[:inputs], refs[inputs:]
    extra_refs, out_refs = out_refs[: len(out_refs) - apart], out_refs[len(out_refs) - apart :]
    last = in_refs[0].shape[0] - (0 if extra_refs else extra)
    count = 1 if place_ref is None else len(out_refs)
    rows = last // count
    for number in range(count):
        start = 0 if count == 1 else pl.multiple_of((place_ref[0] ^ number) * rows, rows)
        total = sum(ref[pl.ds(start, rows), :].astype(F32) for ref in in_refs)
        out_refs[number][:rows, :] = total.astype(BF)
    if extra:
        if extra_refs:
            total = sum(ref[...].astype(F32) for ref in extra_refs).astype(BF)
        else:
            total = sum(ref[last:, :].astype(F32) for ref in in_refs).astype(BF)
        if count > 1:
            for out_ref in out_refs:
                out_ref[rows:, :] = total
        else:
            out_refs[-1][...] = total


def share(parts, stage, extra, extras=()):
    count = 1 if stage is None else 1 << len(stage[2])
    place = None if stage is None else place_of(stage)
    if parts[0].shape[0] // count % 16 and extras:
        parts = [jnp.concatenate(pair, axis=0) for pair in zip(parts, extras)]
        extras = ()
    last, width = parts[0].shape[0] - (0 if extras else extra), parts[0].shape[1]
    rows = last // count
    shapes = [(rows + extra, width)] * count if count > 1 else [(rows, width)]
    if count == 1 and extra:
        shapes.append((extra, width))
    if rows % 16:
        total = sum(part.astype(F32) for part in parts).astype(BF)
        if stage is None:
            return [total[:last], total[last:]] if extra else [total]
        return [
            jnp.concatenate(
                [lax.dynamic_slice_in_dim(total, (place ^ number) * rows, rows, 0), total[last:]], axis=0
            )
            for number in range(count)
        ]
    kernel = functools.partial(share_kernel, len(parts), extra, len(shapes))
    if stage is None:
        kernel = functools.partial(kernel, None)
    return pl.pallas_call(
        kernel,
        out_shape=[shape_of(shape, BF) for shape in shapes],
        in_specs=[smem()] * (stage is not None) + [pl.BlockSpec()] * (len(parts) + len(extras)),
        compiler_params=params(63),
        name="share",
    )(*([] if stage is None else [place.reshape(1)]), *parts, *extras)


def scatter(parts, stage):
    axis, size, bits = stage
    return [
        part if distance == 0 else swap(part, axis, size, distance)
        for part, distance in zip(parts, distances_of(bits))
    ]


def gather(values, stage):
    axis, size, bits = stage
    return [
        values if distance == 0 else swap(values, axis, size, distance)
        for distance in distances_of(bits)
    ]


def join_kernel(place_ref, *refs):
    out_ref = refs[-1]
    for number, ref in enumerate(refs[:-1]):
        rows = ref.shape[0]
        part = pl.ds(pl.multiple_of((place_ref[0] ^ number) * rows, rows), rows)
        out_ref[part, :] = ref[...]


def join(parts, stage):
    place = place_of(stage)
    rows, width = parts[0].shape
    if rows % 16:
        joined = jnp.zeros((rows * len(parts), width), BF)
        for number, part in enumerate(parts):
            joined = lax.dynamic_update_slice_in_dim(joined, part, (place ^ number) * rows, 0)
        return joined
    return pl.pallas_call(
        join_kernel,
        out_shape=shape_of((rows * len(parts), width), BF),
        in_specs=[smem()] + [pl.BlockSpec()] * len(parts),
        compiler_params=params(63),
        name="join",
    )(place.reshape(1), *parts)


def assemble_kernel(count, places_ref, *refs):
    own_refs, other_refs = refs[:count], refs[count : 2 * count]
    weight_refs, out_refs, gain_ref = refs[2 * count : -3], refs[-3:-1], refs[-1]
    source = places_ref[1] ^ pl.program_id(0)
    for number in range(count):
        for core in range(2):

            @pl.when((source == number) & (places_ref[0] == core))
            def _(number=number, core=core):
                out_refs[core][...] = own_refs[number][...].astype(F32)
                out_refs[1 - core][...] = other_refs[number][...].astype(F32)

    total = sum(
        jnp.sum(out_ref[...] * weight_ref[...].astype(F32), axis=1, keepdims=True)
        for out_ref, weight_ref in zip(out_refs, weight_refs)
    )
    gain_ref[...] = jnp.broadcast_to(total, gain_ref.shape)


def assemble(own, other, stages, weights):
    rows, width = own[0].shape
    count = len(own)
    block = by_rows(rows, width)
    places = jnp.stack([place_of(stage) for stage in stages])
    return pl.pallas_call(
        functools.partial(assemble_kernel, count),
        grid=(count,),
        out_shape=[shape_of((count * rows, width), F32)] * 2 + [shape_of((count * rows, LANES), F32)],
        in_specs=[smem()] + [whole((rows, width))] * (2 * count) + [block] * len(weights),
        out_specs=[block, block, by_rows(rows, LANES)],
        compiler_params=params(63),
        name="assemble",
    )(places, *own, *other, *weights)


def halving_order(bits):
    if not bits:
        return [0]
    rest = halving_order(bits[1:])
    return rest + [distance | bits[0] for distance in rest]


def on_device(
    dp_size,
    expert_size,
    tokens,
    cotangent,
    lengths,
    routes,
    norm_gain,
    query_weight,
    key_weight,
    value_weight,
    output_weight,
    bucket_head_bias,
    ffn_gain,
    router_weight,
    expert_in,
    expert_out,
):
    seq_count, seq_len, width = tokens.shape
    buckets, heads = bucket_head_bias.shape
    assert seq_count == 1 and buckets == BUCKETS
    experts = router_weight.shape[1]
    capacity = max(2, 5 * seq_len // (4 * experts))
    plan = Plan(expert_size, capacity, experts)
    expert = lax.axis_index("expert").reshape(1)
    group = lax.axis_index("dp")
    rows_in = tokens.reshape(seq_len, width)
    upstream = cotangent.reshape(seq_len, width)
    weights = (query_weight, key_weight, value_weight)

    slot, column, *up_send = slots_part(expert, lengths, routes, upstream, capacity, experts, plan)
    up_there = plan.cross(up_send)
    probs, qkv, lefts, inverse_total, resid, *row_send = forward_part(
        expert,
        lengths,
        slot,
        rows_in,
        norm_gain,
        (*weights, output_weight),
        bucket_head_bias.T,
        ffn_gain,
        plan,
    )
    row_send, up_there = lax.optimization_barrier((row_send, up_there))
    row_there = plan.cross(row_send)
    up_rows, act_grad = expert_up_part(plan.finish(up_there), expert_out, plan)
    cut = len(row_there) - 1 if plan.paired else len(row_there)
    values, back_send = (), []
    for first, some in ((0, row_there[:cut]), (cut, row_there[cut:])):
        if some:
            some = lax.optimization_barrier((some, values[4] if values else act_grad))[0]
            outs = expert_part(
                expert,
                up_rows,
                act_grad,
                expert_in,
                router_weight.T,
                plan.finish(some),
                plan,
                first,
                values,
            )
            values, back_send = outs[:6], back_send + list(outs[6:])
    act, slope, scaled_rows, rows_grad, gate, logit_grad = values
    router_grad = dot(logit_grad, scaled_rows, 0, 0)
    back_there = plan.cross(back_send)

    bits = [1 << n for n in range(dp_size.bit_length() - 1)]
    half = dp_size // 2
    orders = (bits, bits[::-1])
    tiles = [group ^ jnp.array(halving_order(order), jnp.int32) for order in orders]
    grad_terms = [(act, rows_grad, True), (slope, scaled_rows, False)]
    sends = [
        weight_grad_part(dp_size, [(tile[half:], *term)])[0] for tile, term in zip(tiles, grad_terms)
    ]
    arrived = [swap(send, "dp", dp_size, order[0]) for send, order in zip(sends, orders)]
    keeps = weight_grad_part(
        dp_size, [(tile[:half], *term) for tile, term in zip(tiles, grad_terms)]
    )
    result_send = expert_out_part(act, expert_out, gate, plan)
    back_there = lax.optimization_barrier((back_there, keeps, result_send))[0]
    back_arrays = plan.finish(back_there)

    resid_grad, mixed_grad, attn_grad, ffn_gain_grad = middle_part(
        expert, lengths, column, after(resid, *keeps), upstream, output_weight, ffn_gain, back_arrays, plan
    )
    result_send = lax.optimization_barrier((result_send, back_there))[0]
    result_there = plan.cross(result_send)

    arrived = lax.optimization_barrier((arrived, back_arrays))[0]
    seconds = later_sums(keeps, arrived)
    rests = [list(order[1:]) for order in orders]
    arrived_seconds = [
        swap(send, "dp", dp_size, rest[0]) if rest else None for send, rest in zip(seconds, rests)
    ]
    mixed_grad = after(mixed_grad, *seconds)

    stages = stages_of(dp_size, expert_size)
    core = place_of(stages[0])
    back, lines, *grads = backward_part(
        core.reshape(1), qkv, probs, lefts, mixed_grad, attn_grad, inverse_total
    )
    kept, sent = grads[:2], grads[2:]
    back, sent, result_there, arrived_seconds = lax.optimization_barrier(
        (back, sent, result_there, arrived_seconds)
    )

    there = [swap(values, *stages[0][:2], 1) for values in sent]
    extra = extra_part(router_grad, ffn_gain_grad, lines.reshape(heads, -1))
    extra_rows = [0, extra.shape[0]]
    extras = [(), (extra, swap(extra, *stages[0][:2], 1))]
    shares = []
    for values, other, rows, more in zip(kept, there, extra_rows, extras):
        parts = [values, other]
        if shares:
            parts = after(parts, shares[0])
        shares.append(share(parts, stages[1], rows, more))
    moved = [scatter(parts, stages[1]) for parts in shares]
    token_grad = token_grad_part(after(back, *shares[1]), weights, rows_in, norm_gain, resid_grad)
    moved[0], token_grad, result_there = lax.optimization_barrier(
        (moved[0], token_grad, result_there)
    )
    result_arrays = plan.finish(result_there)
    for stage in stages[2:]:
        shares = [share(parts, stage, rows) for parts, rows in zip(moved, extra_rows)]
        moved = [scatter(parts, stage) for parts in shares]
    chunks = [share(parts, None, rows) for parts, rows in zip(moved, extra_rows)]
    extra = chunks[1][1].astype(F32)
    chunks = [chunk[0] for chunk in chunks]
    for stage in stages[:1:-1]:
        chunks = [join(gather(values, stage), stage) for values in chunks]
    there = [gather(values, stages[1]) for values in chunks]
    keeps, arrived, arrived_seconds, resid = lax.optimization_barrier(
        (keeps, arrived, arrived_seconds, resid, chunks)
    )[:4]
    result = result_part(expert, lengths, column, resid, result_arrays, plan)
    weight_sums = []
    for rest, keep, term, second in zip(rests, keeps, arrived, arrived_seconds):
        total = keep[: half // 2].astype(F32) + term[: half // 2].astype(F32)
        if rest:
            total = total + second.astype(F32)
        weight_sums.append(total)
    last = [pieces.pop() for pieces in there]
    over = [[swap(piece, *stages[0][:2], 1) for piece in pieces] for pieces in there]
    last, weight_sums, result = lax.optimization_barrier((last, weight_sums, result))
    for pieces, others, piece in zip(there, over, last):
        pieces.append(piece)
        others.append(swap(piece, *stages[0][:2], 1))
    expert_out_grad, expert_in_grad = weight_sums
    (query_grad, key_grad, gain_sum), (value_grad, output_grad, value_sum) = [
        assemble(own, other, stages[:2], some)
        for own, other, some in zip(there, over, ((query_weight, key_weight), (value_weight,)))
    ]
    norm_gain_grad = (gain_sum + value_sum)[:, 0] / norm_gain.astype(F32)

    return (
        result.reshape(tokens.shape),
        token_grad.reshape(tokens.shape),
        norm_gain_grad,
        query_grad,
        key_grad,
        value_grad,
        output_grad,
        extra[experts + 8 : experts + 8 + heads, :buckets].T,
        extra[experts],
        extra[:experts].T,
        expert_in_grad,
        expert_out_grad,
    )


def solution(mesh):
    in_specs = (
        P(("dp", "expert"), None, None),
        P(("dp", "expert"), None, None),
        P(("dp", "expert")),
        P(("dp", "expert"), None),
        P(),
        P(),
        P(),
        P(),
        P(),
        P(),
        P(),
        P(),
        P("expert", None, None),
        P("expert", None, None),
    )
    out_specs = (
        P(("dp", "expert"), None, None),
        P(("dp", "expert"), None, None),
        P(),
        P(),
        P(),
        P(),
        P(),
        P(),
        P(),
        P(),
        P("expert", None, "dp"),
        P("expert", "dp", None),
    )
    return jax.shard_map(
        functools.partial(on_device, mesh.shape["dp"], mesh.shape["expert"]),
        mesh=mesh,
        in_specs=in_specs,
        out_specs=out_specs,
        check_vma=False,
    )
```

```python
import functools
import math

import jax
import jax.numpy as jnp
from jax import lax
from jax.experimental import pallas as pl
from jax.experimental.pallas import tpu as pltpu
from jax.sharding import PartitionSpec as P

BF = jnp.bfloat16
F32 = jnp.float32
MAXDIST = 128
EPSILON = 1e-06
NEGATIVE = -1000000000.0
TILE = 128
BUCKETS = 32
LANES = 128
HALF = 64
LINE = 4 * TILE
GELU_ONE = math.sqrt(2.0 / math.pi)
GELU_CUBE = 0.044715
SEND_LIMIT = 32


def dot(left, right, left_dim=1, right_dim=0):
    return lax.dot_general(
        left, right, (((left_dim,), (right_dim,)), ((), ())), preferred_element_type=F32
    )


def iota(shape, dim):
    return lax.broadcasted_iota(jnp.int32, shape, dim)


def bucket_of(offset, buckets, far_limit):
    exact_limit = buckets // 4
    half_count = buckets // 2
    distance = jnp.abs(offset)
    bucket_ids = jnp.minimum(distance, exact_limit)
    for bucket_level in range(exact_limit + 1, half_count):
        border = math.ceil(
            exact_limit
            * (far_limit / exact_limit)
            ** ((bucket_level - exact_limit) / (half_count - exact_limit))
        )
        bucket_ids = bucket_ids + (distance >= border).astype(jnp.int32)
    return bucket_ids + jnp.where(offset > 0, half_count, 0).astype(jnp.int32)


def whole(shape):
    return pl.BlockSpec(shape, lambda *_: (0,) * len(shape))


def by_rows(rows, columns):
    return pl.BlockSpec((rows, columns), lambda step: (step, 0))


def add_rows(ref, values):
    @pl.when(pl.program_id(0) == 0)
    def _():
        ref[...] = values

    @pl.when(pl.program_id(0) > 0)
    def _():
        ref[...] += values


def smem():
    return pl.BlockSpec(memory_space=pltpu.SMEM)


def params(mebibytes):
    return pltpu.CompilerParams(vmem_limit_bytes=mebibytes * 1024 * 1024)


def shape_of(shape, dtype):
    return jax.ShapeDtypeStruct(shape, dtype)


def inverse_rms(rows):
    return lax.rsqrt(jnp.mean(rows * rows, axis=-1, keepdims=True) + EPSILON)


def send_rows(expert_ref, slot_row, rows, plan, send_refs):
    block_rows = plan.block_rows
    size = plan.blocks * block_rows
    place = iota((size, 1), 0)
    wanted = place
    if plan.paired:
        for distance in range(plan.blocks):
            first = distance * block_rows
            wanted = jnp.where(
                place >= first, place - first + (expert_ref[0] ^ distance) * block_rows, wanted
            )
    chosen = jnp.where(wanted == slot_row, 1.0, 0.0).astype(BF)
    sent = dot(chosen, rows).astype(BF)
    first = 0
    for send_ref in send_refs:
        send_ref[...] = sent[first : first + send_ref.shape[0]]
        first += send_ref.shape[0]


def home_rows(expert_ref, column, refs, plan):
    block_rows = plan.block_rows
    rows = jnp.concatenate([ref[...] for ref in plan.by_distance(refs)], axis=0)
    place = iota((1, rows.shape[0]), 1)
    wanted = place
    for distance in range(plan.blocks):
        first = distance * block_rows
        base = (expert_ref[0] ^ distance) * block_rows if plan.paired else 0
        wanted = jnp.where(place >= first, place - first + base, wanted)
    chosen = jnp.where(column[:, :1] == wanted, 1.0, 0.0).astype(BF)
    return dot(chosen, rows)


def slots_kernel(
    capacity, experts, plan, expert_ref, length_ref, routes_ref, cotangent_ref, slot_ref, column_ref, *send_refs
):
    seq_len = routes_ref.shape[1]
    routes = routes_ref[...]
    live = iota((1, seq_len), 1) < length_ref[0]
    onehot = jnp.where((iota((experts, seq_len), 0) == routes) & live, 1.0, 0.0)
    earlier = jnp.where(iota((seq_len, seq_len), 0) < iota((seq_len, seq_len), 1), 1.0, 0.0)
    before = dot(onehot.astype(BF), earlier.astype(BF))
    rank = jnp.sum(before * onehot, axis=0, keepdims=True).astype(jnp.int32)
    slot = jnp.where(live & (rank < capacity), routes * capacity + rank, -1)
    slot_ref[...] = slot
    wide = jnp.broadcast_to(slot.astype(F32), (LANES, seq_len))
    column_ref[...] = wide.T.astype(jnp.int32)
    send_rows(expert_ref, slot, cotangent_ref[...], plan, send_refs)


def slots_part(expert, lengths, routes, cotangent, capacity, experts, plan):
    seq_len, width = cotangent.shape
    return pl.pallas_call(
        functools.partial(slots_kernel, capacity, experts, plan),
        out_shape=[shape_of((1, seq_len), jnp.int32), shape_of((seq_len, LANES), jnp.int32)]
        + [shape_of((rows, width), BF) for rows in plan.arrays],
        in_specs=[smem(), smem(), pl.BlockSpec(), pl.BlockSpec()],
        compiler_params=params(58),
        name="slots",
    )(expert, lengths, routes, cotangent)


def forward_kernel(
    plan,
    expert_ref,
    length_ref,
    slot_ref,
    tokens_ref,
    gain_one_ref,
    query_weight_ref,
    key_weight_ref,
    value_weight_ref,
    out_weight_ref,
    bias_ref,
    gain_two_ref,
    *refs,
):
    probs_ref, qkv_ref, lefts_ref, mixed_ref, inverse_ref, resid_ref = refs[:6]
    send_refs = refs[6:-3]
    qkv_s, mixed_s, line_s = refs[-3:]
    pair = pl.program_id(0)
    pairs = pl.num_programs(0)
    seq_len, width = tokens_ref.shape
    tiles = seq_len // TILE

    @pl.when(pair == 0)
    def _():
        buckets = bias_ref.shape[1]
        place = iota((buckets, LINE), 1)
        offset = jnp.where(place < 3 * TILE, place - TILE, place - TILE - LINE)
        chosen = bucket_of(offset, buckets, MAXDIST) == iota((buckets, LINE), 0)
        lines = dot(bias_ref[...], jnp.where(chosen, 1.0, 0.0).astype(BF))
        for number in range(width // LANES):
            line_s[number, 0:2, :] = lines[2 * number : 2 * number + 2]
        rows = tokens_ref[...].astype(F32)
        normed = (rows * inverse_rms(rows) * gain_one_ref[...].astype(F32).reshape(1, width)).astype(BF)
        lefts_ref[0] = normed.T
        for part, weight_ref in enumerate((query_weight_ref, key_weight_ref, value_weight_ref)):
            values = dot(normed, weight_ref[...])
            for number in range(width // LANES):
                block = values[:, number * LANES : (number + 1) * LANES].astype(BF)
                if part == 0:
                    block = block * BF(HALF ** (-0.5))
                qkv_s[part, number] = block

    query = qkv_s[0, pair]
    key = qkv_s[1, pair]
    value = qkv_s[2, pair]
    qkv_ref[0, 0] = query
    qkv_ref[1, 0] = key
    qkv_ref[2, 0] = value
    lane = iota((seq_len, LANES), 1)
    row = iota((seq_len, LANES), 0)
    row_tile = row // TILE
    value_wide = jnp.concatenate([value, jnp.ones((seq_len, LANES), BF)], axis=1)
    query_wides, key_wides, nears = [], [], []
    for half in range(2):
        own = lane < HALF if half == 0 else lane >= HALF
        extra = lane - HALF if half == 0 else lane
        query_wides.append(
            jnp.where(
                own,
                query.astype(F32),
                jnp.where((extra == 0) | (extra == 1 + row_tile), 1.0, 0.0),
            ).astype(BF)
        )
        query_tile = extra - 1
        line = jnp.broadcast_to(line_s[pair, half : half + 1, :], (TILE, LINE))
        far = jnp.where(
            row_tile <= query_tile - 2,
            line[0:1, 0:1],
            jnp.where(row_tile >= query_tile + 2, line[0:1, 3 * TILE - 1 : 3 * TILE], 0.0),
        )
        far = jnp.where((query_tile >= 0) & (query_tile < tiles), far, 0.0)
        far = jnp.where((extra == 0) & (row >= length_ref[0]), NEGATIVE, far)
        key_wides.append(jnp.where(own, key.astype(F32), far).astype(BF))
        nears.append(pltpu.roll(line, 0, 1, stride=1, stride_axis=0)[:, : 3 * TILE])
    first = lane[:TILE] < HALF
    for tile in range(tiles):
        part = slice(tile * TILE, (tile + 1) * TILE)
        low = max(tile - 1, 0)
        high = min(tile + 2, tiles)
        outs = []
        for half in range(2):
            scores = dot(query_wides[half][part], key_wides[half], 1, 1)
            middle = nears[half][:, (low - tile + 1) * TILE : (high - tile + 1) * TILE]
            pieces = [scores[:, low * TILE : high * TILE] + middle]
            if low > 0:
                pieces.insert(0, scores[:, : low * TILE])
            if high < tiles:
                pieces.append(scores[:, high * TILE :])
            scores = jnp.concatenate(pieces, axis=1)
            peak = jnp.max(scores, axis=-1, keepdims=True)
            raised = jnp.exp(scores - peak).astype(BF)
            probs_ref[half, part, :] = raised
            outs.append(dot(raised, value_wide))
        inverse_total = 1.0 / jnp.where(first, outs[0][:, LANES:], outs[1][:, LANES:])
        mixed = jnp.where(first, outs[0][:, :LANES], outs[1][:, :LANES]) * inverse_total
        mixed_s[pair, part, :] = mixed.astype(BF)
        inverse_ref[0, part, :] = inverse_total

    @pl.when(pair == pairs - 1)
    def _():
        mixed_all = jnp.concatenate([mixed_s[number] for number in range(width // LANES)], axis=1)
        lefts_ref[1] = mixed_all.T
        mixed_ref[...] = mixed_all
        resid = tokens_ref[...].astype(F32) + dot(mixed_all, out_weight_ref[...])
        resid_ref[...] = resid
        normed = (resid * inverse_rms(resid) * gain_two_ref[...].astype(F32).reshape(1, width)).astype(BF)
        send_rows(expert_ref, slot_ref[...], normed, plan, send_refs)


def forward_part(expert, lengths, slot, tokens, gain_one, weights, bias, gain_two, plan):
    seq_len, width = tokens.shape
    pairs = width // LANES
    square = whole((width, width))
    return pl.pallas_call(
        functools.partial(forward_kernel, plan),
        grid=(pairs,),
        out_shape=[
            shape_of((2 * pairs, seq_len, seq_len), BF),
            shape_of((3, pairs, seq_len, LANES), BF),
            shape_of((2, width, seq_len), BF),
            shape_of((seq_len, width), BF),
            shape_of((pairs, seq_len, LANES), F32),
            shape_of((seq_len, width), F32),
        ]
        + [shape_of((rows, width), BF) for rows in plan.arrays],
        in_specs=[
            smem(),
            smem(),
            whole((1, seq_len)),
            whole((seq_len, width)),
            whole((width,)),
            square,
            square,
            square,
            square,
            whole(bias.shape),
            whole((width,)),
        ],
        out_specs=[
            pl.BlockSpec((2, seq_len, seq_len), lambda p: (p, 0, 0)),
            pl.BlockSpec((3, 1, seq_len, LANES), lambda p: (0, p, 0, 0)),
            whole((2, width, seq_len)),
            whole((seq_len, width)),
            pl.BlockSpec((1, seq_len, LANES), lambda p: (p, 0, 0)),
            whole((seq_len, width)),
        ]
        + [whole((rows, width)) for rows in plan.arrays],
        scratch_shapes=[
            pltpu.VMEM((3, pairs, seq_len, LANES), BF),
            pltpu.VMEM((pairs, seq_len, LANES), BF),
            pltpu.VMEM((pairs, 8, LINE), F32),
        ],
        compiler_params=params(58),
        name="attention_forward",
    )(expert, lengths, slot, tokens, gain_one, *weights, bias, gain_two)


def expert_up_kernel(plan, out_ref, *refs):
    up_refs = refs[:-2]
    up_ref, act_grad_ref = refs[-2:]

    @pl.when(pl.program_id(0) == 0)
    def _():
        for number, ref in enumerate(plan.by_distance(up_refs)):
            rows = plan.block_rows
            up_ref[number * rows : (number + 1) * rows, :] = ref[...]

    act_grad_ref[...] = dot(up_ref[...], out_ref[0], 1, 1).astype(BF)


def expert_up_part(up_arrays, expert_out, plan):
    width = expert_out.shape[2]
    hidden = expert_out.shape[1]
    rows = sum(plan.arrays)
    tile = 512
    return pl.pallas_call(
        functools.partial(expert_up_kernel, plan),
        grid=(hidden // tile,),
        out_shape=[shape_of((rows, width), BF), shape_of((rows, hidden), BF)],
        in_specs=[pl.BlockSpec((1, tile, width), lambda f: (0, f, 0))]
        + plan.specs(up_arrays),
        out_specs=[whole((rows, width)), pl.BlockSpec((rows, tile), lambda f: (0, f))],
        compiler_params=params(28),
        name="expert_activation_gradient",
    )(expert_out, *up_arrays)


def expert_kernel(plan, inputs, count, expert_ref, up_ref, act_grad_ref, in_ref, router_ref, *refs):
    row_refs = refs[:inputs]
    act_ref, slope_ref, scaled_ref, rows_grad_ref, gate_ref, logit_grad_ref = refs[
        -(7 + count) : -(1 + count)
    ]
    back_refs, rows_ref = refs[-(1 + count) : -1], refs[-1]
    block_rows = plan.block_rows
    step = pl.program_id(0)
    steps = count
    rows, hidden = act_ref.shape
    experts = router_ref.shape[0]
    blocks = plan.by_distance(row_refs)
    for number in range(steps):

        @pl.when(step == number)
        def _(number=number):
            each = len(blocks) // steps
            for place in range(each):
                rows_ref[place * block_rows : (place + 1) * block_rows, :] = blocks[
                    number * each + place
                ][...]

    own = iota((rows, experts), 1) == expert_ref[0]
    logits = dot(rows_ref[...], router_ref[...], 1, 1)
    raised = jnp.exp(logits - jnp.max(logits, axis=-1, keepdims=True))
    probs = raised / jnp.sum(raised, axis=-1, keepdims=True)
    gate = jnp.sum(jnp.where(own, probs, 0.0), axis=-1, keepdims=True)
    gate_ref[...] = gate
    rows_grad_ref[...] = (up_ref[...].astype(F32) * gate).astype(BF)
    scaled_ref[...] = (rows_ref[...].astype(F32) * gate).astype(BF)
    gate_grad = jnp.zeros((rows, LANES), F32)
    tile = 512
    for first in range(0, hidden, tile):
        part = slice(first, first + tile)
        pre = dot(rows_ref[...], in_ref[0, :, part])
        act_grad = act_grad_ref[:, part]
        square = pre * pre
        level = 0.5 + 0.5 * jnp.tanh(pre * (GELU_ONE + GELU_ONE * GELU_CUBE * square))
        act = (pre * level).astype(BF)
        level = level.astype(BF)
        slope = level + act * (BF(1.0) - level) * (
            BF(2.0 * GELU_ONE) + BF(6.0 * GELU_ONE * GELU_CUBE) * square.astype(BF)
        )
        act_ref[:, part] = act
        product = (act * act_grad).astype(F32)
        for place in range(0, tile, LANES):
            gate_grad += product[:, place : place + LANES]
        slope_ref[:, part] = act_grad * slope
    gate_grad = jnp.sum(gate_grad, axis=-1, keepdims=True)
    logit_grad = gate_grad * (jnp.where(own, 1.0, 0.0) - probs)
    logit_grad_ref[...] = logit_grad.astype(BF)
    logit_grad = (gate * logit_grad).astype(BF)
    back = gate * dot(slope_ref[...], in_ref[0], 1, 1) + dot(logit_grad, router_ref[...])
    back = back.astype(BF)
    for number in range(steps):

        @pl.when(step == number)
        def _(number=number):
            back_refs[number][...] = back


def expert_part(expert, up_rows, act_grad, expert_in, router, row_arrays, plan, first, previous):
    rows, width = up_rows.shape
    hidden = expert_in.shape[2]
    experts = router.shape[0]
    some = rows // len(plan.arrays)
    steps = len(row_arrays) // 2 if plan.paired else 1

    def block(columns):
        return pl.BlockSpec((some, columns), lambda r: (first + r, 0))

    return pl.pallas_call(
        functools.partial(expert_kernel, plan, len(row_arrays), steps),
        grid=(steps,),
        out_shape=[
            shape_of((rows, hidden), BF),
            shape_of((rows, hidden), BF),
            shape_of((rows, width), BF),
            shape_of((rows, width), BF),
            shape_of((rows, 1), F32),
            shape_of((rows, experts), BF),
        ]
        + [shape_of((count, width), BF) for count in plan.arrays[:steps]],
        in_specs=[
            smem(),
            block(width),
            block(hidden),
            whole((1, width, hidden)),
            whole((experts, width)),
        ]
        + plan.specs(row_arrays)
        + [pl.BlockSpec(memory_space=pl.ANY)] * len(previous),
        out_specs=[block(columns) for columns in (hidden, hidden, width, width, 1, experts)]
        + [whole((count, width)) for count in plan.arrays[:steps]],
        input_output_aliases={5 + len(row_arrays) + n: n for n in range(len(previous))},
        scratch_shapes=[pltpu.VMEM((some, width), BF)],
        compiler_params=params(44),
        name="expert_rows",
    )(expert, up_rows, act_grad, expert_in, router, *row_arrays, *previous)


def later_sums_kernel(*refs):
    count = len(refs) // 3
    for keep_ref, there_ref, out_ref in zip(refs[:count], refs[count : 2 * count], refs[2 * count :]):
        out_ref[...] = (keep_ref[...].astype(F32) + there_ref[...].astype(F32)).astype(BF)


def later_sums(keeps, theres):
    count, rows, columns = keeps[0].shape
    later = count // 2
    some = rows // 4

    def block(first):
        return pl.BlockSpec((1, some, columns), lambda t, r: (first + t, r, 0))

    return pl.pallas_call(
        later_sums_kernel,
        grid=(later, 4),
        out_shape=[shape_of((later, rows, columns), BF)] * len(keeps),
        in_specs=[block(count - later)] * (2 * len(keeps)),
        out_specs=[block(0)] * len(keeps),
        compiler_params=params(63),
        name="later_sums",
    )(*keeps, *theres)


def weight_grad_kernel(transposed, count, *refs):
    _, wide_refs, rows_refs, out_refs = [refs[n * count : (n + 1) * count] for n in range(4)]
    for turned, wide_ref, rows_ref, out_ref in zip(transposed, wide_refs, rows_refs, out_refs):
        left_ref, right_ref = (wide_ref, rows_ref) if turned else (rows_ref, wide_ref)
        out_ref[0] = dot(left_ref[...], right_ref[...], 0, 0).astype(BF)


def weight_grad_part(parts, terms):
    tiles, wides, rows, transposed = zip(*terms)
    steps = tiles[0].shape[0]
    count, width = rows[0].shape
    tile = wides[0].shape[1] // parts
    shapes = [(tile, width) if turned else (width, tile) for turned in transposed]
    return pl.pallas_call(
        functools.partial(weight_grad_kernel, transposed, len(terms)),
        grid_spec=pltpu.PrefetchScalarGridSpec(
            num_scalar_prefetch=len(terms),
            grid=(steps,),
            in_specs=[
                pl.BlockSpec((count, tile), lambda s, *refs, number=number: (0, refs[number][s]))
                for number in range(len(terms))
            ]
            + [whole((count, width))] * len(terms),
            out_specs=[pl.BlockSpec((1,) + shape, lambda s, *_: (s, 0, 0)) for shape in shapes],
        ),
        out_shape=[shape_of((steps,) + shape, BF) for shape in shapes],
        compiler_params=params(SEND_LIMIT),
        name="expert_weight_gradients",
    )(*tiles, *wides, *rows)


def expert_out_kernel(act_ref, out_ref, gate_ref, *send_refs):
    rows = (dot(act_ref[...], out_ref[0]) * gate_ref[...]).astype(BF)
    for number, send_ref in enumerate(send_refs):

        @pl.when(pl.program_id(0) == number)
        def _(send_ref=send_ref):
            send_ref[...] = rows


def expert_out_part(act, expert_out, gate, plan):
    rows, hidden = act.shape
    width = expert_out.shape[2]
    steps = len(plan.arrays)
    return pl.pallas_call(
        expert_out_kernel,
        grid=(steps,),
        out_shape=[shape_of((count, width), BF) for count in plan.arrays],
        in_specs=[
            by_rows(rows // steps, hidden),
            whole((1, hidden, width)),
            by_rows(rows // steps, 1),
        ],
        out_specs=[whole((count, width)) for count in plan.arrays],
        compiler_params=params(32),
        name="expert_output",
    )(act, expert_out, gate)


ROW_STEPS = 2


def result_kernel(plan, expert_ref, length_ref, column_ref, resid_ref, *refs):
    total = resid_ref[...] + home_rows(expert_ref, column_ref[...], refs[:-1], plan)
    rows = total.shape[0]
    live = iota((rows, 1), 0) + pl.program_id(0) * rows < length_ref[0]
    refs[-1][...] = jnp.where(live, total, 0.0).astype(BF)


def result_part(expert, lengths, column, resid, arrays, plan):
    seq_len, width = resid.shape
    rows = seq_len // ROW_STEPS
    return pl.pallas_call(
        functools.partial(result_kernel, plan),
        grid=(ROW_STEPS,),
        out_shape=shape_of(resid.shape, BF),
        in_specs=[smem(), smem(), by_rows(rows, LANES), by_rows(rows, width)]
        + plan.specs(arrays),
        out_specs=by_rows(rows, width),
        compiler_params=params(63),
        name="result",
    )(expert, lengths, column, resid, *arrays)


def middle_kernel(
    plan,
    expert_ref,
    length_ref,
    column_ref,
    resid_ref,
    cotangent_ref,
    out_weight_ref,
    gain_ref,
    *refs,
):
    resid_grad_ref, mixed_grad_ref, attn_grad_ref, gain_grad_ref = refs[-4:]
    upstream = home_rows(expert_ref, column_ref[...], refs[:-4], plan)
    resid = resid_ref[...]
    rows = resid.shape[0]
    inverse = inverse_rms(resid)
    scaled = gain_ref[...].astype(F32).reshape(1, -1) * upstream
    add_rows(gain_grad_ref, jnp.sum(upstream * resid * inverse, axis=0, keepdims=True))
    live = iota((rows, 1), 0) + pl.program_id(0) * rows < length_ref[0]
    resid_grad = (
        jnp.where(live, cotangent_ref[...].astype(F32), 0.0)
        + inverse * scaled
        - resid * (inverse * inverse * inverse * jnp.mean(scaled * resid, axis=-1, keepdims=True))
    )
    resid_grad_ref[...] = resid_grad
    attn_grad = resid_grad.astype(BF)
    mixed_grad_ref[...] = dot(attn_grad, out_weight_ref[...], 1, 1).astype(BF)
    attn_grad_ref[...] = attn_grad


def middle_part(expert, lengths, column, resid, cotangent, out_weight, gain, arrays, plan):
    seq_len, width = resid.shape
    rows = seq_len // ROW_STEPS
    block = by_rows(rows, width)
    return pl.pallas_call(
        functools.partial(middle_kernel, plan),
        grid=(ROW_STEPS,),
        out_shape=[
            shape_of((seq_len, width), F32),
            shape_of((seq_len, width), BF),
            shape_of((seq_len, width), BF),
            shape_of((1, width), F32),
        ],
        in_specs=[smem(), smem(), by_rows(rows, LANES), block, block, whole((width, width)), whole((width,))]
        + plan.specs(arrays),
        out_specs=[block, block, block, whole((1, width))],
        compiler_params=params(63),
        name="expert_norm_backward",
    )(expert, lengths, column, resid, cotangent, out_weight, gain, *arrays)


def backward_kernel(
    core_ref,
    qkv_ref,
    probs_ref,
    lefts_ref,
    mixed_ref,
    grad_ref,
    attn_grad_ref,
    inverse_ref,
    back_ref,
    line_ref,
    *refs,
):
    own_refs, other_refs, score_s, backs_s = refs[:2], refs[2:4], *refs[4:]
    seq_len = grad_ref.shape[0]

    tiles = seq_len // TILE
    query = qkv_ref[0, 0]
    key = qkv_ref[1, 0]
    value = qkv_ref[2, 0]
    lane = iota((seq_len, LANES), 1)
    row_tile = iota((seq_len, LANES), 0) // TILE
    scaled = grad_ref[...].astype(F32) * inverse_ref[0]
    product = scaled * mixed_ref[...].astype(F32)
    scaled_low = scaled.astype(BF)
    key_wide = jnp.concatenate([key, jnp.where(lane == row_tile, 1.0, 0.0).astype(BF)], axis=1)
    backward_rows = jnp.where(iota((TILE, TILE), 0) + iota((TILE, TILE), 1) == TILE - 1, 1.0, 0.0)
    query_backs = []
    key_backs = []
    value_backs = []
    for half in range(2):
        own = lane < HALF if half == 0 else lane >= HALF
        extra = lane - HALF if half == 0 else lane
        delta = jnp.sum(jnp.where(own, product, 0.0), axis=-1, keepdims=True)
        high = delta.astype(BF).astype(F32)
        grad_wide = jnp.where(
            own, scaled, jnp.where(extra == 0, -high, jnp.where(extra == 1, high - delta, 0.0))
        ).astype(BF)
        value_wide = jnp.where(
            own, value.astype(F32), jnp.where((extra == 0) | (extra == 1), 1.0, 0.0)
        ).astype(BF)
        near = [jnp.zeros((TILE, TILE), F32) for _ in range(3)]
        for tile in range(tiles):
            part = slice(tile * TILE, (tile + 1) * TILE)
            prob_grad = dot(grad_wide[part], value_wide, 1, 1)
            score_grad = (probs_ref[half, part, :].astype(F32) * prob_grad).astype(BF)
            score_s[half, part, :] = score_grad
            for side in range(3):
                other = tile + side - 1
                if 0 <= other < tiles:
                    near[side] = near[side] + score_grad[
                        :, other * TILE : (other + 1) * TILE
                    ].astype(F32)
        query_wide = dot(score_s[half], key_wide)
        query_backs.append(query_wide[:, :LANES])
        sums = query_wide[:, LANES:]
        far_left = jnp.sum(jnp.where(lane <= row_tile - 2, sums, 0.0), axis=0, keepdims=True)
        far_right = jnp.sum(jnp.where(lane >= row_tile + 2, sums, 0.0), axis=0, keepdims=True)
        line_ref[0, half : half + 1, LINE : LINE + LANES] = far_left
        line_ref[0, half : half + 1, LINE + LANES :] = far_right
        key_backs.append(dot(query, score_s[half], 0, 0))
        value_backs.append(dot(scaled_low, probs_ref[half], 0, 0))
        spread = lax.dot_general(
            backward_rows,
            jnp.concatenate(near, axis=1),
            (((1,), (0,)), ((), ())),
            precision=lax.Precision.HIGHEST,
            preferred_element_type=F32,
        )
        spread = jnp.concatenate([spread, jnp.zeros((TILE, TILE), F32)], axis=1)
        spread = pltpu.roll(spread, 0, 1, stride=1, stride_axis=0)
        line_ref[0, half : half + 1, :LINE] = jnp.sum(spread, axis=0, keepdims=True)
    first = lane < HALF
    backs = [(jnp.where(first, query_backs[0], query_backs[1]) * HALF ** (-0.5)).astype(BF)]
    for halves in (key_backs, value_backs):
        joined = jnp.concatenate([halves[0][:HALF], halves[1][HALF:]], axis=0)
        backs.append(joined.T.astype(BF))
    backs.append(attn_grad_ref[...])
    for place, values in enumerate(backs):
        if place < 3:
            back_ref[place] = values

    @pl.when(pl.program_id(0) % 2 == 0)
    def _():
        for place, values in enumerate(backs):
            backs_s[place] = values

    @pl.when(pl.program_id(0) % 2 == 1)
    def _():
        wides = [jnp.concatenate([backs_s[n], values], axis=1) for n, values in enumerate(backs)]
        grads = [dot(lefts_ref[n // 3], wide).astype(BF) for n, wide in enumerate(wides)]
        for core in range(2):

            @pl.when(core_ref[0] == core)
            def _(core=core):
                for target_refs, place in ((own_refs, core), (other_refs, 1 - core)):
                    target_refs[0][...] = grads[place]
                    target_refs[1][...] = grads[2 + place]


def backward_part(core, qkv, probs, lefts, mixed, mixed_grad, attn_grad, inverse):
    seq_len, width = mixed.shape
    pairs = width // LANES
    assert pairs % 2 == 0
    column = pl.BlockSpec((seq_len, LANES), lambda p: (0, p))
    grad = pl.BlockSpec((width, 2 * LANES), lambda p: (0, p // 2))
    return pl.pallas_call(
        backward_kernel,
        grid=(pairs,),
        out_shape=[
            shape_of((3, seq_len, width), BF),
            shape_of((pairs, 2, LINE + 2 * LANES), F32),
        ]
        + [shape_of((width, width), BF)] * 4,
        in_specs=[
            smem(),
            pl.BlockSpec((3, 1, seq_len, LANES), lambda p: (0, p, 0, 0)),
            pl.BlockSpec((2, seq_len, seq_len), lambda p: (p, 0, 0)),
            whole(lefts.shape),
            column,
            column,
            column,
            pl.BlockSpec((1, seq_len, LANES), lambda p: (p, 0, 0)),
        ],
        out_specs=[
            pl.BlockSpec((3, seq_len, LANES), lambda p: (0, 0, p)),
            pl.BlockSpec((1, 2, LINE + 2 * LANES), lambda p: (p, 0, 0)),
        ]
        + [grad] * 4,
        scratch_shapes=[
            pltpu.VMEM((2, seq_len, seq_len), BF),
            pltpu.VMEM((4, seq_len, LANES), BF),
        ],
        compiler_params=params(58),
        name="attention_backward",
    )(core, qkv, probs, lefts, mixed, mixed_grad, attn_grad, inverse)


def extra_kernel(router_ref, gain_ref, line_ref, out_ref):
    experts, width = router_ref.shape
    heads, places = line_ref.shape
    place = iota((places, width), 0)
    bucket = iota((places, width), 1)
    own = bucket_of(place - (2 * TILE - 1), BUCKETS, MAXDIST)
    own = jnp.where(place >= LINE, BUCKETS // 2 - 1, own)
    own = jnp.where(place >= LINE + LANES, BUCKETS - 1, own)
    sums = lax.dot_general(
        line_ref[...],
        jnp.where(own == bucket, 1.0, 0.0),
        (((1,), (0,)), ((), ())),
        precision=lax.Precision.HIGHEST,
        preferred_element_type=F32,
    )
    rows = [
        router_ref[...],
        jnp.broadcast_to(gain_ref[...], (8, width)),
        sums,
        jnp.zeros((out_ref.shape[0] - experts - 8 - heads, width), F32),
    ]
    out_ref[...] = jnp.concatenate(rows, axis=0).astype(BF)


def extra_part(router_grad, gain_grad, lines):
    experts, width = router_grad.shape
    rows = -(-(experts + 8 + lines.shape[0]) // 16) * 16
    return pl.pallas_call(
        extra_kernel,
        out_shape=shape_of((rows, width), BF),
        compiler_params=params(63),
        name="extra_rows",
    )(router_grad, gain_grad, lines)


def token_grad_kernel(
    back_ref,
    query_weight_ref,
    key_weight_ref,
    value_weight_ref,
    tokens_ref,
    gain_ref,
    resid_grad_ref,
    out_ref,
):
    upstream = None
    for part, weight_ref in enumerate((query_weight_ref, key_weight_ref, value_weight_ref)):
        term = dot(back_ref[part], weight_ref[...], 1, 1)
        upstream = term if upstream is None else upstream + term
    rows = tokens_ref[...].astype(F32)
    inverse = inverse_rms(rows)
    scaled = gain_ref[...].astype(F32).reshape(1, -1) * upstream
    out_ref[...] = (
        resid_grad_ref[...]
        + inverse * scaled
        - rows * (inverse * inverse * inverse * jnp.mean(scaled * rows, axis=-1, keepdims=True))
    )


def token_grad_part(back, weights, tokens, gain, resid_grad):
    seq_len, width = tokens.shape
    rows = seq_len // ROW_STEPS
    block = by_rows(rows, width)
    return pl.pallas_call(
        token_grad_kernel,
        grid=(ROW_STEPS,),
        out_shape=shape_of((seq_len, width), F32),
        in_specs=[pl.BlockSpec((3, rows, width), lambda step: (0, step, 0))]
        + [whole((width, width))] * 3
        + [block, whole((width,)), block],
        out_specs=block,
        compiler_params=params(63),
        name="token_gradient",
    )(back, *weights, tokens, gain, resid_grad)


def swap(values, axis, size, distance):
    return lax.ppermute(values, axis, [(place, place ^ distance) for place in range(size)])


def after(values, *others):
    return lax.optimization_barrier((values, *others))[0]


class Plan:
    def __init__(self, size, capacity, experts):
        self.size = size
        self.capacity = capacity
        self.paired = size == 8 and capacity % 16 == 0
        if self.paired:
            self.block_rows = capacity
            self.blocks = size
            self.arrays = [2 * capacity] * (size // 2)
        else:
            self.block_rows = experts * capacity
            self.blocks = 1
            self.arrays = [experts * capacity]

    def turn(self, rows):
        parts = rows.reshape(self.size, self.capacity, rows.shape[1])
        parts = lax.all_to_all(parts, "expert", split_axis=0, concat_axis=0, tiled=True)
        return parts.reshape(rows.shape)

    def cross(self, arrays):
        if not self.paired:
            return [self.turn(array) for array in arrays]
        return [
            array if k == 0 else swap(array, "expert", self.size, 2 * k)
            for k, array in enumerate(arrays)
        ]

    def finish(self, arrays):
        if not self.paired:
            return arrays
        return [*arrays, *[swap(array, "expert", self.size, 1) for array in arrays]]

    def specs(self, arrays):
        if not self.paired:
            return [whole(array.shape) for array in arrays]
        return [
            pl.BlockSpec((self.block_rows, array.shape[1]), lambda *_, n=n: (2 * n // len(arrays), 0))
            for n, array in enumerate(arrays)
        ]

    def by_distance(self, refs):
        half = len(refs) // 2
        return [ref for pair in zip(refs[:half], refs[half:]) for ref in pair] if self.paired else refs


def stages_of(dp_size, expert_size):
    stages = [("expert", expert_size, (1,))]
    bits = [1 << n for n in range(dp_size.bit_length() - 1)]
    stages += [("dp", dp_size, tuple(bits[n : n + 2])) for n in range(0, len(bits), 2)]
    bits = [1 << n for n in range(1, expert_size.bit_length() - 1)]
    return stages + [("expert", expert_size, tuple(bits[n : n + 2])) for n in range(0, len(bits), 2)]


def distances_of(bits):
    return [sum(bit for n, bit in enumerate(bits) if (k >> n) & 1) for k in range(1 << len(bits))]


def place_of(stage):
    axis, _, bits = stage
    index = lax.axis_index(axis)
    return sum(((index // bit) % 2) << n for n, bit in enumerate(bits))


def share_kernel(inputs, extra, apart, place_ref, *refs):
    in_refs, out_refs = refs[:inputs], refs[inputs:]
    extra_refs, out_refs = out_refs[: len(out_refs) - apart], out_refs[len(out_refs) - apart :]
    last = in_refs[0].shape[0] - (0 if extra_refs else extra)
    count = 1 if place_ref is None else len(out_refs)
    rows = last // count
    for number in range(count):
        start = 0 if count == 1 else pl.multiple_of((place_ref[0] ^ number) * rows, rows)
        total = sum(ref[pl.ds(start, rows), :].astype(F32) for ref in in_refs)
        out_refs[number][:rows, :] = total.astype(BF)
    if extra:
        if extra_refs:
            total = sum(ref[...].astype(F32) for ref in extra_refs).astype(BF)
        else:
            total = sum(ref[last:, :].astype(F32) for ref in in_refs).astype(BF)
        if count > 1:
            for out_ref in out_refs:
                out_ref[rows:, :] = total
        else:
            out_refs[-1][...] = total


def share(parts, stage, extra, extras=()):
    count = 1 if stage is None else 1 << len(stage[2])
    place = None if stage is None else place_of(stage)
    if parts[0].shape[0] // count % 16 and extras:
        parts = [jnp.concatenate(pair, axis=0) for pair in zip(parts, extras)]
        extras = ()
    last, width = parts[0].shape[0] - (0 if extras else extra), parts[0].shape[1]
    rows = last // count
    shapes = [(rows + extra, width)] * count if count > 1 else [(rows, width)]
    if count == 1 and extra:
        shapes.append((extra, width))
    if rows % 16:
        total = sum(part.astype(F32) for part in parts).astype(BF)
        if stage is None:
            return [total[:last], total[last:]] if extra else [total]
        return [
            jnp.concatenate(
                [lax.dynamic_slice_in_dim(total, (place ^ number) * rows, rows, 0), total[last:]], axis=0
            )
            for number in range(count)
        ]
    kernel = functools.partial(share_kernel, len(parts), extra, len(shapes))
    if stage is None:
        kernel = functools.partial(kernel, None)
    return pl.pallas_call(
        kernel,
        out_shape=[shape_of(shape, BF) for shape in shapes],
        in_specs=[smem()] * (stage is not None) + [pl.BlockSpec()] * (len(parts) + len(extras)),
        compiler_params=params(63),
        name="share",
    )(*([] if stage is None else [place.reshape(1)]), *parts, *extras)


def scatter(parts, stage):
    axis, size, bits = stage
    return [
        part if distance == 0 else swap(part, axis, size, distance)
        for part, distance in zip(parts, distances_of(bits))
    ]


def gather(values, stage):
    axis, size, bits = stage
    return [
        values if distance == 0 else swap(values, axis, size, distance)
        for distance in distances_of(bits)
    ]


def join_kernel(place_ref, *refs):
    out_ref = refs[-1]
    for number, ref in enumerate(refs[:-1]):
        rows = ref.shape[0]
        part = pl.ds(pl.multiple_of((place_ref[0] ^ number) * rows, rows), rows)
        out_ref[part, :] = ref[...]


def join(parts, stage):
    place = place_of(stage)
    rows, width = parts[0].shape
    if rows % 16:
        joined = jnp.zeros((rows * len(parts), width), BF)
        for number, part in enumerate(parts):
            joined = lax.dynamic_update_slice_in_dim(joined, part, (place ^ number) * rows, 0)
        return joined
    return pl.pallas_call(
        join_kernel,
        out_shape=shape_of((rows * len(parts), width), BF),
        in_specs=[smem()] + [pl.BlockSpec()] * len(parts),
        compiler_params=params(63),
        name="join",
    )(place.reshape(1), *parts)


def assemble_kernel(count, places_ref, *refs):
    own_refs, other_refs = refs[:count], refs[count : 2 * count]
    weight_refs, out_refs, gain_ref = refs[2 * count : -3], refs[-3:-1], refs[-1]
    source = places_ref[1] ^ pl.program_id(0)
    for number in range(count):
        for core in range(2):

            @pl.when((source == number) & (places_ref[0] == core))
            def _(number=number, core=core):
                out_refs[core][...] = own_refs[number][...].astype(F32)
                out_refs[1 - core][...] = other_refs[number][...].astype(F32)

    total = sum(
        jnp.sum(out_ref[...] * weight_ref[...].astype(F32), axis=1, keepdims=True)
        for out_ref, weight_ref in zip(out_refs, weight_refs)
    )
    gain_ref[...] = jnp.broadcast_to(total, gain_ref.shape)


def assemble(own, other, stages, weights):
    rows, width = own[0].shape
    count = len(own)
    block = by_rows(rows, width)
    places = jnp.stack([place_of(stage) for stage in stages])
    return pl.pallas_call(
        functools.partial(assemble_kernel, count),
        grid=(count,),
        out_shape=[shape_of((count * rows, width), F32)] * 2 + [shape_of((count * rows, LANES), F32)],
        in_specs=[smem()] + [whole((rows, width))] * (2 * count) + [block] * len(weights),
        out_specs=[block, block, by_rows(rows, LANES)],
        compiler_params=params(63),
        name="assemble",
    )(places, *own, *other, *weights)


def halving_order(bits):
    if not bits:
        return [0]
    rest = halving_order(bits[1:])
    return rest + [distance | bits[0] for distance in rest]


def on_device(
    dp_size,
    expert_size,
    tokens,
    cotangent,
    lengths,
    routes,
    norm_gain,
    query_weight,
    key_weight,
    value_weight,
    output_weight,
    bucket_head_bias,
    ffn_gain,
    router_weight,
    expert_in,
    expert_out,
):
    seq_count, seq_len, width = tokens.shape
    buckets, heads = bucket_head_bias.shape
    assert seq_count == 1 and buckets == BUCKETS
    experts = router_weight.shape[1]
    capacity = max(2, 5 * seq_len // (4 * experts))
    plan = Plan(expert_size, capacity, experts)
    expert = lax.axis_index("expert").reshape(1)
    group = lax.axis_index("dp")
    rows_in = tokens.reshape(seq_len, width)
    upstream = cotangent.reshape(seq_len, width)
    weights = (query_weight, key_weight, value_weight)

    slot, column, *up_send = slots_part(expert, lengths, routes, upstream, capacity, experts, plan)
    up_there = plan.cross(up_send)
    probs, qkv, lefts, mixed, inverse_total, resid, *row_send = forward_part(
        expert,
        lengths,
        slot,
        rows_in,
        norm_gain,
        (*weights, output_weight),
        bucket_head_bias.T,
        ffn_gain,
        plan,
    )
    row_send, up_there = lax.optimization_barrier((row_send, up_there))
    row_there = plan.cross(row_send)
    up_rows, act_grad = expert_up_part(plan.finish(up_there), expert_out, plan)
    cut = len(row_there) - 1 if plan.paired else len(row_there)
    values, back_send = (), []
    for first, some in ((0, row_there[:cut]), (cut, row_there[cut:])):
        if some:
            some = lax.optimization_barrier((some, values[4] if values else act_grad))[0]
            outs = expert_part(
                expert,
                up_rows,
                act_grad,
                expert_in,
                router_weight.T,
                plan.finish(some),
                plan,
                first,
                values,
            )
            values, back_send = outs[:6], back_send + list(outs[6:])
    act, slope, scaled_rows, rows_grad, gate, logit_grad = values
    router_grad = dot(logit_grad, scaled_rows, 0, 0)
    back_there = plan.cross(back_send)

    bits = [1 << n for n in range(dp_size.bit_length() - 1)]
    half = dp_size // 2
    orders = (bits, bits[::-1])
    tiles = [group ^ jnp.array(halving_order(order), jnp.int32) for order in orders]
    grad_terms = [(act, rows_grad, True), (slope, scaled_rows, False)]
    sends = [
        weight_grad_part(dp_size, [(tile[half:], *term)])[0] for tile, term in zip(tiles, grad_terms)
    ]
    arrived = [swap(send, "dp", dp_size, order[0]) for send, order in zip(sends, orders)]
    keeps = weight_grad_part(
        dp_size, [(tile[:half], *term) for tile, term in zip(tiles, grad_terms)]
    )
    result_send = expert_out_part(act, expert_out, gate, plan)
    back_there = lax.optimization_barrier((back_there, keeps, result_send))[0]
    back_arrays = plan.finish(back_there)

    resid_grad, mixed_grad, attn_grad, ffn_gain_grad = middle_part(
        expert, lengths, column, after(resid, *keeps), upstream, output_weight, ffn_gain, back_arrays, plan
    )
    result_send = lax.optimization_barrier((result_send, back_there))[0]
    result_there = plan.cross(result_send)

    arrived = lax.optimization_barrier((arrived, back_arrays))[0]
    seconds = later_sums(keeps, arrived)
    rests = [list(order[1:]) for order in orders]
    arrived_seconds = [
        swap(send, "dp", dp_size, rest[0]) if rest else None for send, rest in zip(seconds, rests)
    ]
    mixed_grad = after(mixed_grad, *seconds)

    stages = stages_of(dp_size, expert_size)
    core = place_of(stages[0])
    back, lines, *grads = backward_part(
        core.reshape(1), qkv, probs, lefts, mixed, mixed_grad, attn_grad, inverse_total
    )
    kept, sent = grads[:2], grads[2:]
    back, sent, result_there, arrived_seconds = lax.optimization_barrier(
        (back, sent, result_there, arrived_seconds)
    )

    there = [swap(values, *stages[0][:2], 1) for values in sent]
    extra = extra_part(router_grad, ffn_gain_grad, lines.reshape(heads, -1))
    extra_rows = [0, extra.shape[0]]
    extras = [(), (extra, swap(extra, *stages[0][:2], 1))]
    shares = []
    for values, other, rows, more in zip(kept, there, extra_rows, extras):
        parts = [values, other]
        if shares:
            parts = after(parts, shares[0])
        shares.append(share(parts, stages[1], rows, more))
    moved = [scatter(parts, stages[1]) for parts in shares]
    token_grad = token_grad_part(after(back, *shares[1]), weights, rows_in, norm_gain, resid_grad)
    moved[0], token_grad, result_there = lax.optimization_barrier(
        (moved[0], token_grad, result_there)
    )
    result_arrays = plan.finish(result_there)
    for stage in stages[2:]:
        shares = [share(parts, stage, rows) for parts, rows in zip(moved, extra_rows)]
        moved = [scatter(parts, stage) for parts in shares]
    chunks = [share(parts, None, rows) for parts, rows in zip(moved, extra_rows)]
    extra = chunks[1][1].astype(F32)
    chunks = [chunk[0] for chunk in chunks]
    for stage in stages[:1:-1]:
        chunks = [join(gather(values, stage), stage) for values in chunks]
    there = [gather(values, stages[1]) for values in chunks]
    keeps, arrived, arrived_seconds, resid = lax.optimization_barrier(
        (keeps, arrived, arrived_seconds, resid, chunks)
    )[:4]
    result = result_part(expert, lengths, column, resid, result_arrays, plan)
    weight_sums = []
    for rest, keep, term, second in zip(rests, keeps, arrived, arrived_seconds):
        total = keep[: half // 2].astype(F32) + term[: half // 2].astype(F32)
        if rest:
            total = total + second.astype(F32)
        weight_sums.append(total)
    last = [pieces.pop() for pieces in there]
    over = [[swap(piece, *stages[0][:2], 1) for piece in pieces] for pieces in there]
    last, weight_sums, result = lax.optimization_barrier((last, weight_sums, result))
    for pieces, others, piece in zip(there, over, last):
        pieces.append(piece)
        others.append(swap(piece, *stages[0][:2], 1))
    expert_out_grad, expert_in_grad = weight_sums
    (query_grad, key_grad, gain_sum), (value_grad, output_grad, value_sum) = [
        assemble(own, other, stages[:2], some)
        for own, other, some in zip(there, over, ((query_weight, key_weight), (value_weight,)))
    ]
    norm_gain_grad = (gain_sum + value_sum)[:, 0] / norm_gain.astype(F32)

    return (
        result.reshape(tokens.shape),
        token_grad.reshape(tokens.shape),
        norm_gain_grad,
        query_grad,
        key_grad,
        value_grad,
        output_grad,
        extra[experts + 8 : experts + 8 + heads, :buckets].T,
        extra[experts],
        extra[:experts].T,
        expert_in_grad,
        expert_out_grad,
    )


def solution(mesh):
    in_specs = (
        P(("dp", "expert"), None, None),
        P(("dp", "expert"), None, None),
        P(("dp", "expert")),
        P(("dp", "expert"), None),
        P(),
        P(),
        P(),
        P(),
        P(),
        P(),
        P(),
        P(),
        P("expert", None, None),
        P("expert", None, None),
    )
    out_specs = (
        P(("dp", "expert"), None, None),
        P(("dp", "expert"), None, None),
        P(),
        P(),
        P(),
        P(),
        P(),
        P(),
        P(),
        P(),
        P("expert", None, "dp"),
        P("expert", "dp", None),
    )
    return jax.shard_map(
        functools.partial(on_device, mesh.shape["dp"], mesh.shape["expert"]),
        mesh=mesh,
        in_specs=in_specs,
        out_specs=out_specs,
        check_vma=False,
    )
```
